32 devices in a mesh: shards: 2 (over x), tensor: 4 (over y, core), replica: 4 (over z).
Axes of the slice: x: 2, y: 2, z: 4, core: 2. Of those that a mesh axis runs over, the one named last changes fastest.
Arguments:
- activations: bfloat16 [32768, 1024], P(('shards', 'tensor', 'replica')), may hold values from -6 to 6
- grads_out: bfloat16 [32768, 1024], P(('shards', 'tensor', 'replica')), may hold values from -6 to 6
- grad_parts: float32 [8, 1024, 1024], P(('shards', 'replica'), None, 'tensor'), may hold values from -80 to 80
- old_factors: float32 [16, 128, 128], replicated, may hold values from -16 to 16, as said below
- block_owner: int32 [16], replicated, may hold values from 0 to 1, as said below
- weights: float32 [1024, 1024], P(('shards', 'replica'), 'tensor'), may hold values from -0.1875 to 0.1875
- momentum: float32 [1024, 1024], P(('shards', 'replica'), 'tensor'), may hold values from -4 to 4
Outputs:
- weights_next: float32 [1024, 1024], P(None, 'tensor')
- momentum_next: float32 [1024, 1024], P(('shards', 'replica'), 'tensor')
- next_factor_blocks: float32 [18, 128, 128], P('shards')
The draws below stay inside these ranges and needn't reach their ends.
Inputs may be any that keep to these rules, and one draw needn't show every extreme that they name: `block_owner`: each shard index owns at most 9 of the 16 blocks, and some index owns exactly 9. `old_factors`: each block is symmetric and positive definite.
All inputs are finite; a program needn't handle non-finite values. Where the reference program divides by a largest or mean magnitude, that divisor is 1e-20 or more.
Results may differ from the reference program's by a relative error of at most 0.0003.
Values sent between devices are 32-bit elements; how exact they have to be, the bound alone decides.
A program may use at most 64 MiB of HBM per device.

```python
import math
import jax
import jax.numpy as jnp
from jax import lax

D = 1024
D_OUT = 1024
BLOCK_ORDER_SIZE = 128
NS_STEPS = 4
TOK_DEV = 1024
TOKENS = 32768
DATA = 8
NBLK = 16
BLOCKS_PER_SHARD = 9
OWNER_SLOT_TOTAL = 18


def draw_grad_parts(key, part):
    first_key = jax.random.fold_in(key, 11)
    row_frac = jnp.arange(D, dtype=jnp.float32) / D
    row_rise = jnp.power(3.0, row_frac)
    normal_part = jnp.clip(jax.random.normal(first_key, (DATA, D, D_OUT), jnp.float32), -6.0, 6.0)
    return normal_part * row_rise[None, :, None]


def draw_old_factors(key, part):
    first_key = jax.random.fold_in(key, 21)
    second_key = jax.random.fold_in(key, 22)
    diagonal = jnp.exp(jax.random.uniform(first_key, (NBLK, BLOCK_ORDER_SIZE), jnp.float32, 0.0, math.log(4.0)))
    uniform_part = jax.random.uniform(second_key, (NBLK, BLOCK_ORDER_SIZE, BLOCK_ORDER_SIZE), jnp.float32, -1.0, 1.0)
    symmetric = 0.5 * (uniform_part + jnp.transpose(uniform_part, (0, 2, 1)))
    root_diag = jnp.sqrt(diagonal)
    identity = jnp.eye(BLOCK_ORDER_SIZE, dtype=jnp.float32)
    off_part = symmetric * (0.9 / BLOCK_ORDER_SIZE) * root_diag[:, :, None] * root_diag[:, None, :]
    return off_part * (1.0 - identity) + diagonal[:, :, None] * identity


def draw_block_owner(key, part):
    block_owner_list = OWNER_SLOT_TOTAL // BLOCKS_PER_SHARD
    first_key = jax.random.fold_in(key, 31)
    second_key = jax.random.fold_in(key, 32)
    third_key = jax.random.fold_in(key, 33)
    busiest = jax.random.randint(first_key, (), 0, block_owner_list)
    block_order = jax.random.permutation(second_key, NBLK)
    others = jax.random.permutation(third_key, (block_owner_list - 1) * BLOCKS_PER_SHARD)[:NBLK - BLOCKS_PER_SHARD] // BLOCKS_PER_SHARD
    others = others + (others >= busiest).astype(jnp.int32)
    assigned = jnp.concatenate([jnp.full((BLOCKS_PER_SHARD,), busiest, jnp.int32), others.astype(jnp.int32)])
    return jnp.zeros((NBLK,), jnp.int32).at[block_order].set(assigned)


def with_spikes(values, stream_key, source, target, blocks, factor):
    def block_of(axis_at):
        return (jnp.arange(values.shape[axis_at]) // (values.shape[axis_at] // blocks)).reshape((-1,) + (1,) * (values.ndim - 1 - axis_at))

    one_side = jax.random.permutation(stream_key, blocks)[block_of(target)]
    other_side = (block_of(target) + blocks // 2) % blocks
    return jnp.where((block_of(source) == one_side) | (block_of(source) == other_side), factor * values, values)


def block_levels(key, shape, split, low, top_value):
    gain = 1.0
    for axis_at, shards_of in split:
        heights = jax.random.uniform(jax.random.fold_in(jax.random.fold_in(key, 6), axis_at), (shards_of,), jnp.float32, low / len(split), top_value / len(split))
        gain = gain * jnp.repeat(jnp.exp(heights), shape[axis_at] // shards_of).reshape((-1,) + (1,) * (len(shape) - 1 - axis_at))
    return gain


def bell_draw(stream_key, dims, scale, most, shards=(), held_as=jnp.bfloat16):
    gain = block_levels(stream_key, dims, shards, -0.22, 0.18) if shards else 1.0
    array = jax.random.normal(stream_key, dims, jnp.float32) * scale * gain
    return jnp.minimum(jnp.maximum(array, -most), most).astype(held_as)


def bell_draw_with(key, extent, spread, reach, cuts, heavy, held_as=jnp.bfloat16):
    array = spread * jax.random.normal(key, extent, jnp.float32)
    if cuts:
        array = array * block_levels(key, extent, cuts, -0.22, 0.18)
    return jnp.clip(with_spikes(array, jax.random.fold_in(key, 3), *heavy), -reach, reach).astype(held_as)


def setup_inputs(seed: int = 0) -> dict:
    key_list = jax.random.split(jax.random.key(seed), 8)
    return {
        "activations": bell_draw_with(key_list[0], (TOKENS, D), 1.0, 6.0, ((0, 32),), (0, 1, 32, 2.75)),
        "grads_out": bell_draw_with(key_list[1], (TOKENS, D_OUT), 1.0, 6.0, ((0, 32),), (0, 1, 32, 2.75)),
        "grad_parts": draw_grad_parts(jax.random.fold_in(key_list[7], 71), 0),
        "old_factors": draw_old_factors(jax.random.fold_in(key_list[7], 71), 0),
        "block_owner": draw_block_owner(jax.random.fold_in(key_list[7], 71), 0),
        "weights": bell_draw(key_list[5], (D, D_OUT), D ** -0.5, 0.1875, ((0, 8), (1, 4)), jnp.float32),
        "momentum": bell_draw(key_list[6], (D, D_OUT), 0.3, 4.0, ((0, 8), (1, 4)), jnp.float32),
    }


exact_mode = lax.Precision.HIGHEST
decay_rate = 0.75
damping = 0.1
damp_shift = 0.001
clip_norm = 256.0
momentum_rate = 0.9
step_rate = 0.05

def block_stats(samples):
    block_count = samples.shape[1] // BLOCK_ORDER_SIZE
    pieces = samples.reshape(-1, TOK_DEV, block_count, BLOCK_ORDER_SIZE)

    def accumulate(summed, shard_piece):
        widened = shard_piece.astype(jnp.float32)
        return (summed + jnp.einsum('tnb,tnc->nbc', widened, widened, precision=exact_mode), None)
    summed, _ = lax.scan(accumulate, jnp.zeros((block_count, BLOCK_ORDER_SIZE, BLOCK_ORDER_SIZE), jnp.float32), pieces)
    return summed

def newton_inverse(mixed_factor_blocks):
    block_size = mixed_factor_blocks.shape[-1]
    identity = jnp.eye(block_size, dtype=jnp.float32)
    traces = jnp.trace(mixed_factor_blocks, axis1=1, axis2=2)
    damped = mixed_factor_blocks + (damping * traces / block_size + damp_shift)[:, None, None] * identity
    bounds = lax.optimization_barrier(jnp.max(lax.optimization_barrier(jnp.sum(jnp.abs(damped), axis=2)), axis=1))
    approx = identity[None, :, :] / bounds[:, None, None]
    for iteration in range(NS_STEPS):
        left_part = jnp.einsum('nab,nbc->nac', approx, damped, precision=exact_mode)
        approx = 2.0 * approx - jnp.einsum('nab,nbc->nac', left_part, approx, precision=exact_mode)
    return approx

def reference(activations, grads_out, grad_parts, old_factors, block_owner, weights, momentum):
    sample_count = activations.shape[0]
    statistics = jnp.concatenate([block_stats(activations), block_stats(grads_out)], axis=0) / sample_count
    mixed_factor_blocks = decay_rate * old_factors + (1.0 - decay_rate) * statistics
    inverses = newton_inverse(mixed_factor_blocks)
    left_count = D // BLOCK_ORDER_SIZE
    gradient = lax.optimization_barrier(jnp.sum(grad_parts, axis=0))
    left_part = jnp.einsum('nab,nbc->nac', inverses[:left_count], gradient.reshape(left_count, BLOCK_ORDER_SIZE, D_OUT), precision=exact_mode).reshape(D, D_OUT)
    precond = jnp.einsum('rnb,nbc->rnc', left_part.reshape(D, D_OUT // BLOCK_ORDER_SIZE, BLOCK_ORDER_SIZE), inverses[left_count:], precision=exact_mode).reshape(D, D_OUT)
    alignment_sum = jnp.sum(precond * gradient)
    clip_scale = jnp.minimum(1.0, clip_norm / jnp.sqrt(alignment_sum))
    momentum_next = momentum_rate * momentum + clip_scale * precond
    weights_next = weights - step_rate * momentum_next
    positions = jnp.arange(NBLK, dtype=jnp.int32)
    earlier = (block_owner[:, None] == block_owner[None, :]) & (positions[None, :] < positions[:, None])
    owner_slot_list = (block_owner * BLOCKS_PER_SHARD + lax.optimization_barrier(jnp.sum(earlier.astype(jnp.int32), axis=1))).astype(jnp.int32)
    next_factor_blocks = jnp.zeros((OWNER_SLOT_TOTAL, BLOCK_ORDER_SIZE, BLOCK_ORDER_SIZE), jnp.float32).at[owner_slot_list].set(mixed_factor_blocks)
    return (weights_next, momentum_next, next_factor_blocks)
```

```python
import functools

import jax
import jax.numpy as jnp
from jax import lax
from jax.experimental import pallas as pl
from jax.experimental.pallas import tpu as pltpu
from jax.sharding import PartitionSpec as P

MESH = pl.DeviceIdType.MESH

NS_STEPS = 4


exact_mode = lax.Precision.HIGHEST
decay_rate = 0.75
damping = 0.1
damp_shift = 0.001
clip_norm = 256.0
momentum_rate = 0.9
step_rate = 0.05


def sample_stats(samples, block_size):
    sample_rows, width = samples.shape
    blocks = samples.reshape(sample_rows, width // block_size, block_size)
    return jnp.einsum("tnb,tnc->nbc", blocks, blocks, preferred_element_type=jnp.float32)


def build_slots(block_owner, capacity, slot_count):
    block_count = block_owner.shape[0]
    positions = jnp.arange(block_count, dtype=jnp.int32)
    earlier = (block_owner[:, None] == block_owner[None, :]) & (
        positions[None, :] < positions[:, None]
    )
    owner_slot_list = block_owner * capacity + jnp.sum(earlier.astype(jnp.int32), axis=1)
    return (owner_slot_list[None, :] == jnp.arange(slot_count, dtype=jnp.int32)[:, None]).astype(
        jnp.float32
    )


def newton_inverse(mixed_factor_blocks):
    block_size = mixed_factor_blocks.shape[-1]
    identity = jnp.eye(block_size, dtype=jnp.float32)
    traces = jnp.trace(mixed_factor_blocks, axis1=1, axis2=2)
    damped = (
        mixed_factor_blocks + (damping * traces / block_size + damp_shift)[:, None, None] * identity
    )
    bounds = jnp.max(jnp.sum(jnp.abs(damped), axis=2), axis=1)
    approx = identity[None, :, :] / bounds[:, None, None]
    for iteration in range(NS_STEPS):
        left_part = jnp.einsum("nab,nbc->nac", approx, damped, precision=exact_mode)
        approx = 2.0 * approx - jnp.einsum("nab,nbc->nac", left_part, approx, precision=exact_mode)
    return approx


def apply_right(left_part, right_inv, block_size):
    row_count, col_count = left_part.shape
    right_count = col_count // block_size
    return jnp.einsum(
        "rnb,nbc->rnc",
        left_part.reshape(row_count, right_count, block_size),
        right_inv,
        precision=exact_mode,
    ).reshape(row_count, col_count)


def body(activations, grads_out, grad_parts, old_factors, block_owner, weights, momentum):
    shard_count = lax.axis_size("shards")
    block_count = old_factors.shape[0]
    block_size = old_factors.shape[1]
    capacity = (block_count + shard_count - 1) // shard_count + 1
    slot_count = capacity * shard_count
    slot_table = build_slots(block_owner, capacity, slot_count)
    local_stats = jnp.concatenate(
        [sample_stats(activations, block_size), sample_stats(grads_out, block_size)], axis=0
    )
    packed = jnp.dot(
        slot_table, local_stats.reshape(block_count, block_size * block_size), precision=exact_mode
    )
    first_slot = lax.axis_index("shards") * capacity
    summed = lax.psum(packed, ("shards", "tensor", "replica"))
    owned = lax.dynamic_slice_in_dim(summed, first_slot, capacity, 0)
    sample_count = (
        activations.shape[0] * shard_count * lax.axis_size("tensor") * lax.axis_size("replica")
    )
    owned_table = lax.dynamic_slice_in_dim(slot_table, first_slot, capacity, 0)
    old_owned = jnp.dot(
        owned_table, old_factors.reshape(block_count, block_size * block_size), precision=exact_mode
    )
    mixed_factor_blocks = (
        decay_rate * old_owned + (1.0 - decay_rate) * (owned / sample_count)
    ).reshape(capacity, block_size, block_size)
    inverse_owned = newton_inverse(mixed_factor_blocks)
    start_blocks = jnp.zeros((block_count, block_size * block_size), jnp.float32)
    shard_piece = lax.all_gather(inverse_owned, "shards", axis=0, tiled=True)
    piece_rows = shard_piece.shape[0]
    rows_table = lax.slice_in_dim(slot_table, 0, piece_rows, axis=0)
    flat_piece = shard_piece.reshape(piece_rows, block_size * block_size)
    inverse_flat = start_blocks + jnp.einsum(
        "sb,sk->bk", rows_table, flat_piece, precision=exact_mode
    )
    inverse_blocks = inverse_flat.reshape(block_count, block_size, block_size)
    partial_grad = grad_parts[0]
    row_count, col_count = partial_grad.shape
    left_count = row_count // block_size
    right_count = col_count // block_size
    right_first = left_count + lax.axis_index("tensor") * right_count
    right_inv = lax.dynamic_slice_in_dim(inverse_blocks, right_first, right_count, 0)
    left_part = jnp.einsum(
        "nab,nbc->nac",
        inverse_blocks[:left_count],
        partial_grad.reshape(left_count, block_size, col_count),
        precision=exact_mode,
    ).reshape(row_count, col_count)
    precond = apply_right(left_part, right_inv, block_size)
    total_precond, total_grad = (
        lax.psum_scatter(precond, ("shards", "replica"), scatter_dimension=0, tiled=True),
        lax.psum_scatter(partial_grad, ("shards", "replica"), scatter_dimension=0, tiled=True),
    )
    alignment_sum = lax.psum(jnp.sum(total_precond * total_grad), ("shards", "tensor", "replica"))
    clip_scale = jnp.minimum(1.0, clip_norm / jnp.sqrt(alignment_sum))
    momentum_next = momentum_rate * momentum + clip_scale * total_precond
    weights_next = weights - step_rate * momentum_next
    gathered = lax.all_gather(weights_next, ("shards", "replica"), axis=0, tiled=True)
    return (gathered, momentum_next, mixed_factor_blocks)


def remote(src, dst, sends, recvs, index, device):
    return pltpu.make_async_remote_copy(
        src_ref=src,
        dst_ref=dst,
        send_sem=sends.at[index],
        recv_sem=recvs.at[index],
        device_id=device,
        device_id_type=MESH,
    )


def unpack_pair(packed, diagonal, lower, on_diagonal):
    flipped = packed.T
    first = jnp.where(lower, flipped, packed)
    second = jnp.where(lower, packed, jnp.where(on_diagonal, diagonal, flipped))
    return first, second


def dot_exact(a, b):
    return jnp.dot(a, b, precision=exact_mode, preferred_element_type=jnp.float32)


def fused_kernel(
    sample_total,
    owner_ref,
    act_ref,
    gout_ref,
    grad_ref,
    old_ref,
    weights_ref,
    momentum_ref,
    weights_out,
    momentum_out,
    factors_out,
    act_v,
    gout_v,
    packed_v,
    core_in,
    y_in,
    z_out,
    z_in,
    x_out,
    x_in,
    full_v,
    diag_out,
    diag_in,
    diag_z,
    grad_own,
    grad_x,
    grad_z,
    sum_out,
    sum_xz,
    sum_tensor,
    new_weights,
    mixed_v,
    local_sem,
    sends,
    recvs,
):
    s = lax.axis_index("shards")
    t = lax.axis_index("tensor")
    r = lax.axis_index("replica")
    y = t // 2
    c = t % 2
    n = 128
    half = 512
    quarter = 256
    x_peer = (1 - s, t, r)
    y_peer = (s, 2 * (1 - y) + c, r)
    c_peer = (s, 2 * y + 1 - c, r)
    yc_peer = (s, 2 * (1 - y) + 1 - c, r)
    z_ranks = [(r + d) % 4 for d in (1, 2, 3)]
    z_peers = [(s, t, q) for q in z_ranks]
    xz_peers = [(1 - s, t, q) for q in z_ranks]

    def part(ref, start, size):
        return ref.at[pl.ds(pl.multiple_of(start, 8), size)]

    loads = []
    for k, core in enumerate((1 - c, c)):
        columns = pl.ds(pl.multiple_of(core * half, half), half)
        for src, dst in ((act_ref, act_v), (gout_ref, gout_v)):
            copy = pltpu.make_async_copy(
                src.at[:, columns], dst.at[:, columns], local_sem.at[len(loads)]
            )
            copy.start()
            loads.append(copy)
    own_load = pltpu.make_async_copy(
        grad_ref.at[0, pl.ds(pl.multiple_of(s * half, half), half)], grad_own, local_sem.at[4]
    )
    own_load.start()

    barrier = pltpu.get_barrier_semaphore()
    peers = [x_peer, y_peer, c_peer, yc_peer] + z_peers + xz_peers
    for peer in peers:
        pl.semaphore_signal(barrier, inc=1, device_id=peer, device_id_type=MESH)
    pl.semaphore_wait(barrier, len(peers))

    count = 0
    grad_x_copies = []
    for k in range(4):
        copy = remote(
            grad_ref.at[0, pl.ds(pl.multiple_of((1 - s) * half + k * n, n), n)],
            grad_x.at[k],
            sends,
            recvs,
            count,
            x_peer,
        )
        count += 1
        copy.start()
        grad_x_copies.append(copy)

    rows = lax.broadcasted_iota(jnp.int32, (n, n), 0)
    cols = lax.broadcasted_iota(jnp.int32, (n, n), 1)
    lower = rows > cols
    on_diagonal = rows == cols
    pair_rows = lax.broadcasted_iota(jnp.int32, (8, n), 0)
    identity = on_diagonal.astype(jnp.float32)

    diag = jnp.zeros((8, n), jnp.float32)
    core_copies = []
    y_copy = None
    for j, (core, side) in enumerate(((1 - c, 1 - y), (1 - c, y), (c, 1 - y), (c, y))):
        if j % 2 == 0:
            loads[j].wait()
            loads[j + 1].wait()
        start = pl.multiple_of(core * half + side * quarter, quarter)
        columns = pl.ds(start, quarter)
        a = act_v[:, columns]
        g = gout_v[:, columns]
        across = (((0,), (0,)), ((), ()))
        left = lax.dot_general(a, a, across, preferred_element_type=jnp.float32)
        right = lax.dot_general(g, g, across, preferred_element_type=jnp.float32)
        for k in range(2):
            span = slice(k * n, (k + 1) * n)
            second = right[span, span]
            packed_v[pl.ds(start + k * n, n), :] = jnp.where(lower, second, left[span, span])
            row = jnp.sum(jnp.where(on_diagonal, second, 0.0), axis=0, keepdims=True)
            diag = jnp.where(pair_rows == core * 4 + side * 2 + k, row, diag)
        if j < 2:
            copy = remote(
                part(packed_v, start, quarter), core_in.at[j], sends, recvs, count, c_peer
            )
            count += 1
            copy.start()
            core_copies.append(copy)
        elif j == 2:
            core_copies[0].wait()
            packed_v[pl.ds(start, quarter), :] += core_in[0]
            y_copy = remote(part(packed_v, start, quarter), y_in, sends, recvs, count, y_peer)
            count += 1
            y_copy.start()
    diag_out[0] = diag
    copy = remote(diag_out.at[0], diag_in.at[0], sends, recvs, count, c_peer)
    count += 1
    copy.start()
    core_copies[1].wait()
    copy.wait()
    diag = diag + diag_in[0]
    diag_out[1] = diag
    diag_copy = remote(diag_out.at[1], diag_in.at[1], sends, recvs, count, y_peer)
    count += 1
    diag_copy.start()
    start = pl.multiple_of(c * half + y * quarter, quarter)
    mine = packed_v[pl.ds(start, quarter), :] + core_in[1]
    y_copy.wait()
    z_out[...] = (mine + y_in[...]).reshape(4, 64, n)
    z_copies = []
    for d in range(3):
        copy = remote(z_out.at[z_ranks[d]], z_in.at[r], sends, recvs, count, z_peers[d])
        count += 1
        copy.start()
        z_copies.append(copy)
    diag_copy.wait()
    diag = diag + diag_in[1]
    diag_out[2] = diag
    for d in range(3):
        copy = remote(diag_out.at[2], diag_z.at[r], sends, recvs, count, z_peers[d])
        count += 1
        copy.start()
        z_copies.append(copy)
    z_in[r] = z_out[r]
    diag_z[r] = diag
    for copy in z_copies:
        copy.wait()
    x_out[...] = (z_in[0] + z_in[1]) + (z_in[2] + z_in[3])
    x_copy = remote(part(x_out, (1 - s) * 32, 32), x_in, sends, recvs, count, x_peer)
    count += 1
    x_copy.start()
    diag = (diag_z[0] + diag_z[1]) + (diag_z[2] + diag_z[3])
    diag_out[3] = diag
    diag_copy = remote(diag_out.at[3], diag_in.at[2], sends, recvs, count, x_peer)
    count += 1
    diag_copy.start()
    x_copy.wait()
    z_base = c * half + y * quarter + r * 64
    start = pl.multiple_of(z_base + s * 32, 32)
    full_v[pl.ds(start, 32), :] = x_out[pl.ds(pl.multiple_of(s * 32, 32), 32), :] + x_in[...]
    region = part(full_v, start, 32)
    copy = remote(region, region, sends, recvs, count, x_peer)
    count += 1
    copy.start()
    diag_copy.wait()
    diag = diag + diag_in[2]
    diag_out[4] = diag
    copy.wait()
    z_copies = []
    region = part(full_v, z_base, 64)
    for d in range(3):
        copy = remote(region, region, sends, recvs, count, z_peers[d])
        count += 1
        copy.start()
        z_copies.append(copy)
    own_load.wait()
    for copy in z_copies:
        copy.wait()
    region = part(full_v, c * half + y * quarter, quarter)
    y_copy = remote(region, region, sends, recvs, count, y_peer)
    count += 1
    y_copy.start()
    for k in range(4):
        grad_x_copies[k].wait()
        grad_x[k] = grad_x[k] + grad_own[pl.ds(k * n, n), :]
    grad_copies = []
    for d in range(3):
        copy = remote(grad_x.at[z_ranks[d]], grad_z.at[r], sends, recvs, count, z_peers[d])
        count += 1
        copy.start()
        grad_copies.append(copy)
    grad_z[r] = grad_x[r]
    y_copy.wait()
    region = part(full_v, c * half, half)
    copy = remote(region, region, sends, recvs, count, c_peer)
    count += 1
    copy.start()
    copy.wait()

    def blend(pair):
        first, second = unpack_pair(
            full_v[pl.ds(pl.multiple_of(pair * n, n), n), :],
            diag_out[4, pl.ds(pair, 1), :],
            lower,
            on_diagonal,
        )
        return (
            decay_rate * old_ref[pair] + (1.0 - decay_rate) * (first / sample_total),
            decay_rate * old_ref[8 + pair] + (1.0 - decay_rate) * (second / sample_total),
        )

    mixed = [blend(s * 4 + r)[0], blend(2 * t)[1], blend(2 * t + 1)[1]]
    scales, rests = [], []
    for block in mixed:
        trace = jnp.sum(jnp.where(on_diagonal, block, 0.0), keepdims=True)
        damped = block + (damping * trace / n + damp_shift) * identity
        bound = jnp.max(
            jnp.sum(jnp.abs(damped), axis=1, keepdims=True), axis=0, keepdims=True
        )
        scales.append(1.0 / bound)
        rests.append(identity - damped / bound)
    inverses = [identity + rest for rest in rests]
    for _ in range(NS_STEPS - 1):
        rests = [dot_exact(rest, rest) for rest in rests]
        inverses = [inv + dot_exact(inv, rest) for inv, rest in zip(inverses, rests)]
    inverses = [inv * scale for inv, scale in zip(inverses, scales)]

    for copy in grad_copies:
        copy.wait()
    gradient = (grad_z[0] + grad_z[1]) + (grad_z[2] + grad_z[3])
    left = dot_exact(inverses[0], gradient)
    precond = jnp.concatenate(
        [dot_exact(left[:, :n], inverses[1]), dot_exact(left[:, n:], inverses[2])], axis=1
    )
    products = precond * gradient
    products = products[:, :n] + products[:, n:]
    tile = jnp.sum(products.reshape(16, 8, n), axis=0)

    place = s * 4 + r
    sum_out[0] = tile
    sum_copies = []
    for peer in [x_peer] + z_peers + xz_peers:
        copy = remote(sum_out.at[0], sum_xz.at[place], sends, recvs, count, peer)
        count += 1
        copy.start()
        sum_copies.append(copy)
    sum_xz[place] = tile
    for copy in sum_copies:
        copy.wait()
    tile = jnp.sum(sum_xz[...], axis=0)
    sum_out[1] = tile
    sum_copies = []
    for peer in (c_peer, y_peer, yc_peer):
        copy = remote(sum_out.at[1], sum_tensor.at[t], sends, recvs, count, peer)
        count += 1
        copy.start()
        sum_copies.append(copy)
    sum_tensor[t] = tile
    for copy in sum_copies:
        copy.wait()
    alignment = jnp.sum(jnp.sum(sum_tensor[...], axis=0), keepdims=True)
    clip_scale = jnp.minimum(1.0, clip_norm / jnp.sqrt(alignment))
    momentum_next = momentum_rate * momentum_ref[...] + clip_scale * precond
    momentum_out[...] = momentum_next
    new_weights[...] = weights_ref[...] - step_rate * momentum_next

    target = part(weights_out, place * n, n)
    own_store = pltpu.make_async_copy(new_weights, target, local_sem.at[5])
    own_store.start()
    gather = []
    for peer in z_peers + [x_peer]:
        copy = remote(new_weights, target, sends, recvs, count, peer)
        count += 1
        copy.start()
        gather.append(copy)

    for pair in range(8):
        mixed_v[pair], mixed_v[8 + pair] = blend(pair)
    mixed_v[16] = jnp.zeros((n, n), jnp.float32)
    block_total = owner_ref.shape[0]
    chosen = [jnp.int32(block_total)] * factors_out.shape[0]
    used = jnp.int32(0)
    for b in range(block_total):
        here = owner_ref[b] == s
        for k in range(min(b + 1, len(chosen))):
            chosen[k] = jnp.where(here & (used == k), jnp.int32(b), chosen[k])
        used = used + jnp.where(here, jnp.int32(1), jnp.int32(0))
    for k in range(len(chosen)):
        factors_out[k] = mixed_v[chosen[k]]

    for d in range(3):
        gather[d].wait()
        origin = s * 4 + (r + 3 - d) % 4
        region = part(weights_out, origin * n, n)
        copy = remote(region, region, sends, recvs, count, x_peer)
        count += 1
        copy.start()
        gather.append(copy)
    for copy in gather[3:]:
        copy.wait()
    own_store.wait()


def fused_step(activations, grads_out, grad_parts, old_factors, block_owner, weights, momentum):
    n = old_factors.shape[1]
    shards = lax.axis_size("shards")
    capacity = (old_factors.shape[0] + shards - 1) // shards + 1
    devices = shards * lax.axis_size("tensor") * lax.axis_size("replica")
    f32 = jnp.float32
    anywhere = pl.BlockSpec(memory_space=pl.ANY)
    vmem = pl.BlockSpec(memory_space=pltpu.VMEM)
    return pl.pallas_call(
        functools.partial(fused_kernel, float(activations.shape[0] * devices)),
        out_shape=(
            jax.ShapeDtypeStruct(grad_parts.shape[1:], f32),
            jax.ShapeDtypeStruct(momentum.shape, f32),
            jax.ShapeDtypeStruct((capacity, n, n), f32),
        ),
        in_specs=[
            pl.BlockSpec(memory_space=pltpu.SMEM),
            anywhere,
            anywhere,
            anywhere,
            vmem,
            vmem,
            vmem,
        ],
        out_specs=(anywhere, vmem, vmem),
        scratch_shapes=[
            pltpu.VMEM(activations.shape, activations.dtype),
            pltpu.VMEM(grads_out.shape, grads_out.dtype),
            pltpu.VMEM((1024, n), f32),
            pltpu.VMEM((2, 256, n), f32),
            pltpu.VMEM((256, n), f32),
            pltpu.VMEM((4, 64, n), f32),
            pltpu.VMEM((4, 64, n), f32),
            pltpu.VMEM((64, n), f32),
            pltpu.VMEM((32, n), f32),
            pltpu.VMEM((1024, n), f32),
            pltpu.VMEM((5, 8, n), f32),
            pltpu.VMEM((3, 8, n), f32),
            pltpu.VMEM((4, 8, n), f32),
            pltpu.VMEM((512, 256), f32),
            pltpu.VMEM((4, n, 256), f32),
            pltpu.VMEM((4, n, 256), f32),
            pltpu.VMEM((2, 8, n), f32),
            pltpu.VMEM((8, 8, n), f32),
            pltpu.VMEM((4, 8, n), f32),
            pltpu.VMEM((n, 256), f32),
            pltpu.VMEM((17, n, n), f32),
            pltpu.SemaphoreType.DMA((6,)),
            pltpu.SemaphoreType.DMA((48,)),
            pltpu.SemaphoreType.DMA((48,)),
        ],
        compiler_params=pltpu.CompilerParams(
            collective_id=0, has_side_effects=True, vmem_limit_bytes=40 * 1024 * 1024
        ),
        cost_estimate=pl.CostEstimate(
            flops=1_200_000_000, bytes_accessed=10_000_000, transcendentals=0
        ),
    )(block_owner, activations, grads_out, grad_parts, old_factors, weights, momentum)


def step(activations, grads_out, grad_parts, old_factors, block_owner, weights, momentum):
    sizes = tuple(lax.axis_size(name) for name in ("shards", "tensor", "replica"))
    fits = (
        sizes == (2, 4, 4)
        and weights.shape == (128, 256)
        and old_factors.shape == (16, 128, 128)
        and activations.shape == grads_out.shape == (1024, 1024)
    )
    chosen = fused_step if fits else body
    return chosen(
        activations, grads_out, grad_parts, old_factors, block_owner, weights, momentum
    )


def solution(mesh):
    placed = (
        P(("shards", "tensor", "replica"), None),
        P(("shards", "tensor", "replica"), None),
        P(("shards", "replica"), None, "tensor"),
        P(),
        P(),
        P(("shards", "replica"), "tensor"),
        P(("shards", "replica"), "tensor"),
    )
    return jax.shard_map(
        step,
        mesh=mesh,
        in_specs=placed,
        out_specs=(P(None, "tensor"), P(("shards", "replica"), "tensor"), P("shards", None, None)),
        check_vma=False,
    )
```

```python
import functools

import jax
import jax.numpy as jnp
from jax import lax
from jax.experimental import pallas as pl
from jax.experimental.pallas import tpu as pltpu
from jax.sharding import PartitionSpec as P

MESH = pl.DeviceIdType.MESH

NS_STEPS = 4


exact_mode = lax.Precision.HIGHEST
decay_rate = 0.75
damping = 0.1
damp_shift = 0.001
clip_norm = 256.0
momentum_rate = 0.9
step_rate = 0.05


def sample_stats(samples, block_size):
    sample_rows, width = samples.shape
    blocks = samples.reshape(sample_rows, width // block_size, block_size)
    return jnp.einsum("tnb,tnc->nbc", blocks, blocks, preferred_element_type=jnp.float32)


def build_slots(block_owner, capacity, slot_count):
    block_count = block_owner.shape[0]
    positions = jnp.arange(block_count, dtype=jnp.int32)
    earlier = (block_owner[:, None] == block_owner[None, :]) & (
        positions[None, :] < positions[:, None]
    )
    owner_slot_list = block_owner * capacity + jnp.sum(earlier.astype(jnp.int32), axis=1)
    return (owner_slot_list[None, :] == jnp.arange(slot_count, dtype=jnp.int32)[:, None]).astype(
        jnp.float32
    )


def newton_inverse(mixed_factor_blocks):
    block_size = mixed_factor_blocks.shape[-1]
    identity = jnp.eye(block_size, dtype=jnp.float32)
    traces = jnp.trace(mixed_factor_blocks, axis1=1, axis2=2)
    damped = (
        mixed_factor_blocks + (damping * traces / block_size + damp_shift)[:, None, None] * identity
    )
    bounds = jnp.max(jnp.sum(jnp.abs(damped), axis=2), axis=1)
    approx = identity[None, :, :] / bounds[:, None, None]
    for iteration in range(NS_STEPS):
        left_part = jnp.einsum("nab,nbc->nac", approx, damped, precision=exact_mode)
        approx = 2.0 * approx - jnp.einsum("nab,nbc->nac", left_part, approx, precision=exact_mode)
    return approx


def apply_right(left_part, right_inv, block_size):
    row_count, col_count = left_part.shape
    right_count = col_count // block_size
    return jnp.einsum(
        "rnb,nbc->rnc",
        left_part.reshape(row_count, right_count, block_size),
        right_inv,
        precision=exact_mode,
    ).reshape(row_count, col_count)


def body(activations, grads_out, grad_parts, old_factors, block_owner, weights, momentum):
    shard_count = lax.axis_size("shards")
    block_count = old_factors.shape[0]
    block_size = old_factors.shape[1]
    capacity = (block_count + shard_count - 1) // shard_count + 1
    slot_count = capacity * shard_count
    slot_table = build_slots(block_owner, capacity, slot_count)
    local_stats = jnp.concatenate(
        [sample_stats(activations, block_size), sample_stats(grads_out, block_size)], axis=0
    )
    packed = jnp.dot(
        slot_table, local_stats.reshape(block_count, block_size * block_size), precision=exact_mode
    )
    first_slot = lax.axis_index("shards") * capacity
    summed = lax.psum(packed, ("shards", "tensor", "replica"))
    owned = lax.dynamic_slice_in_dim(summed, first_slot, capacity, 0)
    sample_count = (
        activations.shape[0] * shard_count * lax.axis_size("tensor") * lax.axis_size("replica")
    )
    owned_table = lax.dynamic_slice_in_dim(slot_table, first_slot, capacity, 0)
    old_owned = jnp.dot(
        owned_table, old_factors.reshape(block_count, block_size * block_size), precision=exact_mode
    )
    mixed_factor_blocks = (
        decay_rate * old_owned + (1.0 - decay_rate) * (owned / sample_count)
    ).reshape(capacity, block_size, block_size)
    inverse_owned = newton_inverse(mixed_factor_blocks)
    start_blocks = jnp.zeros((block_count, block_size * block_size), jnp.float32)
    shard_piece = lax.all_gather(inverse_owned, "shards", axis=0, tiled=True)
    piece_rows = shard_piece.shape[0]
    rows_table = lax.slice_in_dim(slot_table, 0, piece_rows, axis=0)
    flat_piece = shard_piece.reshape(piece_rows, block_size * block_size)
    inverse_flat = start_blocks + jnp.einsum(
        "sb,sk->bk", rows_table, flat_piece, precision=exact_mode
    )
    inverse_blocks = inverse_flat.reshape(block_count, block_size, block_size)
    partial_grad = grad_parts[0]
    row_count, col_count = partial_grad.shape
    left_count = row_count // block_size
    right_count = col_count // block_size
    right_first = left_count + lax.axis_index("tensor") * right_count
    right_inv = lax.dynamic_slice_in_dim(inverse_blocks, right_first, right_count, 0)
    left_part = jnp.einsum(
        "nab,nbc->nac",
        inverse_blocks[:left_count],
        partial_grad.reshape(left_count, block_size, col_count),
        precision=exact_mode,
    ).reshape(row_count, col_count)
    precond = apply_right(left_part, right_inv, block_size)
    total_precond, total_grad = (
        lax.psum_scatter(precond, ("shards", "replica"), scatter_dimension=0, tiled=True),
        lax.psum_scatter(partial_grad, ("shards", "replica"), scatter_dimension=0, tiled=True),
    )
    alignment_sum = lax.psum(jnp.sum(total_precond * total_grad), ("shards", "tensor", "replica"))
    clip_scale = jnp.minimum(1.0, clip_norm / jnp.sqrt(alignment_sum))
    momentum_next = momentum_rate * momentum + clip_scale * total_precond
    weights_next = weights - step_rate * momentum_next
    gathered = lax.all_gather(weights_next, ("shards", "replica"), axis=0, tiled=True)
    return (gathered, momentum_next, mixed_factor_blocks)


def remote(src, dst, sends, recvs, index, device):
    return pltpu.make_async_remote_copy(
        src_ref=src,
        dst_ref=dst,
        send_sem=sends.at[index],
        recv_sem=recvs.at[index],
        device_id=device,
        device_id_type=MESH,
    )


def unpack_pair(packed, diagonal, lower, on_diagonal):
    flipped = packed.T
    first = jnp.where(lower, flipped, packed)
    second = jnp.where(lower, packed, jnp.where(on_diagonal, diagonal, flipped))
    return first, second


def split_halves(a):
    high = a.astype(jnp.bfloat16)
    return high, (a - high.astype(jnp.float32)).astype(jnp.bfloat16)


def dot_exact(a, b):
    a_high, a_low = split_halves(a)
    b_high, b_low = split_halves(b)
    dot = functools.partial(jnp.dot, preferred_element_type=jnp.float32)
    return dot(a_high, b_high) + (dot(a_high, b_low) + dot(a_low, b_high))


def ordered_sum(ref, count):
    terms = [ref[k] for k in range(count)]
    while len(terms) > 1:
        terms = [terms[k] + terms[k + 1] for k in range(0, len(terms), 2)]
    return terms[0]


def fused_kernel(
    sample_total,
    owner_ref,
    act_ref,
    gout_ref,
    grad_ref,
    old_ref,
    weights_ref,
    momentum_ref,
    weights_out,
    momentum_out,
    factors_out,
    act_v,
    gout_v,
    old_v,
    weights_v,
    momentum_v,
    packed_v,
    core_in,
    y_in,
    xz_out,
    xz_in,
    full_v,
    diag_out,
    diag_in,
    diag_xz,
    grad_own,
    grad_x,
    grad_z,
    sum_out,
    sum_xz,
    sum_tensor,
    base_all,
    precond_all,
    mixed_v,
    local_sem,
    sends,
    recvs,
):
    s = lax.axis_index("shards")
    t = lax.axis_index("tensor")
    r = lax.axis_index("replica")
    y = t // 2
    c = t % 2
    n = 128
    half = 512
    quarter = 256
    place = s * 4 + r
    x_peer = (1 - s, t, r)
    y_peer = (s, 2 * (1 - y) + c, r)
    c_peer = (s, 2 * y + 1 - c, r)
    yc_peer = (s, 2 * (1 - y) + 1 - c, r)
    z_ranks = [(r + d) % 4 for d in (1, 2, 3)]
    z_peers = [(s, t, q) for q in z_ranks]
    xz_peers = z_peers + [(1 - s, t, q) for q in z_ranks] + [x_peer]
    xz_places = [s * 4 + q for q in z_ranks] + [(1 - s) * 4 + q for q in z_ranks]
    xz_places = xz_places + [(1 - s) * 4 + r]
    used_sems = [0]

    def part(ref, start, size):
        return ref.at[pl.ds(pl.multiple_of(start, 8), size)]

    def send(src, dst, device):
        copy = remote(src, dst, sends, recvs, used_sems[0], device)
        used_sems[0] += 1
        copy.start()
        return copy

    def load(src, dst, index):
        copy = pltpu.make_async_copy(src, dst, local_sem.at[index])
        copy.start()
        return copy

    barrier = pltpu.get_barrier_semaphore()
    peers = xz_peers + [y_peer, c_peer, yc_peer]
    for peer in peers:
        pl.semaphore_signal(barrier, inc=1, device_id=peer, device_id_type=MESH)

    groups = ((1 - y, 1 - c), (y, 1 - c), (1 - y, c), (y, c))
    starts = [pl.multiple_of(side * half + core * quarter, quarter) for side, core in groups]
    loads = []
    for k, start in enumerate(starts):
        columns = pl.ds(start, quarter)
        loads.append(load(act_ref.at[:, columns], act_v.at[:, columns], 2 * k))
        loads.append(load(gout_ref.at[:, columns], gout_v.at[:, columns], 2 * k + 1))
    weights_load = load(weights_ref, weights_v, 8)
    momentum_load = load(momentum_ref, momentum_v, 9)
    own_load = load(
        grad_ref.at[0, pl.ds(pl.multiple_of(s * half, half), half)], grad_own, 10
    )
    old_load = load(old_ref, old_v, 11)

    rows = lax.broadcasted_iota(jnp.int32, (n, n), 0)
    cols = lax.broadcasted_iota(jnp.int32, (n, n), 1)
    lower = rows > cols
    on_diagonal = rows == cols
    pair_rows = lax.broadcasted_iota(jnp.int32, (8, n), 0)
    identity = on_diagonal.astype(jnp.float32)

    diag = jnp.zeros((8, n), jnp.float32)
    core_copies = []
    for j, (side, core) in enumerate(groups):
        loads[2 * j].wait()
        loads[2 * j + 1].wait()
        start = starts[j]
        a = act_v[:, pl.ds(start, quarter)]
        g = gout_v[:, pl.ds(start, quarter)]
        across = (((0,), (0,)), ((), ()))
        left = lax.dot_general(a, a, across, preferred_element_type=jnp.float32)
        right = lax.dot_general(g, g, across, preferred_element_type=jnp.float32)
        for k in range(2):
            span = slice(k * n, (k + 1) * n)
            second = right[span, span]
            packed_v[pl.ds(start + k * n, n), :] = jnp.where(lower, second, left[span, span])
            row = jnp.sum(jnp.where(on_diagonal, second, 0.0), axis=0, keepdims=True)
            diag = jnp.where(pair_rows == side * 4 + core * 2 + k, row, diag)
        if j == 0:
            pl.semaphore_wait(barrier, len(peers))
        if j < 2:
            core_copies.append(send(part(packed_v, start, quarter), core_in.at[j], c_peer))
        if j == 0:
            grad_x_copies = [
                send(
                    grad_ref.at[0, pl.ds(pl.multiple_of((1 - s) * half + k * n, n), n)],
                    grad_x.at[k],
                    x_peer,
                )
                for k in range(4)
            ]
        elif j == 1:
            weights_load.wait()
            momentum_load.wait()
            own_rows = pl.ds(pl.multiple_of(place * n, n), n)
            base_all[own_rows, :] = weights_v[...] - (step_rate * momentum_rate) * momentum_v[...]
            base_own = part(base_all, place * n, n)
            base_copies = [send(base_own, base_own, peer) for peer in z_peers]
        elif j == 2:
            core_copies[0].wait()
            packed_v[pl.ds(start, quarter), :] += core_in[0]
            y_copy = send(part(packed_v, start, quarter), y_in, y_peer)
    diag_out[0] = diag
    copy = send(diag_out.at[0], diag_in.at[0], c_peer)
    core_copies[1].wait()
    mine = packed_v[pl.ds(starts[3], quarter), :] + core_in[1]
    copy.wait()
    diag = diag + diag_in[0]
    diag_out[1] = diag
    diag_copy = send(diag_out.at[1], diag_in.at[1], y_peer)
    y_copy.wait()
    xz_out[...] = (mine + y_in[...]).reshape(8, 32, n)
    copies = [
        send(xz_out.at[q], xz_in.at[place], peer) for q, peer in zip(xz_places, xz_peers)
    ]
    diag_copy.wait()
    diag = diag + diag_in[1]
    diag_out[2] = diag
    diag_copies = [send(diag_out.at[2], diag_xz.at[place], peer) for peer in xz_peers]
    xz_in[place] = xz_out[place]
    diag_xz[place] = diag
    for copy in copies:
        copy.wait()
    start = pl.multiple_of(starts[3] + place * 32, 32)
    full_v[pl.ds(start, 32), :] = ordered_sum(xz_in, 8)
    region = part(full_v, start, 32)
    copies = [send(region, region, peer) for peer in xz_peers]
    for copy in diag_copies:
        copy.wait()
    diag_out[3] = ordered_sum(diag_xz, 8)
    own_load.wait()
    for k in range(4):
        grad_x_copies[k].wait()
        grad_x[k] = grad_x[k] + grad_own[pl.ds(k * n, n), :]
    for copy in copies:
        copy.wait()
    region = part(full_v, starts[3], quarter)
    y_copy = send(region, region, y_peer)
    core_copies = [send(region, region, c_peer)]
    grad_copies = [
        send(grad_x.at[q], grad_z.at[r], peer) for q, peer in zip(z_ranks, z_peers)
    ]
    grad_z[r] = grad_x[r]
    for copy in base_copies:
        copy.wait()
    region = part(base_all, s * half, half)
    base_copy = send(region, region, x_peer)

    def blend(pair):
        first, second = unpack_pair(
            full_v[pl.ds(pl.multiple_of(pair * n, n), n), :],
            diag_out[3, pl.ds(pair, 1), :],
            lower,
            on_diagonal,
        )
        return (
            decay_rate * old_v[pair] + (1.0 - decay_rate) * (first / sample_total),
            decay_rate * old_v[8 + pair] + (1.0 - decay_rate) * (second / sample_total),
        )

    def invert(blocks):
        scales, rests = [], []
        for block in blocks:
            trace = jnp.sum(jnp.where(on_diagonal, block, 0.0), keepdims=True)
            damped = block + (damping * trace / n + damp_shift) * identity
            bound = jnp.max(
                jnp.sum(jnp.abs(damped), axis=1, keepdims=True), axis=0, keepdims=True
            )
            scales.append(1.0 / bound)
            rests.append(identity - damped / bound)
        inverses = [identity + rest for rest in rests]
        for _ in range(NS_STEPS - 1):
            rests = [dot_exact(rest, rest) for rest in rests]
            inverses = [inv + dot_exact(inv, rest) for inv, rest in zip(inverses, rests)]
        return [inv * scale for inv, scale in zip(inverses, scales)]

    old_load.wait()
    right_inverses = invert([blend(2 * t)[1], blend(2 * t + 1)[1]])
    y_copy.wait()
    region = part(full_v, starts[2], quarter)
    core_copies.append(send(region, region, c_peer))
    for copy in core_copies:
        copy.wait()
    left_inverse = invert([blend(place)[0]])[0]

    for copy in grad_copies:
        copy.wait()
    gradient = (grad_z[0] + grad_z[1]) + (grad_z[2] + grad_z[3])
    left = dot_exact(left_inverse, gradient)
    precond = jnp.concatenate(
        [dot_exact(left[:, k * n : (k + 1) * n], right_inverses[k]) for k in range(2)], axis=1
    )
    products = precond * gradient
    products = products[:, :n] + products[:, n:]
    tile = jnp.sum(products.reshape(16, 8, n), axis=0)

    sum_out[0] = tile
    sum_copies = [send(sum_out.at[0], sum_xz.at[place], peer) for peer in xz_peers]
    precond_all[pl.ds(pl.multiple_of(place * n, n), n), :] = precond
    own = part(precond_all, place * n, n)
    x_copies = [send(own, own, x_peer)]

    first_sem = used_sems[0]
    used_sems[0] += 14

    def passing(hop, way, peer, hand_on):
        origin = r - hop if way == 0 else r + hop
        region = part(precond_all, (s * 4 + origin) * n, n)
        index = first_sem + 6 * hand_on + 2 * hop + way
        return remote(region, region, sends, recvs, index, peer)

    ways = ((s, t, r + 1), (s, t, r - 1))

    def sends_on(hop, way):
        return (r >= hop) & (r < 3) if way == 0 else (r <= 3 - hop) & (r > 0)

    def gets(hop, way):
        return r >= hop + 1 if way == 0 else r <= 2 - hop

    def start_hop(hop):
        for way in range(2):

            @pl.when(sends_on(hop, way))
            def _():
                passing(hop, way, ways[way], 0).start()

    def arrived(hop):
        for way in range(2):

            @pl.when(gets(hop, way))
            def _():
                back = ways[1 - way]
                origin = r - hop - 1 if way == 0 else r + hop + 1
                region = part(precond_all, (s * 4 + origin) * n, n)
                index = first_sem + 2 * hop + way
                remote(region, region, sends, recvs, index, back).wait_recv()

    def hand_on(hop):
        for way in range(2):

            @pl.when(gets(hop, way))
            def _():
                passing(hop + 1, way, x_peer, 1).start()

    start_hop(0)
    sum_xz[place] = tile
    for copy in sum_copies:
        copy.wait()
    tile = ordered_sum(sum_xz, 8)
    sum_out[1] = tile
    sum_copies = [
        send(sum_out.at[1], sum_tensor.at[t], peer) for peer in (c_peer, y_peer, yc_peer)
    ]
    sum_tensor[t] = tile
    arrived(0)
    start_hop(1)
    hand_on(0)
    for copy in sum_copies:
        copy.wait()
    alignment = jnp.sum(ordered_sum(sum_tensor, 4), keepdims=True)
    clip_scale = jnp.minimum(1.0, clip_norm / jnp.sqrt(alignment))
    momentum_out[...] = momentum_rate * momentum_v[...] + clip_scale * precond
    arrived(1)
    start_hop(2)
    hand_on(1)

    for pair in range(8):
        mixed_v[pair], mixed_v[8 + pair] = blend(pair)
    mixed_v[16] = jnp.zeros((n, n), jnp.float32)
    block_total = owner_ref.shape[0]
    chosen = [jnp.int32(block_total)] * factors_out.shape[0]
    used = jnp.int32(0)
    for b in range(block_total):
        here = owner_ref[b] == s
        for k in range(min(b + 1, len(chosen))):
            chosen[k] = jnp.where(here & (used == k), jnp.int32(b), chosen[k])
        used = used + jnp.where(here, jnp.int32(1), jnp.int32(0))
    for k in range(len(chosen)):
        factors_out[k] = mixed_v[chosen[k]]

    arrived(2)
    hand_on(2)
    base_copy.wait()
    for copy in x_copies:
        copy.wait()
    for hop in range(3):
        for way in range(2):

            @pl.when(sends_on(hop, way))
            def _():
                passing(hop, way, ways[way], 0).wait_send()

            @pl.when(gets(hop, way))
            def _():
                passing(hop + 1, way, x_peer, 1).wait()

    weights_out[...] = base_all[...] - (step_rate * clip_scale) * precond_all[...]


def fused_step(activations, grads_out, grad_parts, old_factors, block_owner, weights, momentum):
    n = old_factors.shape[1]
    shards = lax.axis_size("shards")
    capacity = (old_factors.shape[0] + shards - 1) // shards + 1
    devices = shards * lax.axis_size("tensor") * lax.axis_size("replica")
    f32 = jnp.float32
    anywhere = pl.BlockSpec(memory_space=pl.ANY)
    vmem = pl.BlockSpec(memory_space=pltpu.VMEM)
    return pl.pallas_call(
        functools.partial(fused_kernel, float(activations.shape[0] * devices)),
        out_shape=(
            jax.ShapeDtypeStruct(grad_parts.shape[1:], f32),
            jax.ShapeDtypeStruct(momentum.shape, f32),
            jax.ShapeDtypeStruct((capacity, n, n), f32),
        ),
        in_specs=[
            pl.BlockSpec(memory_space=pltpu.SMEM),
            anywhere,
            anywhere,
            anywhere,
            anywhere,
            anywhere,
            anywhere,
        ],
        out_specs=(vmem, vmem, vmem),
        scratch_shapes=[
            pltpu.VMEM(activations.shape, activations.dtype),
            pltpu.VMEM(grads_out.shape, grads_out.dtype),
            pltpu.VMEM(old_factors.shape, f32),
            pltpu.VMEM(weights.shape, f32),
            pltpu.VMEM(momentum.shape, f32),
            pltpu.VMEM((1024, n), f32),
            pltpu.VMEM((2, 256, n), f32),
            pltpu.VMEM((256, n), f32),
            pltpu.VMEM((8, 32, n), f32),
            pltpu.VMEM((8, 32, n), f32),
            pltpu.VMEM((1024, n), f32),
            pltpu.VMEM((4, 8, n), f32),
            pltpu.VMEM((2, 8, n), f32),
            pltpu.VMEM((8, 8, n), f32),
            pltpu.VMEM((512, 256), f32),
            pltpu.VMEM((4, n, 256), f32),
            pltpu.VMEM((4, n, 256), f32),
            pltpu.VMEM((2, 8, n), f32),
            pltpu.VMEM((8, 8, n), f32),
            pltpu.VMEM((4, 8, n), f32),
            pltpu.VMEM((1024, 256), f32),
            pltpu.VMEM((1024, 256), f32),
            pltpu.VMEM((17, n, n), f32),
            pltpu.SemaphoreType.DMA((12,)),
            pltpu.SemaphoreType.DMA((72,)),
            pltpu.SemaphoreType.DMA((72,)),
        ],
        compiler_params=pltpu.CompilerParams(
            collective_id=0, has_side_effects=True, vmem_limit_bytes=60 * 1024 * 1024
        ),
        cost_estimate=pl.CostEstimate(
            flops=1_200_000_000, bytes_accessed=10_000_000, transcendentals=0
        ),
    )(block_owner, activations, grads_out, grad_parts, old_factors, weights, momentum)


def step(activations, grads_out, grad_parts, old_factors, block_owner, weights, momentum):
    sizes = tuple(lax.axis_size(name) for name in ("shards", "tensor", "replica"))
    fits = (
        sizes == (2, 4, 4)
        and weights.shape == (128, 256)
        and old_factors.shape == (16, 128, 128)
        and activations.shape == grads_out.shape == (1024, 1024)
    )
    chosen = fused_step if fits else body
    return chosen(
        activations, grads_out, grad_parts, old_factors, block_owner, weights, momentum
    )


def solution(mesh):
    placed = (
        P(("shards", "tensor", "replica"), None),
        P(("shards", "tensor", "replica"), None),
        P(("shards", "replica"), None, "tensor"),
        P(),
        P(),
        P(("shards", "replica"), "tensor"),
        P(("shards", "replica"), "tensor"),
    )
    return jax.shard_map(
        step,
        mesh=mesh,
        in_specs=placed,
        out_specs=(P(None, "tensor"), P(("shards", "replica"), "tensor"), P("shards", None, None)),
        check_vma=False,
    )
```

```python
import functools

import jax
import jax.numpy as jnp
from jax import lax
from jax.experimental import pallas as pl
from jax.experimental.pallas import tpu as pltpu
from jax.sharding import PartitionSpec as P

MESH = pl.DeviceIdType.MESH

NS_STEPS = 4


exact_mode = lax.Precision.HIGHEST
decay_rate = 0.75
damping = 0.1
damp_shift = 0.001
clip_norm = 256.0
momentum_rate = 0.9
step_rate = 0.05


def sample_stats(samples, block_size):
    sample_rows, width = samples.shape
    blocks = samples.reshape(sample_rows, width // block_size, block_size)
    return jnp.einsum("tnb,tnc->nbc", blocks, blocks, preferred_element_type=jnp.float32)


def build_slots(block_owner, capacity, slot_count):
    block_count = block_owner.shape[0]
    positions = jnp.arange(block_count, dtype=jnp.int32)
    earlier = (block_owner[:, None] == block_owner[None, :]) & (
        positions[None, :] < positions[:, None]
    )
    owner_slot_list = block_owner * capacity + jnp.sum(earlier.astype(jnp.int32), axis=1)
    return (owner_slot_list[None, :] == jnp.arange(slot_count, dtype=jnp.int32)[:, None]).astype(
        jnp.float32
    )


def newton_inverse(mixed_factor_blocks):
    block_size = mixed_factor_blocks.shape[-1]
    identity = jnp.eye(block_size, dtype=jnp.float32)
    traces = jnp.trace(mixed_factor_blocks, axis1=1, axis2=2)
    damped = (
        mixed_factor_blocks + (damping * traces / block_size + damp_shift)[:, None, None] * identity
    )
    bounds = jnp.max(jnp.sum(jnp.abs(damped), axis=2), axis=1)
    approx = identity[None, :, :] / bounds[:, None, None]
    for iteration in range(NS_STEPS):
        left_part = jnp.einsum("nab,nbc->nac", approx, damped, precision=exact_mode)
        approx = 2.0 * approx - jnp.einsum("nab,nbc->nac", left_part, approx, precision=exact_mode)
    return approx


def apply_right(left_part, right_inv, block_size):
    row_count, col_count = left_part.shape
    right_count = col_count // block_size
    return jnp.einsum(
        "rnb,nbc->rnc",
        left_part.reshape(row_count, right_count, block_size),
        right_inv,
        precision=exact_mode,
    ).reshape(row_count, col_count)


def body(activations, grads_out, grad_parts, old_factors, block_owner, weights, momentum):
    shard_count = lax.axis_size("shards")
    block_count = old_factors.shape[0]
    block_size = old_factors.shape[1]
    capacity = (block_count + shard_count - 1) // shard_count + 1
    slot_count = capacity * shard_count
    slot_table = build_slots(block_owner, capacity, slot_count)
    local_stats = jnp.concatenate(
        [sample_stats(activations, block_size), sample_stats(grads_out, block_size)], axis=0
    )
    packed = jnp.dot(
        slot_table, local_stats.reshape(block_count, block_size * block_size), precision=exact_mode
    )
    first_slot = lax.axis_index("shards") * capacity
    summed = lax.psum(packed, ("shards", "tensor", "replica"))
    owned = lax.dynamic_slice_in_dim(summed, first_slot, capacity, 0)
    sample_count = (
        activations.shape[0] * shard_count * lax.axis_size("tensor") * lax.axis_size("replica")
    )
    owned_table = lax.dynamic_slice_in_dim(slot_table, first_slot, capacity, 0)
    old_owned = jnp.dot(
        owned_table, old_factors.reshape(block_count, block_size * block_size), precision=exact_mode
    )
    mixed_factor_blocks = (
        decay_rate * old_owned + (1.0 - decay_rate) * (owned / sample_count)
    ).reshape(capacity, block_size, block_size)
    inverse_owned = newton_inverse(mixed_factor_blocks)
    start_blocks = jnp.zeros((block_count, block_size * block_size), jnp.float32)
    shard_piece = lax.all_gather(inverse_owned, "shards", axis=0, tiled=True)
    piece_rows = shard_piece.shape[0]
    rows_table = lax.slice_in_dim(slot_table, 0, piece_rows, axis=0)
    flat_piece = shard_piece.reshape(piece_rows, block_size * block_size)
    inverse_flat = start_blocks + jnp.einsum(
        "sb,sk->bk", rows_table, flat_piece, precision=exact_mode
    )
    inverse_blocks = inverse_flat.reshape(block_count, block_size, block_size)
    partial_grad = grad_parts[0]
    row_count, col_count = partial_grad.shape
    left_count = row_count // block_size
    right_count = col_count // block_size
    right_first = left_count + lax.axis_index("tensor") * right_count
    right_inv = lax.dynamic_slice_in_dim(inverse_blocks, right_first, right_count, 0)
    left_part = jnp.einsum(
        "nab,nbc->nac",
        inverse_blocks[:left_count],
        partial_grad.reshape(left_count, block_size, col_count),
        precision=exact_mode,
    ).reshape(row_count, col_count)
    precond = apply_right(left_part, right_inv, block_size)
    total_precond, total_grad = (
        lax.psum_scatter(precond, ("shards", "replica"), scatter_dimension=0, tiled=True),
        lax.psum_scatter(partial_grad, ("shards", "replica"), scatter_dimension=0, tiled=True),
    )
    alignment_sum = lax.psum(jnp.sum(total_precond * total_grad), ("shards", "tensor", "replica"))
    clip_scale = jnp.minimum(1.0, clip_norm / jnp.sqrt(alignment_sum))
    momentum_next = momentum_rate * momentum + clip_scale * total_precond
    weights_next = weights - step_rate * momentum_next
    gathered = lax.all_gather(weights_next, ("shards", "replica"), axis=0, tiled=True)
    return (gathered, momentum_next, mixed_factor_blocks)


def remote(src, dst, sends, recvs, index, device):
    return pltpu.make_async_remote_copy(
        src_ref=src,
        dst_ref=dst,
        send_sem=sends.at[index],
        recv_sem=recvs.at[index],
        device_id=device,
        device_id_type=MESH,
    )


def unpack_pair(packed, diagonal, lower, on_diagonal):
    flipped = packed.T
    first = jnp.where(lower, flipped, packed)
    second = jnp.where(lower, packed, jnp.where(on_diagonal, diagonal, flipped))
    return first, second


def split_halves(a):
    high = a.astype(jnp.bfloat16)
    return high, (a - high.astype(jnp.float32)).astype(jnp.bfloat16)


def dot_exact(a, b):
    a_high, a_low = split_halves(a)
    b_high, b_low = split_halves(b)
    dot = functools.partial(jnp.dot, preferred_element_type=jnp.float32)
    return dot(a_high, b_high) + (dot(a_high, b_low) + dot(a_low, b_high))


def ordered_sum(ref, count):
    terms = [ref[k] for k in range(count)]
    while len(terms) > 1:
        terms = [terms[k] + terms[k + 1] for k in range(0, len(terms), 2)]
    return terms[0]


def fused_kernel(
    sample_total,
    owner_ref,
    act_ref,
    gout_ref,
    grad_ref,
    old_ref,
    weights_ref,
    momentum_ref,
    weights_out,
    momentum_out,
    factors_out,
    act_v,
    gout_v,
    old_v,
    weights_v,
    momentum_v,
    packed_v,
    core_in,
    y_in,
    xz_out,
    xz_in,
    full_v,
    left_pair,
    diag_out,
    diag_in,
    diag_xz,
    grad_own,
    grad_x,
    grad_z,
    sum_out,
    sum_xz,
    sum_tensor,
    base_all,
    precond_all,
    mixed_v,
    local_sem,
    sends,
    recvs,
):
    s = lax.axis_index("shards")
    t = lax.axis_index("tensor")
    r = lax.axis_index("replica")
    y = t // 2
    c = t % 2
    n = 128
    half = 512
    quarter = 256
    place = s * 4 + r
    x_peer = (1 - s, t, r)
    y_peer = (s, 2 * (1 - y) + c, r)
    c_peer = (s, 2 * y + 1 - c, r)
    yc_peer = (s, 2 * (1 - y) + 1 - c, r)
    z_ranks = [(r + d) % 4 for d in (1, 2, 3)]
    z_peers = [(s, t, q) for q in z_ranks]
    xz_peers = z_peers + [(1 - s, t, q) for q in z_ranks] + [x_peer]
    xz_places = [s * 4 + q for q in z_ranks] + [(1 - s) * 4 + q for q in z_ranks]
    xz_places = xz_places + [(1 - s) * 4 + r]
    used_sems = [0]

    def part(ref, start, size):
        return ref.at[pl.ds(pl.multiple_of(start, 8), size)]

    def send(src, dst, device):
        copy = remote(src, dst, sends, recvs, used_sems[0], device)
        used_sems[0] += 1
        copy.start()
        return copy

    def load(src, dst, index):
        copy = pltpu.make_async_copy(src, dst, local_sem.at[index])
        copy.start()
        return copy

    barrier = pltpu.get_barrier_semaphore()
    peers = xz_peers + [y_peer, c_peer, yc_peer]
    for peer in peers:
        pl.semaphore_signal(barrier, inc=1, device_id=peer, device_id_type=MESH)

    groups = ((1 - y, 1 - c), (y, 1 - c), (1 - y, c), (y, c))
    starts = [pl.multiple_of(side * half + core * quarter, quarter) for side, core in groups]
    loads = []
    for k, start in enumerate(starts):
        columns = pl.ds(start, quarter)
        loads.append(load(act_ref.at[:, columns], act_v.at[:, columns], 2 * k))
        loads.append(load(gout_ref.at[:, columns], gout_v.at[:, columns], 2 * k + 1))
    weights_load = load(weights_ref, weights_v, 8)
    momentum_load = load(momentum_ref, momentum_v, 9)
    own_load = load(
        grad_ref.at[0, pl.ds(pl.multiple_of(s * half, half), half)], grad_own, 10
    )
    old_load = load(old_ref, old_v, 11)

    rows = lax.broadcasted_iota(jnp.int32, (n, n), 0)
    cols = lax.broadcasted_iota(jnp.int32, (n, n), 1)
    lower = rows > cols
    on_diagonal = rows == cols
    pair_rows = lax.broadcasted_iota(jnp.int32, (8, n), 0)
    identity = on_diagonal.astype(jnp.float32)

    diag = jnp.zeros((8, n), jnp.float32)
    core_copies = []
    for j, (side, core) in enumerate(groups):
        loads[2 * j].wait()
        loads[2 * j + 1].wait()
        start = starts[j]
        a = act_v[:, pl.ds(start, quarter)]
        g = gout_v[:, pl.ds(start, quarter)]
        across = (((0,), (0,)), ((), ()))
        left = lax.dot_general(a, a, across, preferred_element_type=jnp.float32)
        right = lax.dot_general(g, g, across, preferred_element_type=jnp.float32)
        for k in range(2):
            span = slice(k * n, (k + 1) * n)
            second = right[span, span]
            packed_v[pl.ds(start + k * n, n), :] = jnp.where(lower, second, left[span, span])
            row = jnp.sum(jnp.where(on_diagonal, second, 0.0), axis=0, keepdims=True)
            diag = jnp.where(pair_rows == side * 4 + core * 2 + k, row, diag)
        if j == 0:
            pl.semaphore_wait(barrier, len(peers))
        if j < 2:
            core_copies.append(send(part(packed_v, start, quarter), core_in.at[j], c_peer))
        if j == 0:
            grad_x_copies = [
                send(
                    grad_ref.at[0, pl.ds(pl.multiple_of((1 - s) * half + k * n, n), n)],
                    grad_x.at[k],
                    x_peer,
                )
                for k in range(4)
            ]
        elif j == 1:
            weights_load.wait()
            momentum_load.wait()
            own_rows = pl.ds(pl.multiple_of(place * n, n), n)
            base_all[own_rows, :] = weights_v[...] - (step_rate * momentum_rate) * momentum_v[...]
            base_own = part(base_all, place * n, n)
            base_copies = [send(base_own, base_own, peer) for peer in z_peers]
        elif j == 2:
            core_copies[0].wait()
            packed_v[pl.ds(start, quarter), :] += core_in[0]
            y_copy = send(part(packed_v, start, quarter), y_in, y_peer)
    diag_out[0] = diag
    copy = send(diag_out.at[0], diag_in.at[0], c_peer)
    core_copies[1].wait()
    mine = packed_v[pl.ds(starts[3], quarter), :] + core_in[1]
    copy.wait()
    diag = diag + diag_in[0]
    diag_out[1] = diag
    diag_copy = send(diag_out.at[1], diag_in.at[1], y_peer)
    y_copy.wait()
    xz_out[...] = (mine + y_in[...]).reshape(8, 32, n)
    copies = [
        send(xz_out.at[q], xz_in.at[place], peer) for q, peer in zip(xz_places, xz_peers)
    ]
    diag_copy.wait()
    diag = diag + diag_in[1]
    diag_out[2] = diag
    diag_copies = [send(diag_out.at[2], diag_xz.at[place], peer) for peer in xz_peers]
    xz_in[place] = xz_out[place]
    diag_xz[place] = diag
    own_load.wait()
    for k in range(4):
        grad_x_copies[k].wait()
        grad_x[k] = grad_x[k] + grad_own[pl.ds(k * n, n), :]
    grad_copies = [
        send(grad_x.at[q], grad_z.at[r], peer) for q, peer in zip(z_ranks, z_peers)
    ]
    grad_z[r] = grad_x[r]
    for copy in copies:
        copy.wait()
    start = pl.multiple_of(starts[3] + place * 32, 32)
    full_v[pl.ds(start, 32), :] = ordered_sum(xz_in, 8)
    region = part(full_v, start, 32)
    copies = [send(region, region, peer) for peer in xz_peers]
    for copy in diag_copies:
        copy.wait()
    diag_out[3] = ordered_sum(diag_xz, 8)
    for copy in copies:
        copy.wait()

    holder = (s == y) & (r // 2 == c)
    pair_sem = used_sems[0]
    used_sems[0] += 3
    pair_copies = [
        pltpu.make_async_remote_copy(
            src_ref=part(full_v, place * n, n),
            dst_ref=left_pair,
            send_sem=sends.at[pair_sem + k],
            recv_sem=recvs.at[pair_sem],
            device_id=peer,
            device_id_type=MESH,
        )
        for k, peer in enumerate((yc_peer, y_peer, c_peer))
    ]

    @pl.when(holder)
    def _():
        for copy in pair_copies:
            copy.start()
        left_pair[...] = full_v[pl.ds(pl.multiple_of(place * n, n), n), :]

    region = part(full_v, starts[3], quarter)
    y_copy = send(region, region, y_peer)
    core_copies = [send(region, region, c_peer)]
    for copy in base_copies:
        copy.wait()
    region = part(base_all, s * half, half)
    base_copy = send(region, region, x_peer)

    def blend(pair, packed=None):
        if packed is None:
            packed = full_v[pl.ds(pl.multiple_of(pair * n, n), n), :]
        first, second = unpack_pair(
            packed,
            diag_out[3, pl.ds(pair, 1), :],
            lower,
            on_diagonal,
        )
        return (
            decay_rate * old_v[pair] + (1.0 - decay_rate) * (first / sample_total),
            decay_rate * old_v[8 + pair] + (1.0 - decay_rate) * (second / sample_total),
        )

    def invert(blocks):
        scales, rests = [], []
        for block in blocks:
            trace = jnp.sum(jnp.where(on_diagonal, block, 0.0), keepdims=True)
            damped = block + (damping * trace / n + damp_shift) * identity
            bound = jnp.max(
                jnp.sum(jnp.abs(damped), axis=1, keepdims=True), axis=0, keepdims=True
            )
            scales.append(1.0 / bound)
            rests.append(identity - damped / bound)
        inverses = [identity + rest for rest in rests]
        for _ in range(NS_STEPS - 1):
            rests = [dot_exact(rest, rest) for rest in rests]
            inverses = [inv + dot_exact(inv, rest) for inv, rest in zip(inverses, rests)]
        return [inv * scale for inv, scale in zip(inverses, scales)]

    old_load.wait()
    right_inverses = invert([blend(2 * t)[1], blend(2 * t + 1)[1]])

    @pl.when(jnp.logical_not(holder))
    def _():
        pair_copies[0].wait_recv()

    left_inverse = invert([blend(place, left_pair[...])[0]])[0]
    y_copy.wait()
    region = part(full_v, starts[2], quarter)
    core_copies.append(send(region, region, c_peer))

    for copy in grad_copies:
        copy.wait()
    gradient = (grad_z[0] + grad_z[1]) + (grad_z[2] + grad_z[3])
    left = dot_exact(left_inverse, gradient)
    precond = jnp.concatenate(
        [dot_exact(left[:, k * n : (k + 1) * n], right_inverses[k]) for k in range(2)], axis=1
    )
    products = precond * gradient
    products = products[:, :n] + products[:, n:]
    tile = jnp.sum(products.reshape(16, 8, n), axis=0)

    sum_out[0] = tile
    sum_copies = [send(sum_out.at[0], sum_xz.at[place], peer) for peer in xz_peers]
    precond_all[pl.ds(pl.multiple_of(place * n, n), n), :] = precond
    own = part(precond_all, place * n, n)
    x_copies = [send(own, own, x_peer)]

    first_sem = used_sems[0]
    used_sems[0] += 14

    def passing(hop, way, peer, hand_on):
        origin = r - hop if way == 0 else r + hop
        region = part(precond_all, (s * 4 + origin) * n, n)
        index = first_sem + 6 * hand_on + 2 * hop + way
        return remote(region, region, sends, recvs, index, peer)

    ways = ((s, t, r + 1), (s, t, r - 1))

    def sends_on(hop, way):
        return (r >= hop) & (r < 3) if way == 0 else (r <= 3 - hop) & (r > 0)

    def gets(hop, way):
        return r >= hop + 1 if way == 0 else r <= 2 - hop

    def start_hop(hop):
        for way in range(2):

            @pl.when(sends_on(hop, way))
            def _():
                passing(hop, way, ways[way], 0).start()

    def arrived(hop):
        for way in range(2):

            @pl.when(gets(hop, way))
            def _():
                back = ways[1 - way]
                origin = r - hop - 1 if way == 0 else r + hop + 1
                region = part(precond_all, (s * 4 + origin) * n, n)
                index = first_sem + 2 * hop + way
                remote(region, region, sends, recvs, index, back).wait_recv()

    def hand_on(hop):
        for way in range(2):

            @pl.when(gets(hop, way))
            def _():
                passing(hop + 1, way, x_peer, 1).start()

    start_hop(0)
    sum_xz[place] = tile
    for copy in sum_copies:
        copy.wait()
    tile = ordered_sum(sum_xz, 8)
    sum_out[1] = tile
    sum_copies = [
        send(sum_out.at[1], sum_tensor.at[t], peer) for peer in (c_peer, y_peer, yc_peer)
    ]
    sum_tensor[t] = tile
    arrived(0)
    start_hop(1)
    hand_on(0)
    for copy in sum_copies:
        copy.wait()
    alignment = jnp.sum(ordered_sum(sum_tensor, 4), keepdims=True)
    clip_scale = jnp.minimum(1.0, clip_norm / jnp.sqrt(alignment))
    momentum_out[...] = momentum_rate * momentum_v[...] + clip_scale * precond
    arrived(1)
    start_hop(2)
    hand_on(1)

    for copy in core_copies:
        copy.wait()

    @pl.when(holder)
    def _():
        for copy in pair_copies:
            copy.wait_send()

    for pair in range(8):
        mixed_v[pair], mixed_v[8 + pair] = blend(pair)
    mixed_v[16] = jnp.zeros((n, n), jnp.float32)
    block_total = owner_ref.shape[0]
    chosen = [jnp.int32(block_total)] * factors_out.shape[0]
    used = jnp.int32(0)
    for b in range(block_total):
        here = owner_ref[b] == s
        for k in range(min(b + 1, len(chosen))):
            chosen[k] = jnp.where(here & (used == k), jnp.int32(b), chosen[k])
        used = used + jnp.where(here, jnp.int32(1), jnp.int32(0))
    for k in range(len(chosen)):
        factors_out[k] = mixed_v[chosen[k]]

    arrived(2)
    hand_on(2)
    base_copy.wait()
    for copy in x_copies:
        copy.wait()
    for hop in range(3):
        for way in range(2):

            @pl.when(sends_on(hop, way))
            def _():
                passing(hop, way, ways[way], 0).wait_send()

            @pl.when(gets(hop, way))
            def _():
                passing(hop + 1, way, x_peer, 1).wait()

    weights_out[...] = base_all[...] - (step_rate * clip_scale) * precond_all[...]


def copy_out_kernel(weights, momentum, factors, weights_out, momentum_out, factors_out, sems):
    copies = []
    for src, dst, parts in (
        (weights, weights_out, 4),
        (factors, factors_out, 3),
        (momentum, momentum_out, 1),
    ):
        size = src.shape[0] // parts
        for k in range(parts):
            span = pl.ds(k * size, size)
            copy = pltpu.make_async_copy(src.at[span], dst.at[span], sems.at[len(copies)])
            copy.start()
            copies.append(copy)
    for copy in copies:
        copy.wait()


def fused_step(activations, grads_out, grad_parts, old_factors, block_owner, weights, momentum):
    n = old_factors.shape[1]
    shards = lax.axis_size("shards")
    capacity = (old_factors.shape[0] + shards - 1) // shards + 1
    devices = shards * lax.axis_size("tensor") * lax.axis_size("replica")
    f32 = jnp.float32
    anywhere = pl.BlockSpec(memory_space=pl.ANY)
    vmem = pl.BlockSpec(memory_space=pltpu.VMEM)
    results = pl.pallas_call(
        functools.partial(fused_kernel, float(activations.shape[0] * devices)),
        out_shape=(
            jax.ShapeDtypeStruct(grad_parts.shape[1:], f32),
            jax.ShapeDtypeStruct(momentum.shape, f32),
            jax.ShapeDtypeStruct((capacity, n, n), f32),
        ),
        in_specs=[
            pl.BlockSpec(memory_space=pltpu.SMEM),
            anywhere,
            anywhere,
            anywhere,
            anywhere,
            anywhere,
            anywhere,
        ],
        out_specs=(vmem, vmem, vmem),
        scratch_shapes=[
            pltpu.VMEM(activations.shape, activations.dtype),
            pltpu.VMEM(grads_out.shape, grads_out.dtype),
            pltpu.VMEM(old_factors.shape, f32),
            pltpu.VMEM(weights.shape, f32),
            pltpu.VMEM(momentum.shape, f32),
            pltpu.VMEM((1024, n), f32),
            pltpu.VMEM((2, 256, n), f32),
            pltpu.VMEM((256, n), f32),
            pltpu.VMEM((8, 32, n), f32),
            pltpu.VMEM((8, 32, n), f32),
            pltpu.VMEM((1024, n), f32),
            pltpu.VMEM((n, n), f32),
            pltpu.VMEM((4, 8, n), f32),
            pltpu.VMEM((2, 8, n), f32),
            pltpu.VMEM((8, 8, n), f32),
            pltpu.VMEM((512, 256), f32),
            pltpu.VMEM((4, n, 256), f32),
            pltpu.VMEM((4, n, 256), f32),
            pltpu.VMEM((2, 8, n), f32),
            pltpu.VMEM((8, 8, n), f32),
            pltpu.VMEM((4, 8, n), f32),
            pltpu.VMEM((1024, 256), f32),
            pltpu.VMEM((1024, 256), f32),
            pltpu.VMEM((17, n, n), f32),
            pltpu.SemaphoreType.DMA((12,)),
            pltpu.SemaphoreType.DMA((72,)),
            pltpu.SemaphoreType.DMA((72,)),
        ],
        compiler_params=pltpu.CompilerParams(
            collective_id=0, has_side_effects=True, vmem_limit_bytes=60 * 1024 * 1024
        ),
        cost_estimate=pl.CostEstimate(
            flops=1_200_000_000, bytes_accessed=10_000_000, transcendentals=0
        ),
    )(block_owner, activations, grads_out, grad_parts, old_factors, weights, momentum)
    return pl.pallas_call(
        copy_out_kernel,
        out_shape=tuple(jax.ShapeDtypeStruct(a.shape, a.dtype) for a in results),
        in_specs=[anywhere] * 3,
        out_specs=(anywhere,) * 3,
        scratch_shapes=[pltpu.SemaphoreType.DMA((8,))],
        cost_estimate=pl.CostEstimate(flops=0, bytes_accessed=3_500_000, transcendentals=0),
    )(*results)


def step(activations, grads_out, grad_parts, old_factors, block_owner, weights, momentum):
    sizes = tuple(lax.axis_size(name) for name in ("shards", "tensor", "replica"))
    fits = (
        sizes == (2, 4, 4)
        and weights.shape == (128, 256)
        and old_factors.shape == (16, 128, 128)
        and activations.shape == grads_out.shape == (1024, 1024)
    )
    chosen = fused_step if fits else body
    return chosen(
        activations, grads_out, grad_parts, old_factors, block_owner, weights, momentum
    )


def solution(mesh):
    placed = (
        P(("shards", "tensor", "replica"), None),
        P(("shards", "tensor", "replica"), None),
        P(("shards", "replica"), None, "tensor"),
        P(),
        P(),
        P(("shards", "replica"), "tensor"),
        P(("shards", "replica"), "tensor"),
    )
    return jax.shard_map(
        step,
        mesh=mesh,
        in_specs=placed,
        out_specs=(P(None, "tensor"), P(("shards", "replica"), "tensor"), P("shards", None, None)),
        check_vma=False,
    )
```

```python
import functools

import jax
import jax.numpy as jnp
from jax import lax
from jax.experimental import pallas as pl
from jax.experimental.pallas import tpu as pltpu
from jax.sharding import PartitionSpec as P

MESH = pl.DeviceIdType.MESH

NS_STEPS = 4


exact_mode = lax.Precision.HIGHEST
decay_rate = 0.75
damping = 0.1
damp_shift = 0.001
clip_norm = 256.0
momentum_rate = 0.9
step_rate = 0.05


def sample_stats(samples, block_size):
    sample_rows, width = samples.shape
    blocks = samples.reshape(sample_rows, width // block_size, block_size)
    return jnp.einsum("tnb,tnc->nbc", blocks, blocks, preferred_element_type=jnp.float32)


def build_slots(block_owner, capacity, slot_count):
    block_count = block_owner.shape[0]
    positions = jnp.arange(block_count, dtype=jnp.int32)
    earlier = (block_owner[:, None] == block_owner[None, :]) & (
        positions[None, :] < positions[:, None]
    )
    owner_slot_list = block_owner * capacity + jnp.sum(earlier.astype(jnp.int32), axis=1)
    return (owner_slot_list[None, :] == jnp.arange(slot_count, dtype=jnp.int32)[:, None]).astype(
        jnp.float32
    )


def newton_inverse(mixed_factor_blocks):
    block_size = mixed_factor_blocks.shape[-1]
    identity = jnp.eye(block_size, dtype=jnp.float32)
    traces = jnp.trace(mixed_factor_blocks, axis1=1, axis2=2)
    damped = (
        mixed_factor_blocks + (damping * traces / block_size + damp_shift)[:, None, None] * identity
    )
    bounds = jnp.max(jnp.sum(jnp.abs(damped), axis=2), axis=1)
    approx = identity[None, :, :] / bounds[:, None, None]
    for iteration in range(NS_STEPS):
        left_part = jnp.einsum("nab,nbc->nac", approx, damped, precision=exact_mode)
        approx = 2.0 * approx - jnp.einsum("nab,nbc->nac", left_part, approx, precision=exact_mode)
    return approx


def apply_right(left_part, right_inv, block_size):
    row_count, col_count = left_part.shape
    right_count = col_count // block_size
    return jnp.einsum(
        "rnb,nbc->rnc",
        left_part.reshape(row_count, right_count, block_size),
        right_inv,
        precision=exact_mode,
    ).reshape(row_count, col_count)


def body(activations, grads_out, grad_parts, old_factors, block_owner, weights, momentum):
    shard_count = lax.axis_size("shards")
    block_count = old_factors.shape[0]
    block_size = old_factors.shape[1]
    capacity = (block_count + shard_count - 1) // shard_count + 1
    slot_count = capacity * shard_count
    slot_table = build_slots(block_owner, capacity, slot_count)
    local_stats = jnp.concatenate(
        [sample_stats(activations, block_size), sample_stats(grads_out, block_size)], axis=0
    )
    packed = jnp.dot(
        slot_table, local_stats.reshape(block_count, block_size * block_size), precision=exact_mode
    )
    first_slot = lax.axis_index("shards") * capacity
    summed = lax.psum(packed, ("shards", "tensor", "replica"))
    owned = lax.dynamic_slice_in_dim(summed, first_slot, capacity, 0)
    sample_count = (
        activations.shape[0] * shard_count * lax.axis_size("tensor") * lax.axis_size("replica")
    )
    owned_table = lax.dynamic_slice_in_dim(slot_table, first_slot, capacity, 0)
    old_owned = jnp.dot(
        owned_table, old_factors.reshape(block_count, block_size * block_size), precision=exact_mode
    )
    mixed_factor_blocks = (
        decay_rate * old_owned + (1.0 - decay_rate) * (owned / sample_count)
    ).reshape(capacity, block_size, block_size)
    inverse_owned = newton_inverse(mixed_factor_blocks)
    start_blocks = jnp.zeros((block_count, block_size * block_size), jnp.float32)
    shard_piece = lax.all_gather(inverse_owned, "shards", axis=0, tiled=True)
    piece_rows = shard_piece.shape[0]
    rows_table = lax.slice_in_dim(slot_table, 0, piece_rows, axis=0)
    flat_piece = shard_piece.reshape(piece_rows, block_size * block_size)
    inverse_flat = start_blocks + jnp.einsum(
        "sb,sk->bk", rows_table, flat_piece, precision=exact_mode
    )
    inverse_blocks = inverse_flat.reshape(block_count, block_size, block_size)
    partial_grad = grad_parts[0]
    row_count, col_count = partial_grad.shape
    left_count = row_count // block_size
    right_count = col_count // block_size
    right_first = left_count + lax.axis_index("tensor") * right_count
    right_inv = lax.dynamic_slice_in_dim(inverse_blocks, right_first, right_count, 0)
    left_part = jnp.einsum(
        "nab,nbc->nac",
        inverse_blocks[:left_count],
        partial_grad.reshape(left_count, block_size, col_count),
        precision=exact_mode,
    ).reshape(row_count, col_count)
    precond = apply_right(left_part, right_inv, block_size)
    total_precond, total_grad = (
        lax.psum_scatter(precond, ("shards", "replica"), scatter_dimension=0, tiled=True),
        lax.psum_scatter(partial_grad, ("shards", "replica"), scatter_dimension=0, tiled=True),
    )
    alignment_sum = lax.psum(jnp.sum(total_precond * total_grad), ("shards", "tensor", "replica"))
    clip_scale = jnp.minimum(1.0, clip_norm / jnp.sqrt(alignment_sum))
    momentum_next = momentum_rate * momentum + clip_scale * total_precond
    weights_next = weights - step_rate * momentum_next
    gathered = lax.all_gather(weights_next, ("shards", "replica"), axis=0, tiled=True)
    return (gathered, momentum_next, mixed_factor_blocks)


def remote(src, dst, sends, recvs, index, device):
    return pltpu.make_async_remote_copy(
        src_ref=src,
        dst_ref=dst,
        send_sem=sends.at[index],
        recv_sem=recvs.at[index],
        device_id=device,
        device_id_type=MESH,
    )


def unpack_pair(packed, diagonal, lower, on_diagonal):
    flipped = packed.T
    first = jnp.where(lower, flipped, packed)
    second = jnp.where(lower, packed, jnp.where(on_diagonal, diagonal, flipped))
    return first, second


def split_halves(a):
    high = a.astype(jnp.bfloat16)
    return high, (a - high.astype(jnp.float32)).astype(jnp.bfloat16)


def dot_exact(a, b):
    a_high, a_low = split_halves(a)
    b_high, b_low = split_halves(b)
    dot = functools.partial(jnp.dot, preferred_element_type=jnp.float32)
    return dot(a_high, b_high) + (dot(a_high, b_low) + dot(a_low, b_high))


def ordered_sum(ref, count):
    terms = [ref[k] for k in range(count)]
    while len(terms) > 1:
        terms = [terms[k] + terms[k + 1] for k in range(0, len(terms), 2)]
    return terms[0]


def fused_kernel(
    sample_total,
    owner_ref,
    act_ref,
    gout_ref,
    grad_ref,
    old_ref,
    weights_ref,
    momentum_ref,
    weights_out,
    momentum_out,
    factors_out,
    act_v,
    gout_v,
    old_v,
    weights_v,
    momentum_v,
    packed_v,
    core_in,
    y_in,
    xz_out,
    xz_in,
    full_v,
    left_pair,
    diag_out,
    diag_in,
    diag_xz,
    grad_own,
    grad_x,
    grad_z,
    sum_out,
    sum_xz,
    sum_tensor,
    base_all,
    precond_all,
    mixed_v,
    local_sem,
    sends,
    recvs,
):
    s = lax.axis_index("shards")
    t = lax.axis_index("tensor")
    r = lax.axis_index("replica")
    y = t // 2
    c = t % 2
    n = 128
    half = 512
    quarter = 256
    place = s * 4 + r
    x_peer = (1 - s, t, r)
    y_peer = (s, 2 * (1 - y) + c, r)
    c_peer = (s, 2 * y + 1 - c, r)
    yc_peer = (s, 2 * (1 - y) + 1 - c, r)
    z_ranks = [(r + d) % 4 for d in (1, 2, 3)]
    z_peers = [(s, t, q) for q in z_ranks]
    xz_peers = z_peers + [(1 - s, t, q) for q in z_ranks] + [x_peer]
    xz_places = [s * 4 + q for q in z_ranks] + [(1 - s) * 4 + q for q in z_ranks]
    xz_places = xz_places + [(1 - s) * 4 + r]
    used_sems = [0]

    def part(ref, start, size):
        return ref.at[pl.ds(pl.multiple_of(start, 8), size)]

    def send(src, dst, device):
        copy = remote(src, dst, sends, recvs, used_sems[0], device)
        used_sems[0] += 1
        copy.start()
        return copy

    def load(src, dst, index):
        copy = pltpu.make_async_copy(src, dst, local_sem.at[index])
        copy.start()
        return copy

    barrier = pltpu.get_barrier_semaphore()
    peers = xz_peers + [y_peer, c_peer, yc_peer]
    for peer in peers:
        pl.semaphore_signal(barrier, inc=1, device_id=peer, device_id_type=MESH)

    groups = ((1 - y, 1 - c), (y, 1 - c), (1 - y, c), (y, c))
    starts = [pl.multiple_of(side * half + core * quarter, quarter) for side, core in groups]
    loads = []
    for k, start in enumerate(starts):
        columns = pl.ds(start, quarter)
        loads.append(load(act_ref.at[:, columns], act_v.at[:, columns], 2 * k))
        loads.append(load(gout_ref.at[:, columns], gout_v.at[:, columns], 2 * k + 1))
    weights_load = load(weights_ref, weights_v, 8)
    momentum_load = load(momentum_ref, momentum_v, 9)
    grad_load = load(grad_ref.at[0], grad_own, 10)
    old_load = load(old_ref, old_v, 11)

    rows = lax.broadcasted_iota(jnp.int32, (n, n), 0)
    cols = lax.broadcasted_iota(jnp.int32, (n, n), 1)
    lower = rows > cols
    on_diagonal = rows == cols
    pair_rows = lax.broadcasted_iota(jnp.int32, (8, n), 0)
    identity = on_diagonal.astype(jnp.float32)

    diag = jnp.zeros((8, n), jnp.float32)
    core_copies = []
    for j, (side, core) in enumerate(groups):
        loads[2 * j].wait()
        loads[2 * j + 1].wait()
        start = starts[j]
        a = act_v[:, pl.ds(start, quarter)]
        g = gout_v[:, pl.ds(start, quarter)]
        across = (((0,), (0,)), ((), ()))
        left = lax.dot_general(a, a, across, preferred_element_type=jnp.float32)
        right = lax.dot_general(g, g, across, preferred_element_type=jnp.float32)
        for k in range(2):
            span = slice(k * n, (k + 1) * n)
            second = right[span, span]
            packed_v[pl.ds(start + k * n, n), :] = jnp.where(lower, second, left[span, span])
            row = jnp.sum(jnp.where(on_diagonal, second, 0.0), axis=0, keepdims=True)
            diag = jnp.where(pair_rows == side * 4 + core * 2 + k, row, diag)
        if j == 0:
            pl.semaphore_wait(barrier, len(peers))
        if j < 2:
            core_copies.append(send(part(packed_v, start, quarter), core_in.at[j], c_peer))
        if j == 0:
            grad_load.wait()
            grad_x_copies = [
                send(part(grad_own, (1 - s) * half + k * n, n), grad_x.at[k], x_peer)
                for k in range(4)
            ]
        elif j == 1:
            weights_load.wait()
            momentum_load.wait()
            own_rows = pl.ds(pl.multiple_of(place * n, n), n)
            base_all[own_rows, :] = weights_v[...] - (step_rate * momentum_rate) * momentum_v[...]
            base_own = part(base_all, place * n, n)
            base_copies = [send(base_own, base_own, peer) for peer in z_peers]
        elif j == 2:
            core_copies[0].wait()
            packed_v[pl.ds(start, quarter), :] += core_in[0]
            y_copy = send(part(packed_v, start, quarter), y_in, y_peer)
    diag_out[0] = diag
    copy = send(diag_out.at[0], diag_in.at[0], c_peer)
    core_copies[1].wait()
    mine = packed_v[pl.ds(starts[3], quarter), :] + core_in[1]
    copy.wait()
    diag = diag + diag_in[0]
    diag_out[1] = diag
    diag_copy = send(diag_out.at[1], diag_in.at[1], y_peer)
    y_copy.wait()
    xz_out[...] = (mine + y_in[...]).reshape(8, 32, n)
    copies = [
        send(xz_out.at[q], xz_in.at[place], peer) for q, peer in zip(xz_places, xz_peers)
    ]
    diag_copy.wait()
    diag = diag + diag_in[1]
    diag_out[2] = diag
    diag_copies = [send(diag_out.at[2], diag_xz.at[place], peer) for peer in xz_peers]
    xz_in[place] = xz_out[place]
    diag_xz[place] = diag
    for copy in copies:
        copy.wait()
    start = pl.multiple_of(starts[3] + place * 32, 32)
    full_v[pl.ds(start, 32), :] = ordered_sum(xz_in, 8)
    region = part(full_v, start, 32)
    copies = [send(region, region, peer) for peer in xz_peers]
    for copy in diag_copies:
        copy.wait()
    diag_out[3] = ordered_sum(diag_xz, 8)
    for copy in copies:
        copy.wait()

    holder = (s == y) & (r // 2 == c)
    pair_sem = used_sems[0]
    used_sems[0] += 3
    pair_copies = [
        pltpu.make_async_remote_copy(
            src_ref=part(full_v, place * n, n),
            dst_ref=left_pair,
            send_sem=sends.at[pair_sem + k],
            recv_sem=recvs.at[pair_sem],
            device_id=peer,
            device_id_type=MESH,
        )
        for k, peer in enumerate((yc_peer, y_peer, c_peer))
    ]

    @pl.when(holder)
    def _():
        for copy in pair_copies:
            copy.start()
        left_pair[...] = full_v[pl.ds(pl.multiple_of(place * n, n), n), :]

    region = part(full_v, starts[3], quarter)
    y_copy = send(region, region, y_peer)
    core_copies = [send(region, region, c_peer)]
    for k in range(4):
        grad_x_copies[k].wait()
        own_rows = pl.ds(pl.multiple_of(s * half + k * n, n), n)
        grad_x[k] = grad_x[k] + grad_own[own_rows, :]
    grad_copies = [
        send(grad_x.at[q], grad_z.at[r], peer) for q, peer in zip(z_ranks, z_peers)
    ]
    grad_z[r] = grad_x[r]
    for copy in base_copies:
        copy.wait()
    region = part(base_all, s * half, half)
    base_copy = send(region, region, x_peer)

    def blend(pair, packed=None):
        if packed is None:
            packed = full_v[pl.ds(pl.multiple_of(pair * n, n), n), :]
        first, second = unpack_pair(
            packed,
            diag_out[3, pl.ds(pair, 1), :],
            lower,
            on_diagonal,
        )
        return (
            decay_rate * old_v[pair] + (1.0 - decay_rate) * (first / sample_total),
            decay_rate * old_v[8 + pair] + (1.0 - decay_rate) * (second / sample_total),
        )

    def invert(blocks):
        scales, rests = [], []
        for block in blocks:
            trace = jnp.sum(jnp.where(on_diagonal, block, 0.0), keepdims=True)
            damped = block + (damping * trace / n + damp_shift) * identity
            bound = jnp.max(
                jnp.sum(jnp.abs(damped), axis=1, keepdims=True), axis=0, keepdims=True
            )
            scales.append(1.0 / bound)
            rests.append(identity - damped / bound)
        inverses = [identity + rest for rest in rests]
        for _ in range(NS_STEPS - 1):
            rests = [dot_exact(rest, rest) for rest in rests]
            inverses = [inv + dot_exact(inv, rest) for inv, rest in zip(inverses, rests)]
        return [inv * scale for inv, scale in zip(inverses, scales)]

    old_load.wait()
    right_inverses = invert([blend(2 * t)[1], blend(2 * t + 1)[1]])

    @pl.when(jnp.logical_not(holder))
    def _():
        pair_copies[0].wait_recv()

    left_inverse = invert([blend(place, left_pair[...])[0]])[0]
    y_copy.wait()
    region = part(full_v, starts[2], quarter)
    core_copies.append(send(region, region, c_peer))

    for copy in grad_copies:
        copy.wait()
    gradient = (grad_z[0] + grad_z[1]) + (grad_z[2] + grad_z[3])
    left = dot_exact(left_inverse, gradient)
    precond = jnp.concatenate(
        [dot_exact(left[:, k * n : (k + 1) * n], right_inverses[k]) for k in range(2)], axis=1
    )
    products = precond * gradient
    products = products[:, :n] + products[:, n:]
    tile = jnp.sum(products.reshape(16, 8, n), axis=0)

    sum_out[0] = tile
    sum_copies = [send(sum_out.at[0], sum_xz.at[place], peer) for peer in xz_peers]
    precond_all[pl.ds(pl.multiple_of(place * n, n), n), :] = precond
    own = part(precond_all, place * n, n)
    x_copies = [send(own, own, x_peer)]

    first_sem = used_sems[0]
    used_sems[0] += 14

    def passing(hop, way, peer, hand_on):
        origin = r - hop if way == 0 else r + hop
        region = part(precond_all, (s * 4 + origin) * n, n)
        index = first_sem + 6 * hand_on + 2 * hop + way
        return remote(region, region, sends, recvs, index, peer)

    ways = ((s, t, r + 1), (s, t, r - 1))

    def sends_on(hop, way):
        return (r >= hop) & (r < 3) if way == 0 else (r <= 3 - hop) & (r > 0)

    def gets(hop, way):
        return r >= hop + 1 if way == 0 else r <= 2 - hop

    def start_hop(hop):
        for way in range(2):

            @pl.when(sends_on(hop, way))
            def _():
                passing(hop, way, ways[way], 0).start()

    def arrived(hop):
        for way in range(2):

            @pl.when(gets(hop, way))
            def _():
                back = ways[1 - way]
                origin = r - hop - 1 if way == 0 else r + hop + 1
                region = part(precond_all, (s * 4 + origin) * n, n)
                index = first_sem + 2 * hop + way
                remote(region, region, sends, recvs, index, back).wait_recv()

    def hand_on(hop):
        for way in range(2):

            @pl.when(gets(hop, way))
            def _():
                passing(hop + 1, way, x_peer, 1).start()

    start_hop(0)
    sum_xz[place] = tile
    for copy in sum_copies:
        copy.wait()
    tile = ordered_sum(sum_xz, 8)
    sum_out[1] = tile
    sum_copies = [
        send(sum_out.at[1], sum_tensor.at[t], peer) for peer in (c_peer, y_peer, yc_peer)
    ]
    sum_tensor[t] = tile
    arrived(0)
    start_hop(1)
    hand_on(0)
    for copy in sum_copies:
        copy.wait()
    alignment = jnp.sum(ordered_sum(sum_tensor, 4), keepdims=True)
    clip_scale = jnp.minimum(1.0, clip_norm / jnp.sqrt(alignment))
    momentum_out[...] = momentum_rate * momentum_v[...] + clip_scale * precond
    arrived(1)
    start_hop(2)
    hand_on(1)

    for copy in core_copies:
        copy.wait()

    @pl.when(holder)
    def _():
        for copy in pair_copies:
            copy.wait_send()

    for pair in range(8):
        mixed_v[pair], mixed_v[8 + pair] = blend(pair)
    mixed_v[16] = jnp.zeros((n, n), jnp.float32)
    block_total = owner_ref.shape[0]
    chosen = [jnp.int32(block_total)] * factors_out.shape[0]
    used = jnp.int32(0)
    for b in range(block_total):
        here = owner_ref[b] == s
        for k in range(min(b + 1, len(chosen))):
            chosen[k] = jnp.where(here & (used == k), jnp.int32(b), chosen[k])
        used = used + jnp.where(here, jnp.int32(1), jnp.int32(0))
    for k in range(len(chosen)):
        factors_out[k] = mixed_v[chosen[k]]

    arrived(2)
    hand_on(2)
    base_copy.wait()
    for copy in x_copies:
        copy.wait()
    for hop in range(3):
        for way in range(2):

            @pl.when(sends_on(hop, way))
            def _():
                passing(hop, way, ways[way], 0).wait_send()

            @pl.when(gets(hop, way))
            def _():
                passing(hop + 1, way, x_peer, 1).wait()

    weights_out[...] = base_all[...] - (step_rate * clip_scale) * precond_all[...]


def copy_out_kernel(
    weights, momentum, factors, weights_out, momentum_out, factors_out, *held_and_sems
):
    held, (loads, stores) = held_and_sems[:3], held_and_sems[3:]
    pieces = []
    for src, mid, dst, parts in (
        (weights, held[0], weights_out, 4),
        (factors, held[2], factors_out, 3),
        (momentum, held[1], momentum_out, 1),
    ):
        size = src.shape[0] // parts
        for k in range(parts):
            span = pl.ds(k * size, size)
            index = len(pieces)
            first = pltpu.make_async_copy(src.at[span], mid.at[span], loads.at[index])
            first.start()
            second = pltpu.make_async_copy(mid.at[span], dst.at[span], stores.at[index])
            pieces.append((first, second))
    for first, second in pieces:
        first.wait()
        second.start()
    for _, second in pieces:
        second.wait()


def fused_step(activations, grads_out, grad_parts, old_factors, block_owner, weights, momentum):
    n = old_factors.shape[1]
    shards = lax.axis_size("shards")
    capacity = (old_factors.shape[0] + shards - 1) // shards + 1
    devices = shards * lax.axis_size("tensor") * lax.axis_size("replica")
    f32 = jnp.float32
    anywhere = pl.BlockSpec(memory_space=pl.ANY)
    vmem = pl.BlockSpec(memory_space=pltpu.VMEM)
    results = pl.pallas_call(
        functools.partial(fused_kernel, float(activations.shape[0] * devices)),
        out_shape=(
            jax.ShapeDtypeStruct(grad_parts.shape[1:], f32),
            jax.ShapeDtypeStruct(momentum.shape, f32),
            jax.ShapeDtypeStruct((capacity, n, n), f32),
        ),
        in_specs=[
            pl.BlockSpec(memory_space=pltpu.SMEM),
            anywhere,
            anywhere,
            anywhere,
            anywhere,
            anywhere,
            anywhere,
        ],
        out_specs=(vmem, vmem, vmem),
        scratch_shapes=[
            pltpu.VMEM(activations.shape, activations.dtype),
            pltpu.VMEM(grads_out.shape, grads_out.dtype),
            pltpu.VMEM(old_factors.shape, f32),
            pltpu.VMEM(weights.shape, f32),
            pltpu.VMEM(momentum.shape, f32),
            pltpu.VMEM((1024, n), f32),
            pltpu.VMEM((2, 256, n), f32),
            pltpu.VMEM((256, n), f32),
            pltpu.VMEM((8, 32, n), f32),
            pltpu.VMEM((8, 32, n), f32),
            pltpu.VMEM((1024, n), f32),
            pltpu.VMEM((n, n), f32),
            pltpu.VMEM((4, 8, n), f32),
            pltpu.VMEM((2, 8, n), f32),
            pltpu.VMEM((8, 8, n), f32),
            pltpu.VMEM((1024, 256), f32),
            pltpu.VMEM((4, n, 256), f32),
            pltpu.VMEM((4, n, 256), f32),
            pltpu.VMEM((2, 8, n), f32),
            pltpu.VMEM((8, 8, n), f32),
            pltpu.VMEM((4, 8, n), f32),
            pltpu.VMEM((1024, 256), f32),
            pltpu.VMEM((1024, 256), f32),
            pltpu.VMEM((17, n, n), f32),
            pltpu.SemaphoreType.DMA((12,)),
            pltpu.SemaphoreType.DMA((72,)),
            pltpu.SemaphoreType.DMA((72,)),
        ],
        compiler_params=pltpu.CompilerParams(
            collective_id=0, has_side_effects=True, vmem_limit_bytes=60 * 1024 * 1024
        ),
        cost_estimate=pl.CostEstimate(
            flops=1_200_000_000, bytes_accessed=10_000_000, transcendentals=0
        ),
    )(block_owner, activations, grads_out, grad_parts, old_factors, weights, momentum)
    return pl.pallas_call(
        copy_out_kernel,
        out_shape=tuple(jax.ShapeDtypeStruct(a.shape, a.dtype) for a in results),
        in_specs=[anywhere] * 3,
        out_specs=(anywhere,) * 3,
        scratch_shapes=[pltpu.VMEM(a.shape, a.dtype) for a in results]
        + [pltpu.SemaphoreType.DMA((8,))] * 2,
        compiler_params=pltpu.CompilerParams(vmem_limit_bytes=60 * 1024 * 1024),
        cost_estimate=pl.CostEstimate(flops=0, bytes_accessed=3_500_000, transcendentals=0),
    )(*results)


def step(activations, grads_out, grad_parts, old_factors, block_owner, weights, momentum):
    sizes = tuple(lax.axis_size(name) for name in ("shards", "tensor", "replica"))
    fits = (
        sizes == (2, 4, 4)
        and weights.shape == (128, 256)
        and old_factors.shape == (16, 128, 128)
        and activations.shape == grads_out.shape == (1024, 1024)
    )
    chosen = fused_step if fits else body
    return chosen(
        activations, grads_out, grad_parts, old_factors, block_owner, weights, momentum
    )


def solution(mesh):
    placed = (
        P(("shards", "tensor", "replica"), None),
        P(("shards", "tensor", "replica"), None),
        P(("shards", "replica"), None, "tensor"),
        P(),
        P(),
        P(("shards", "replica"), "tensor"),
        P(("shards", "replica"), "tensor"),
    )
    return jax.shard_map(
        step,
        mesh=mesh,
        in_specs=placed,
        out_specs=(P(None, "tensor"), P(("shards", "replica"), "tensor"), P("shards", None, None)),
        check_vma=False,
    )
```

```python
import functools

import jax
import jax.numpy as jnp
from jax import lax
from jax.experimental import pallas as pl
from jax.experimental.pallas import tpu as pltpu
from jax.sharding import PartitionSpec as P

MESH = pl.DeviceIdType.MESH

NS_STEPS = 4


exact_mode = lax.Precision.HIGHEST
decay_rate = 0.75
damping = 0.1
damp_shift = 0.001
clip_norm = 256.0
momentum_rate = 0.9
step_rate = 0.05


def sample_stats(samples, block_size):
    sample_rows, width = samples.shape
    blocks = samples.reshape(sample_rows, width // block_size, block_size)
    return jnp.einsum("tnb,tnc->nbc", blocks, blocks, preferred_element_type=jnp.float32)


def build_slots(block_owner, capacity, slot_count):
    block_count = block_owner.shape[0]
    positions = jnp.arange(block_count, dtype=jnp.int32)
    earlier = (block_owner[:, None] == block_owner[None, :]) & (
        positions[None, :] < positions[:, None]
    )
    owner_slot_list = block_owner * capacity + jnp.sum(earlier.astype(jnp.int32), axis=1)
    return (owner_slot_list[None, :] == jnp.arange(slot_count, dtype=jnp.int32)[:, None]).astype(
        jnp.float32
    )


def newton_inverse(mixed_factor_blocks):
    block_size = mixed_factor_blocks.shape[-1]
    identity = jnp.eye(block_size, dtype=jnp.float32)
    traces = jnp.trace(mixed_factor_blocks, axis1=1, axis2=2)
    damped = (
        mixed_factor_blocks + (damping * traces / block_size + damp_shift)[:, None, None] * identity
    )
    bounds = jnp.max(jnp.sum(jnp.abs(damped), axis=2), axis=1)
    approx = identity[None, :, :] / bounds[:, None, None]
    for iteration in range(NS_STEPS):
        left_part = jnp.einsum("nab,nbc->nac", approx, damped, precision=exact_mode)
        approx = 2.0 * approx - jnp.einsum("nab,nbc->nac", left_part, approx, precision=exact_mode)
    return approx


def apply_right(left_part, right_inv, block_size):
    row_count, col_count = left_part.shape
    right_count = col_count // block_size
    return jnp.einsum(
        "rnb,nbc->rnc",
        left_part.reshape(row_count, right_count, block_size),
        right_inv,
        precision=exact_mode,
    ).reshape(row_count, col_count)


def body(activations, grads_out, grad_parts, old_factors, block_owner, weights, momentum):
    shard_count = lax.axis_size("shards")
    block_count = old_factors.shape[0]
    block_size = old_factors.shape[1]
    capacity = (block_count + shard_count - 1) // shard_count + 1
    slot_count = capacity * shard_count
    slot_table = build_slots(block_owner, capacity, slot_count)
    local_stats = jnp.concatenate(
        [sample_stats(activations, block_size), sample_stats(grads_out, block_size)], axis=0
    )
    packed = jnp.dot(
        slot_table, local_stats.reshape(block_count, block_size * block_size), precision=exact_mode
    )
    first_slot = lax.axis_index("shards") * capacity
    summed = lax.psum(packed, ("shards", "tensor", "replica"))
    owned = lax.dynamic_slice_in_dim(summed, first_slot, capacity, 0)
    sample_count = (
        activations.shape[0] * shard_count * lax.axis_size("tensor") * lax.axis_size("replica")
    )
    owned_table = lax.dynamic_slice_in_dim(slot_table, first_slot, capacity, 0)
    old_owned = jnp.dot(
        owned_table, old_factors.reshape(block_count, block_size * block_size), precision=exact_mode
    )
    mixed_factor_blocks = (
        decay_rate * old_owned + (1.0 - decay_rate) * (owned / sample_count)
    ).reshape(capacity, block_size, block_size)
    inverse_owned = newton_inverse(mixed_factor_blocks)
    start_blocks = jnp.zeros((block_count, block_size * block_size), jnp.float32)
    shard_piece = lax.all_gather(inverse_owned, "shards", axis=0, tiled=True)
    piece_rows = shard_piece.shape[0]
    rows_table = lax.slice_in_dim(slot_table, 0, piece_rows, axis=0)
    flat_piece = shard_piece.reshape(piece_rows, block_size * block_size)
    inverse_flat = start_blocks + jnp.einsum(
        "sb,sk->bk", rows_table, flat_piece, precision=exact_mode
    )
    inverse_blocks = inverse_flat.reshape(block_count, block_size, block_size)
    partial_grad = grad_parts[0]
    row_count, col_count = partial_grad.shape
    left_count = row_count // block_size
    right_count = col_count // block_size
    right_first = left_count + lax.axis_index("tensor") * right_count
    right_inv = lax.dynamic_slice_in_dim(inverse_blocks, right_first, right_count, 0)
    left_part = jnp.einsum(
        "nab,nbc->nac",
        inverse_blocks[:left_count],
        partial_grad.reshape(left_count, block_size, col_count),
        precision=exact_mode,
    ).reshape(row_count, col_count)
    precond = apply_right(left_part, right_inv, block_size)
    total_precond, total_grad = (
        lax.psum_scatter(precond, ("shards", "replica"), scatter_dimension=0, tiled=True),
        lax.psum_scatter(partial_grad, ("shards", "replica"), scatter_dimension=0, tiled=True),
    )
    alignment_sum = lax.psum(jnp.sum(total_precond * total_grad), ("shards", "tensor", "replica"))
    clip_scale = jnp.minimum(1.0, clip_norm / jnp.sqrt(alignment_sum))
    momentum_next = momentum_rate * momentum + clip_scale * total_precond
    weights_next = weights - step_rate * momentum_next
    gathered = lax.all_gather(weights_next, ("shards", "replica"), axis=0, tiled=True)
    return (gathered, momentum_next, mixed_factor_blocks)


def remote(src, dst, sends, recvs, index, device):
    return pltpu.make_async_remote_copy(
        src_ref=src,
        dst_ref=dst,
        send_sem=sends.at[index],
        recv_sem=recvs.at[index],
        device_id=device,
        device_id_type=MESH,
    )


def unpack_pair(packed, diagonal, lower, on_diagonal):
    flipped = packed.T
    first = jnp.where(lower, flipped, packed)
    second = jnp.where(lower, packed, jnp.where(on_diagonal, diagonal, flipped))
    return first, second


def split_halves(a):
    high = a.astype(jnp.bfloat16)
    return high, (a - high.astype(jnp.float32)).astype(jnp.bfloat16)


def dot_exact(a, b):
    a_high, a_low = split_halves(a)
    b_high, b_low = split_halves(b)
    dot = functools.partial(jnp.dot, preferred_element_type=jnp.float32)
    return dot(a_high, b_high) + (dot(a_high, b_low) + dot(a_low, b_high))


def ordered_sum(ref, count):
    terms = [ref[k] for k in range(count)]
    while len(terms) > 1:
        terms = [terms[k] + terms[k + 1] for k in range(0, len(terms), 2)]
    return terms[0]


def fused_kernel(
    sample_total,
    owner_ref,
    act_ref,
    gout_ref,
    grad_ref,
    old_ref,
    weights_ref,
    momentum_ref,
    weights_out,
    momentum_out,
    factors_out,
    act_v,
    gout_v,
    old_v,
    weights_v,
    momentum_v,
    packed_v,
    core_in,
    y_in,
    xz_out,
    xz_in,
    full_v,
    left_pair,
    diag_out,
    diag_in,
    diag_xz,
    grad_own,
    grad_x,
    grad_z,
    sum_out,
    sum_xz,
    sum_tensor,
    weights_all,
    mixed_v,
    local_sem,
    sends,
    recvs,
):
    s = lax.axis_index("shards")
    t = lax.axis_index("tensor")
    r = lax.axis_index("replica")
    y = t // 2
    c = t % 2
    n = 128
    half = 512
    quarter = 256
    place = s * 4 + r
    x_peer = (1 - s, t, r)
    y_peer = (s, 2 * (1 - y) + c, r)
    c_peer = (s, 2 * y + 1 - c, r)
    yc_peer = (s, 2 * (1 - y) + 1 - c, r)
    z_ranks = [(r + d) % 4 for d in (1, 2, 3)]
    z_peers = [(s, t, q) for q in z_ranks]
    xz_peers = z_peers + [(1 - s, t, q) for q in z_ranks] + [x_peer]
    xz_places = [s * 4 + q for q in z_ranks] + [(1 - s) * 4 + q for q in z_ranks]
    xz_places = xz_places + [(1 - s) * 4 + r]
    used_sems = [0]

    def part(ref, start, size):
        return ref.at[pl.ds(pl.multiple_of(start, 8), size)]

    def send(src, dst, device):
        copy = remote(src, dst, sends, recvs, used_sems[0], device)
        used_sems[0] += 1
        copy.start()
        return copy

    def load(src, dst, index):
        copy = pltpu.make_async_copy(src, dst, local_sem.at[index])
        copy.start()
        return copy

    barrier = pltpu.get_barrier_semaphore()
    peers = xz_peers + [y_peer, c_peer, yc_peer]
    for peer in peers:
        pl.semaphore_signal(barrier, inc=1, device_id=peer, device_id_type=MESH)

    groups = ((1 - y, 1 - c), (y, 1 - c), (1 - y, c), (y, c))
    starts = [pl.multiple_of(side * half + core * quarter, quarter) for side, core in groups]
    loads = []
    for k, start in enumerate(starts):
        columns = pl.ds(start, quarter)
        loads.append(load(act_ref.at[:, columns], act_v.at[:, columns], 2 * k))
        loads.append(load(gout_ref.at[:, columns], gout_v.at[:, columns], 2 * k + 1))
    weights_load = load(weights_ref, weights_v, 8)
    momentum_load = load(momentum_ref, momentum_v, 9)
    grad_load = load(grad_ref.at[0], grad_own, 10)
    old_load = load(old_ref, old_v, 11)

    rows = lax.broadcasted_iota(jnp.int32, (n, n), 0)
    cols = lax.broadcasted_iota(jnp.int32, (n, n), 1)
    lower = rows > cols
    on_diagonal = rows == cols
    pair_rows = lax.broadcasted_iota(jnp.int32, (8, n), 0)
    identity = on_diagonal.astype(jnp.float32)

    diag = jnp.zeros((8, n), jnp.float32)
    core_copies = []
    for j, (side, core) in enumerate(groups):
        loads[2 * j].wait()
        loads[2 * j + 1].wait()
        start = starts[j]
        a = act_v[:, pl.ds(start, quarter)]
        g = gout_v[:, pl.ds(start, quarter)]
        across = (((0,), (0,)), ((), ()))
        left = lax.dot_general(a, a, across, preferred_element_type=jnp.float32)
        right = lax.dot_general(g, g, across, preferred_element_type=jnp.float32)
        for k in range(2):
            span = slice(k * n, (k + 1) * n)
            second = right[span, span]
            packed_v[pl.ds(start + k * n, n), :] = jnp.where(lower, second, left[span, span])
            row = jnp.sum(jnp.where(on_diagonal, second, 0.0), axis=0, keepdims=True)
            diag = jnp.where(pair_rows == side * 4 + core * 2 + k, row, diag)
        if j == 0:
            pl.semaphore_wait(barrier, len(peers))
        if j < 2:
            core_copies.append(send(part(packed_v, start, quarter), core_in.at[j], c_peer))
        if j == 0:
            grad_load.wait()
            grad_x_copies = [
                send(part(grad_own, (1 - s) * half + q * n, n), grad_x.at[q], x_peer)
                for q in z_ranks + [r]
            ]
        elif j == 2:
            core_copies[0].wait()
            packed_v[pl.ds(start, quarter), :] += core_in[0]
            y_copy = send(part(packed_v, start, quarter), y_in, y_peer)
    diag_out[0] = diag
    copy = send(diag_out.at[0], diag_in.at[0], c_peer)
    core_copies[1].wait()
    mine = packed_v[pl.ds(starts[3], quarter), :] + core_in[1]
    copy.wait()
    diag = diag + diag_in[0]
    diag_out[1] = diag
    diag_copy = send(diag_out.at[1], diag_in.at[1], y_peer)
    y_copy.wait()
    xz_out[...] = (mine + y_in[...]).reshape(8, 32, n)
    copies = [
        send(xz_out.at[q], xz_in.at[place], peer) for q, peer in zip(xz_places, xz_peers)
    ]

    def add_gradient(k):
        q = (z_ranks + [r])[k]
        grad_x_copies[k].wait()
        grad_x[q] = grad_x[q] + grad_own[pl.ds(pl.multiple_of(s * half + q * n, n), n), :]
        if k < 3:
            grad_copies.append(send(grad_x.at[q], grad_z.at[r], z_peers[k]))

    grad_copies = []
    diag_copy.wait()
    diag = diag + diag_in[1]
    diag_out[2] = diag
    diag_copies = [send(diag_out.at[2], diag_xz.at[place], peer) for peer in xz_peers]
    xz_in[place] = xz_out[place]
    diag_xz[place] = diag
    add_gradient(0)
    for copy in copies:
        copy.wait()
    start = pl.multiple_of(starts[3] + place * 32, 32)
    full_v[pl.ds(start, 32), :] = ordered_sum(xz_in, 8)
    region = part(full_v, start, 32)
    copies = [send(region, region, peer) for peer in xz_peers]
    add_gradient(1)
    add_gradient(2)
    for copy in diag_copies:
        copy.wait()
    diag_out[3] = ordered_sum(diag_xz, 8)
    for copy in copies:
        copy.wait()

    holder = (s == y) & (r // 2 == c)
    pair_sem = used_sems[0]
    used_sems[0] += 3
    pair_copies = [
        pltpu.make_async_remote_copy(
            src_ref=part(full_v, place * n, n),
            dst_ref=left_pair,
            send_sem=sends.at[pair_sem + k],
            recv_sem=recvs.at[pair_sem],
            device_id=peer,
            device_id_type=MESH,
        )
        for k, peer in enumerate((yc_peer, y_peer, c_peer))
    ]

    @pl.when(holder)
    def _():
        for copy in pair_copies:
            copy.start()
        left_pair[...] = full_v[pl.ds(pl.multiple_of(place * n, n), n), :]

    region = part(full_v, starts[3], quarter)
    y_copy = send(region, region, y_peer)
    core_copies = [send(region, region, c_peer)]
    add_gradient(3)
    grad_z[r] = grad_x[r]

    def blend(pair, packed=None):
        if packed is None:
            packed = full_v[pl.ds(pl.multiple_of(pair * n, n), n), :]
        first, second = unpack_pair(
            packed,
            diag_out[3, pl.ds(pair, 1), :],
            lower,
            on_diagonal,
        )
        return (
            decay_rate * old_v[pair] + (1.0 - decay_rate) * (first / sample_total),
            decay_rate * old_v[8 + pair] + (1.0 - decay_rate) * (second / sample_total),
        )

    def invert(blocks):
        scales, rests = [], []
        for block in blocks:
            trace = jnp.sum(jnp.where(on_diagonal, block, 0.0), keepdims=True)
            damped = block + (damping * trace / n + damp_shift) * identity
            bound = jnp.max(
                jnp.sum(jnp.abs(damped), axis=1, keepdims=True), axis=0, keepdims=True
            )
            scales.append(1.0 / bound)
            rests.append(identity - damped / bound)
        inverses = [identity + rest for rest in rests]
        for _ in range(NS_STEPS - 1):
            rests = [dot_exact(rest, rest) for rest in rests]
            inverses = [inv + dot_exact(inv, rest) for inv, rest in zip(inverses, rests)]
        return [inv * scale for inv, scale in zip(inverses, scales)]

    old_load.wait()
    right_inverses = invert([blend(2 * t)[1], blend(2 * t + 1)[1]])

    @pl.when(jnp.logical_not(holder))
    def _():
        pair_copies[0].wait_recv()

    left_inverse = invert([blend(place, left_pair[...])[0]])[0]
    y_copy.wait()
    region = part(full_v, starts[2], quarter)
    core_copies.append(send(region, region, c_peer))

    for copy in grad_copies:
        copy.wait()
    gradient = (grad_z[0] + grad_z[1]) + (grad_z[2] + grad_z[3])
    left = dot_exact(left_inverse, gradient)
    precond = jnp.concatenate(
        [dot_exact(left[:, k * n : (k + 1) * n], right_inverses[k]) for k in range(2)], axis=1
    )
    products = precond * gradient
    products = products[:, :n] + products[:, n:]
    tile = jnp.sum(products.reshape(16, 8, n), axis=0)

    sum_out[0] = tile
    sum_copies = [send(sum_out.at[0], sum_xz.at[place], peer) for peer in xz_peers]

    first_sem = used_sems[0]
    used_sems[0] += 14

    def passing(hop, way, peer, hand_on):
        origin = r - hop if way == 0 else r + hop
        region = part(weights_all, (s * 4 + origin) * n, n)
        index = first_sem + 6 * hand_on + 2 * hop + way
        return remote(region, region, sends, recvs, index, peer)

    ways = ((s, t, r + 1), (s, t, r - 1))

    def sends_on(hop, way):
        return (r >= hop) & (r < 3) if way == 0 else (r <= 3 - hop) & (r > 0)

    def gets(hop, way):
        return r >= hop + 1 if way == 0 else r <= 2 - hop

    def start_hop(hop):
        for way in range(2):

            @pl.when(sends_on(hop, way))
            def _():
                passing(hop, way, ways[way], 0).start()

    def arrived(hop):
        for way in range(2):

            @pl.when(gets(hop, way))
            def _():
                back = ways[1 - way]
                origin = r - hop - 1 if way == 0 else r + hop + 1
                region = part(weights_all, (s * 4 + origin) * n, n)
                index = first_sem + 2 * hop + way
                remote(region, region, sends, recvs, index, back).wait_recv()

    def hand_on(hop):
        for way in range(2):

            @pl.when(gets(hop, way))
            def _():
                passing(hop + 1, way, x_peer, 1).start()

    sum_xz[place] = tile
    for copy in sum_copies:
        copy.wait()
    tile = ordered_sum(sum_xz, 8)
    sum_out[1] = tile
    sum_copies = [
        send(sum_out.at[1], sum_tensor.at[t], peer) for peer in (c_peer, y_peer, yc_peer)
    ]
    sum_tensor[t] = tile
    weights_load.wait()
    momentum_load.wait()
    for copy in sum_copies:
        copy.wait()
    alignment = jnp.sum(ordered_sum(sum_tensor, 4), keepdims=True)
    clip_scale = jnp.minimum(1.0, clip_norm / jnp.sqrt(alignment))
    momentum_next = momentum_rate * momentum_v[...] + clip_scale * precond
    weights_all[pl.ds(pl.multiple_of(place * n, n), n), :] = (
        weights_v[...] - step_rate * momentum_next
    )
    own = part(weights_all, place * n, n)
    x_copies = [send(own, own, x_peer)]
    start_hop(0)
    momentum_out[...] = momentum_next
    arrived(0)
    start_hop(1)
    hand_on(0)
    arrived(1)
    start_hop(2)
    hand_on(1)

    for copy in core_copies:
        copy.wait()

    @pl.when(holder)
    def _():
        for copy in pair_copies:
            copy.wait_send()

    for pair in range(8):
        mixed_v[pair], mixed_v[8 + pair] = blend(pair)
    mixed_v[16] = jnp.zeros((n, n), jnp.float32)
    block_total = owner_ref.shape[0]
    chosen = [jnp.int32(block_total)] * factors_out.shape[0]
    used = jnp.int32(0)
    for b in range(block_total):
        here = owner_ref[b] == s
        for k in range(min(b + 1, len(chosen))):
            chosen[k] = jnp.where(here & (used == k), jnp.int32(b), chosen[k])
        used = used + jnp.where(here, jnp.int32(1), jnp.int32(0))
    for k in range(len(chosen)):
        factors_out[k] = mixed_v[chosen[k]]

    arrived(2)
    hand_on(2)
    for copy in x_copies:
        copy.wait()
    for hop in range(3):
        for way in range(2):

            @pl.when(sends_on(hop, way))
            def _():
                passing(hop, way, ways[way], 0).wait_send()

            @pl.when(gets(hop, way))
            def _():
                passing(hop + 1, way, x_peer, 1).wait()

    weights_out[...] = weights_all[...]


def copy_out_kernel(
    weights, momentum, factors, weights_out, momentum_out, factors_out, *held_and_sems
):
    held, (loads, stores) = held_and_sems[:3], held_and_sems[3:]
    pieces = []
    for src, mid, dst, parts in (
        (weights, held[0], weights_out, 4),
        (factors, held[2], factors_out, 3),
        (momentum, held[1], momentum_out, 1),
    ):
        size = src.shape[0] // parts
        for k in range(parts):
            span = pl.ds(k * size, size)
            index = len(pieces)
            first = pltpu.make_async_copy(src.at[span], mid.at[span], loads.at[index])
            first.start()
            second = pltpu.make_async_copy(mid.at[span], dst.at[span], stores.at[index])
            pieces.append((first, second))
    for first, second in pieces:
        first.wait()
        second.start()
    for _, second in pieces:
        second.wait()


def fused_step(activations, grads_out, grad_parts, old_factors, block_owner, weights, momentum):
    n = old_factors.shape[1]
    shards = lax.axis_size("shards")
    capacity = (old_factors.shape[0] + shards - 1) // shards + 1
    devices = shards * lax.axis_size("tensor") * lax.axis_size("replica")
    f32 = jnp.float32
    anywhere = pl.BlockSpec(memory_space=pl.ANY)
    vmem = pl.BlockSpec(memory_space=pltpu.VMEM)
    results = pl.pallas_call(
        functools.partial(fused_kernel, float(activations.shape[0] * devices)),
        out_shape=(
            jax.ShapeDtypeStruct(grad_parts.shape[1:], f32),
            jax.ShapeDtypeStruct(momentum.shape, f32),
            jax.ShapeDtypeStruct((capacity, n, n), f32),
        ),
        in_specs=[
            pl.BlockSpec(memory_space=pltpu.SMEM),
            anywhere,
            anywhere,
            anywhere,
            anywhere,
            anywhere,
            anywhere,
        ],
        out_specs=(vmem, vmem, vmem),
        scratch_shapes=[
            pltpu.VMEM(activations.shape, activations.dtype),
            pltpu.VMEM(grads_out.shape, grads_out.dtype),
            pltpu.VMEM(old_factors.shape, f32),
            pltpu.VMEM(weights.shape, f32),
            pltpu.VMEM(momentum.shape, f32),
            pltpu.VMEM((1024, n), f32),
            pltpu.VMEM((2, 256, n), f32),
            pltpu.VMEM((256, n), f32),
            pltpu.VMEM((8, 32, n), f32),
            pltpu.VMEM((8, 32, n), f32),
            pltpu.VMEM((1024, n), f32),
            pltpu.VMEM((n, n), f32),
            pltpu.VMEM((4, 8, n), f32),
            pltpu.VMEM((2, 8, n), f32),
            pltpu.VMEM((8, 8, n), f32),
            pltpu.VMEM((1024, 256), f32),
            pltpu.VMEM((4, n, 256), f32),
            pltpu.VMEM((4, n, 256), f32),
            pltpu.VMEM((2, 8, n), f32),
            pltpu.VMEM((8, 8, n), f32),
            pltpu.VMEM((4, 8, n), f32),
            pltpu.VMEM((1024, 256), f32),
            pltpu.VMEM((17, n, n), f32),
            pltpu.SemaphoreType.DMA((12,)),
            pltpu.SemaphoreType.DMA((72,)),
            pltpu.SemaphoreType.DMA((72,)),
        ],
        compiler_params=pltpu.CompilerParams(
            collective_id=0, has_side_effects=True, vmem_limit_bytes=60 * 1024 * 1024
        ),
        cost_estimate=pl.CostEstimate(
            flops=1_200_000_000, bytes_accessed=10_000_000, transcendentals=0
        ),
    )(block_owner, activations, grads_out, grad_parts, old_factors, weights, momentum)
    return pl.pallas_call(
        copy_out_kernel,
        out_shape=tuple(jax.ShapeDtypeStruct(a.shape, a.dtype) for a in results),
        in_specs=[anywhere] * 3,
        out_specs=(anywhere,) * 3,
        scratch_shapes=[pltpu.VMEM(a.shape, a.dtype) for a in results]
        + [pltpu.SemaphoreType.DMA((8,))] * 2,
        compiler_params=pltpu.CompilerParams(vmem_limit_bytes=60 * 1024 * 1024),
        cost_estimate=pl.CostEstimate(flops=0, bytes_accessed=3_500_000, transcendentals=0),
    )(*results)


def step(activations, grads_out, grad_parts, old_factors, block_owner, weights, momentum):
    sizes = tuple(lax.axis_size(name) for name in ("shards", "tensor", "replica"))
    fits = (
        sizes == (2, 4, 4)
        and weights.shape == (128, 256)
        and old_factors.shape == (16, 128, 128)
        and activations.shape == grads_out.shape == (1024, 1024)
    )
    chosen = fused_step if fits else body
    return chosen(
        activations, grads_out, grad_parts, old_factors, block_owner, weights, momentum
    )


def solution(mesh):
    placed = (
        P(("shards", "tensor", "replica"), None),
        P(("shards", "tensor", "replica"), None),
        P(("shards", "replica"), None, "tensor"),
        P(),
        P(),
        P(("shards", "replica"), "tensor"),
        P(("shards", "replica"), "tensor"),
    )
    return jax.shard_map(
        step,
        mesh=mesh,
        in_specs=placed,
        out_specs=(P(None, "tensor"), P(("shards", "replica"), "tensor"), P("shards", None, None)),
        check_vma=False,
    )
```

```python
import functools

import jax
import jax.numpy as jnp
from jax import lax
from jax.experimental import pallas as pl
from jax.experimental.pallas import tpu as pltpu
from jax.sharding import PartitionSpec as P

MESH = pl.DeviceIdType.MESH

NS_STEPS = 4


exact_mode = lax.Precision.HIGHEST
decay_rate = 0.75
damping = 0.1
damp_shift = 0.001
clip_norm = 256.0
momentum_rate = 0.9
step_rate = 0.05


def sample_stats(samples, block_size):
    sample_rows, width = samples.shape
    blocks = samples.reshape(sample_rows, width // block_size, block_size)
    return jnp.einsum("tnb,tnc->nbc", blocks, blocks, preferred_element_type=jnp.float32)


def build_slots(block_owner, capacity, slot_count):
    block_count = block_owner.shape[0]
    positions = jnp.arange(block_count, dtype=jnp.int32)
    earlier = (block_owner[:, None] == block_owner[None, :]) & (
        positions[None, :] < positions[:, None]
    )
    owner_slot_list = block_owner * capacity + jnp.sum(earlier.astype(jnp.int32), axis=1)
    return (owner_slot_list[None, :] == jnp.arange(slot_count, dtype=jnp.int32)[:, None]).astype(
        jnp.float32
    )


def newton_inverse(mixed_factor_blocks):
    block_size = mixed_factor_blocks.shape[-1]
    identity = jnp.eye(block_size, dtype=jnp.float32)
    traces = jnp.trace(mixed_factor_blocks, axis1=1, axis2=2)
    damped = (
        mixed_factor_blocks + (damping * traces / block_size + damp_shift)[:, None, None] * identity
    )
    bounds = jnp.max(jnp.sum(jnp.abs(damped), axis=2), axis=1)
    approx = identity[None, :, :] / bounds[:, None, None]
    for iteration in range(NS_STEPS):
        left_part = jnp.einsum("nab,nbc->nac", approx, damped, precision=exact_mode)
        approx = 2.0 * approx - jnp.einsum("nab,nbc->nac", left_part, approx, precision=exact_mode)
    return approx


def apply_right(left_part, right_inv, block_size):
    row_count, col_count = left_part.shape
    right_count = col_count // block_size
    return jnp.einsum(
        "rnb,nbc->rnc",
        left_part.reshape(row_count, right_count, block_size),
        right_inv,
        precision=exact_mode,
    ).reshape(row_count, col_count)


def body(activations, grads_out, grad_parts, old_factors, block_owner, weights, momentum):
    shard_count = lax.axis_size("shards")
    block_count = old_factors.shape[0]
    block_size = old_factors.shape[1]
    capacity = (block_count + shard_count - 1) // shard_count + 1
    slot_count = capacity * shard_count
    slot_table = build_slots(block_owner, capacity, slot_count)
    local_stats = jnp.concatenate(
        [sample_stats(activations, block_size), sample_stats(grads_out, block_size)], axis=0
    )
    packed = jnp.dot(
        slot_table, local_stats.reshape(block_count, block_size * block_size), precision=exact_mode
    )
    first_slot = lax.axis_index("shards") * capacity
    summed = lax.psum(packed, ("shards", "tensor", "replica"))
    owned = lax.dynamic_slice_in_dim(summed, first_slot, capacity, 0)
    sample_count = (
        activations.shape[0] * shard_count * lax.axis_size("tensor") * lax.axis_size("replica")
    )
    owned_table = lax.dynamic_slice_in_dim(slot_table, first_slot, capacity, 0)
    old_owned = jnp.dot(
        owned_table, old_factors.reshape(block_count, block_size * block_size), precision=exact_mode
    )
    mixed_factor_blocks = (
        decay_rate * old_owned + (1.0 - decay_rate) * (owned / sample_count)
    ).reshape(capacity, block_size, block_size)
    inverse_owned = newton_inverse(mixed_factor_blocks)
    start_blocks = jnp.zeros((block_count, block_size * block_size), jnp.float32)
    shard_piece = lax.all_gather(inverse_owned, "shards", axis=0, tiled=True)
    piece_rows = shard_piece.shape[0]
    rows_table = lax.slice_in_dim(slot_table, 0, piece_rows, axis=0)
    flat_piece = shard_piece.reshape(piece_rows, block_size * block_size)
    inverse_flat = start_blocks + jnp.einsum(
        "sb,sk->bk", rows_table, flat_piece, precision=exact_mode
    )
    inverse_blocks = inverse_flat.reshape(block_count, block_size, block_size)
    partial_grad = grad_parts[0]
    row_count, col_count = partial_grad.shape
    left_count = row_count // block_size
    right_count = col_count // block_size
    right_first = left_count + lax.axis_index("tensor") * right_count
    right_inv = lax.dynamic_slice_in_dim(inverse_blocks, right_first, right_count, 0)
    left_part = jnp.einsum(
        "nab,nbc->nac",
        inverse_blocks[:left_count],
        partial_grad.reshape(left_count, block_size, col_count),
        precision=exact_mode,
    ).reshape(row_count, col_count)
    precond = apply_right(left_part, right_inv, block_size)
    total_precond, total_grad = (
        lax.psum_scatter(precond, ("shards", "replica"), scatter_dimension=0, tiled=True),
        lax.psum_scatter(partial_grad, ("shards", "replica"), scatter_dimension=0, tiled=True),
    )
    alignment_sum = lax.psum(jnp.sum(total_precond * total_grad), ("shards", "tensor", "replica"))
    clip_scale = jnp.minimum(1.0, clip_norm / jnp.sqrt(alignment_sum))
    momentum_next = momentum_rate * momentum + clip_scale * total_precond
    weights_next = weights - step_rate * momentum_next
    gathered = lax.all_gather(weights_next, ("shards", "replica"), axis=0, tiled=True)
    return (gathered, momentum_next, mixed_factor_blocks)


def remote(src, dst, sends, recvs, index, device):
    return pltpu.make_async_remote_copy(
        src_ref=src,
        dst_ref=dst,
        send_sem=sends.at[index],
        recv_sem=recvs.at[index],
        device_id=device,
        device_id_type=MESH,
    )


def unpack_pair(packed, diagonal, lower, on_diagonal):
    flipped = packed.T
    first = jnp.where(lower, flipped, packed)
    second = jnp.where(lower, packed, jnp.where(on_diagonal, diagonal, flipped))
    return first, second


def split_halves(a):
    high = a.astype(jnp.bfloat16)
    return high, (a - high.astype(jnp.float32)).astype(jnp.bfloat16)


def dot_exact(a, b):
    a_high, a_low = split_halves(a)
    b_high, b_low = split_halves(b)
    dot = functools.partial(jnp.dot, preferred_element_type=jnp.float32)
    return dot(a_high, b_high) + (dot(a_high, b_low) + dot(a_low, b_high))


def ordered_sum(ref, count):
    terms = [ref[k] for k in range(count)]
    while len(terms) > 1:
        terms = [terms[k] + terms[k + 1] for k in range(0, len(terms), 2)]
    return terms[0]


def fused_kernel(
    sample_total,
    owner_ref,
    act_ref,
    gout_ref,
    grad_ref,
    old_ref,
    weights_ref,
    momentum_ref,
    weights_out,
    momentum_out,
    factors_out,
    act_v,
    gout_v,
    old_v,
    weights_v,
    momentum_v,
    packed_v,
    core_in,
    y_in,
    xz_out,
    xz_in,
    full_v,
    left_pair,
    diag_out,
    diag_in,
    diag_xz,
    grad_own,
    grad_x,
    grad_z,
    sum_out,
    sum_xz,
    sum_tensor,
    base_all,
    precond_all,
    mixed_v,
    local_sem,
    sends,
    recvs,
):
    s = lax.axis_index("shards")
    t = lax.axis_index("tensor")
    r = lax.axis_index("replica")
    y = t // 2
    c = t % 2
    n = 128
    half = 512
    quarter = 256
    place = s * 4 + r
    x_peer = (1 - s, t, r)
    y_peer = (s, 2 * (1 - y) + c, r)
    c_peer = (s, 2 * y + 1 - c, r)
    yc_peer = (s, 2 * (1 - y) + 1 - c, r)
    z_ranks = [(r + d) % 4 for d in (1, 2, 3)]
    z_peers = [(s, t, q) for q in z_ranks]
    xz_peers = z_peers + [(1 - s, t, q) for q in z_ranks] + [x_peer]
    xz_places = [s * 4 + q for q in z_ranks] + [(1 - s) * 4 + q for q in z_ranks]
    xz_places = xz_places + [(1 - s) * 4 + r]
    used_sems = [0]

    def part(ref, start, size):
        return ref.at[pl.ds(pl.multiple_of(start, 8), size)]

    def send(src, dst, device):
        copy = remote(src, dst, sends, recvs, used_sems[0], device)
        used_sems[0] += 1
        copy.start()
        return copy

    def load(src, dst, index):
        copy = pltpu.make_async_copy(src, dst, local_sem.at[index])
        copy.start()
        return copy

    barrier = pltpu.get_barrier_semaphore()
    peers = xz_peers + [y_peer, c_peer, yc_peer]
    for peer in peers:
        pl.semaphore_signal(barrier, inc=1, device_id=peer, device_id_type=MESH)

    groups = ((1 - y, 1 - c), (y, 1 - c), (1 - y, c), (y, c))
    starts = [pl.multiple_of(side * half + core * quarter, quarter) for side, core in groups]
    loads = []
    for k, start in enumerate(starts):
        columns = pl.ds(start, quarter)
        loads.append(load(act_ref.at[:, columns], act_v.at[:, columns], 2 * k))
        loads.append(load(gout_ref.at[:, columns], gout_v.at[:, columns], 2 * k + 1))
    weights_load = load(weights_ref, weights_v, 8)
    momentum_load = load(momentum_ref, momentum_v, 9)
    grad_load = load(grad_ref.at[0], grad_own, 10)
    old_load = load(old_ref, old_v, 11)

    rows = lax.broadcasted_iota(jnp.int32, (n, n), 0)
    cols = lax.broadcasted_iota(jnp.int32, (n, n), 1)
    lower = rows > cols
    on_diagonal = rows == cols
    pair_rows = lax.broadcasted_iota(jnp.int32, (8, n), 0)
    identity = on_diagonal.astype(jnp.float32)

    diag = jnp.zeros((8, n), jnp.float32)
    core_copies = []
    for j, (side, core) in enumerate(groups):
        loads[2 * j].wait()
        loads[2 * j + 1].wait()
        start = starts[j]
        a = act_v[:, pl.ds(start, quarter)]
        g = gout_v[:, pl.ds(start, quarter)]
        across = (((0,), (0,)), ((), ()))
        left = lax.dot_general(a, a, across, preferred_element_type=jnp.float32)
        right = lax.dot_general(g, g, across, preferred_element_type=jnp.float32)
        for k in range(2):
            span = slice(k * n, (k + 1) * n)
            second = right[span, span]
            packed_v[pl.ds(start + k * n, n), :] = jnp.where(lower, second, left[span, span])
            row = jnp.sum(jnp.where(on_diagonal, second, 0.0), axis=0, keepdims=True)
            diag = jnp.where(pair_rows == side * 4 + core * 2 + k, row, diag)
        if j == 0:
            pl.semaphore_wait(barrier, len(peers))
        if j < 2:
            core_copies.append(send(part(packed_v, start, quarter), core_in.at[j], c_peer))
        if j == 0:
            grad_load.wait()
            grad_x_copies = [
                send(part(grad_own, (1 - s) * half + q * n, n), grad_x.at[q], x_peer)
                for q in z_ranks + [r]
            ]
        elif j == 1:
            weights_load.wait()
            momentum_load.wait()
            own_rows = pl.ds(pl.multiple_of(place * n, n), n)
            base_all[own_rows, :] = weights_v[...] - (step_rate * momentum_rate) * momentum_v[...]
            base_own = part(base_all, place * n, n)
            base_copies = [send(base_own, base_own, peer) for peer in z_peers]
        elif j == 2:
            core_copies[0].wait()
            packed_v[pl.ds(start, quarter), :] += core_in[0]
            y_copy = send(part(packed_v, start, quarter), y_in, y_peer)
    diag_out[0] = diag
    copy = send(diag_out.at[0], diag_in.at[0], c_peer)
    core_copies[1].wait()
    mine = packed_v[pl.ds(starts[3], quarter), :] + core_in[1]
    copy.wait()
    diag = diag + diag_in[0]
    diag_out[1] = diag
    diag_copy = send(diag_out.at[1], diag_in.at[1], y_peer)
    y_copy.wait()
    xz_out[...] = (mine + y_in[...]).reshape(8, 32, n)
    copies = [
        send(xz_out.at[q], xz_in.at[place], peer) for q, peer in zip(xz_places, xz_peers)
    ]

    def add_gradient(k):
        q = (z_ranks + [r])[k]
        grad_x_copies[k].wait()
        grad_x[q] = grad_x[q] + grad_own[pl.ds(pl.multiple_of(s * half + q * n, n), n), :]
        if k < 3:
            grad_copies.append(send(grad_x.at[q], grad_z.at[r], z_peers[k]))

    grad_copies = []
    diag_copy.wait()
    diag = diag + diag_in[1]
    diag_out[2] = diag
    diag_copies = [send(diag_out.at[2], diag_xz.at[place], peer) for peer in xz_peers]
    xz_in[place] = xz_out[place]
    diag_xz[place] = diag
    for copy in copies:
        copy.wait()
    start = pl.multiple_of(starts[3] + place * 32, 32)
    full_v[pl.ds(start, 32), :] = ordered_sum(xz_in, 8)
    region = part(full_v, start, 32)
    copies = [send(region, region, peer) for peer in xz_peers]
    add_gradient(0)
    add_gradient(1)
    for copy in diag_copies:
        copy.wait()
    diag_out[3] = ordered_sum(diag_xz, 8)
    for copy in copies:
        copy.wait()

    holder = (s == y) & (r // 2 == c)
    pair_sem = used_sems[0]
    used_sems[0] += 3
    pair_copies = [
        pltpu.make_async_remote_copy(
            src_ref=part(full_v, place * n, n),
            dst_ref=left_pair,
            send_sem=sends.at[pair_sem + k],
            recv_sem=recvs.at[pair_sem],
            device_id=peer,
            device_id_type=MESH,
        )
        for k, peer in enumerate((yc_peer, y_peer, c_peer))
    ]

    @pl.when(holder)
    def _():
        for copy in pair_copies:
            copy.start()
        left_pair[...] = full_v[pl.ds(pl.multiple_of(place * n, n), n), :]

    region = part(full_v, starts[3], quarter)
    y_copy = send(region, region, y_peer)
    core_copies = [send(region, region, c_peer)]
    add_gradient(2)
    add_gradient(3)
    grad_z[r] = grad_x[r]
    for copy in base_copies:
        copy.wait()
    region = part(base_all, s * half, half)
    base_copy = send(region, region, x_peer)

    def blend(pair, packed=None):
        if packed is None:
            packed = full_v[pl.ds(pl.multiple_of(pair * n, n), n), :]
        first, second = unpack_pair(
            packed,
            diag_out[3, pl.ds(pair, 1), :],
            lower,
            on_diagonal,
        )
        return (
            decay_rate * old_v[pair] + (1.0 - decay_rate) * (first / sample_total),
            decay_rate * old_v[8 + pair] + (1.0 - decay_rate) * (second / sample_total),
        )

    def invert(blocks):
        scales, rests = [], []
        for block in blocks:
            trace = jnp.sum(jnp.where(on_diagonal, block, 0.0), keepdims=True)
            damped = block + (damping * trace / n + damp_shift) * identity
            bound = jnp.max(
                jnp.sum(jnp.abs(damped), axis=1, keepdims=True), axis=0, keepdims=True
            )
            scales.append(1.0 / bound)
            rests.append(identity - damped / bound)
        inverses = [identity + rest for rest in rests]
        for _ in range(NS_STEPS - 1):
            rests = [dot_exact(rest, rest) for rest in rests]
            inverses = [inv + dot_exact(inv, rest) for inv, rest in zip(inverses, rests)]
        return [inv * scale for inv, scale in zip(inverses, scales)]

    old_load.wait()
    right_inverses = invert([blend(2 * t)[1], blend(2 * t + 1)[1]])

    @pl.when(jnp.logical_not(holder))
    def _():
        pair_copies[0].wait_recv()

    left_inverse = invert([blend(place, left_pair[...])[0]])[0]
    y_copy.wait()
    region = part(full_v, starts[2], quarter)
    core_copies.append(send(region, region, c_peer))

    for copy in grad_copies:
        copy.wait()
    gradient = (grad_z[0] + grad_z[1]) + (grad_z[2] + grad_z[3])
    left = dot_exact(left_inverse, gradient)
    precond = jnp.concatenate(
        [dot_exact(left[:, k * n : (k + 1) * n], right_inverses[k]) for k in range(2)], axis=1
    )
    products = precond * gradient
    products = products[:, :n] + products[:, n:]
    tile = jnp.sum(products.reshape(16, 8, n), axis=0)

    sum_out[0] = tile
    sum_copies = [send(sum_out.at[0], sum_xz.at[place], peer) for peer in xz_peers]
    precond_all[pl.ds(pl.multiple_of(place * n, n), n), :] = precond
    own = part(precond_all, place * n, n)
    x_copies = [send(own, own, x_peer)]

    first_sem = used_sems[0]
    used_sems[0] += 14

    def passing(hop, way, peer, hand_on):
        origin = r - hop if way == 0 else r + hop
        region = part(precond_all, (s * 4 + origin) * n, n)
        index = first_sem + 6 * hand_on + 2 * hop + way
        return remote(region, region, sends, recvs, index, peer)

    ways = ((s, t, r + 1), (s, t, r - 1))

    def sends_on(hop, way):
        return (r >= hop) & (r < 3) if way == 0 else (r <= 3 - hop) & (r > 0)

    def gets(hop, way):
        return r >= hop + 1 if way == 0 else r <= 2 - hop

    def start_hop(hop):
        for way in range(2):

            @pl.when(sends_on(hop, way))
            def _():
                passing(hop, way, ways[way], 0).start()

    def arrived(hop):
        for way in range(2):

            @pl.when(gets(hop, way))
            def _():
                back = ways[1 - way]
                origin = r - hop - 1 if way == 0 else r + hop + 1
                region = part(precond_all, (s * 4 + origin) * n, n)
                index = first_sem + 2 * hop + way
                remote(region, region, sends, recvs, index, back).wait_recv()

    def hand_on(hop):
        for way in range(2):

            @pl.when(gets(hop, way))
            def _():
                passing(hop + 1, way, x_peer, 1).start()

    start_hop(0)
    sum_xz[place] = tile
    for copy in sum_copies:
        copy.wait()
    tile = ordered_sum(sum_xz, 8)
    sum_out[1] = tile
    sum_copies = [
        send(sum_out.at[1], sum_tensor.at[t], peer) for peer in (c_peer, y_peer, yc_peer)
    ]
    sum_tensor[t] = tile
    arrived(0)
    start_hop(1)
    hand_on(0)
    for copy in sum_copies:
        copy.wait()
    alignment = jnp.sum(ordered_sum(sum_tensor, 4), keepdims=True)
    clip_scale = jnp.minimum(1.0, clip_norm / jnp.sqrt(alignment))
    momentum_out[...] = momentum_rate * momentum_v[...] + clip_scale * precond
    arrived(1)
    start_hop(2)
    hand_on(1)

    for copy in core_copies:
        copy.wait()

    @pl.when(holder)
    def _():
        for copy in pair_copies:
            copy.wait_send()

    for pair in range(8):
        mixed_v[pair], mixed_v[8 + pair] = blend(pair)
    mixed_v[16] = jnp.zeros((n, n), jnp.float32)
    block_total = owner_ref.shape[0]
    chosen = [jnp.int32(block_total)] * factors_out.shape[0]
    used = jnp.int32(0)
    for b in range(block_total):
        here = owner_ref[b] == s
        for k in range(min(b + 1, len(chosen))):
            chosen[k] = jnp.where(here & (used == k), jnp.int32(b), chosen[k])
        used = used + jnp.where(here, jnp.int32(1), jnp.int32(0))
    for k in range(len(chosen)):
        factors_out[k] = mixed_v[chosen[k]]

    arrived(2)
    hand_on(2)
    base_copy.wait()
    for copy in x_copies:
        copy.wait()
    for hop in range(3):
        for way in range(2):

            @pl.when(sends_on(hop, way))
            def _():
                passing(hop, way, ways[way], 0).wait_send()

            @pl.when(gets(hop, way))
            def _():
                passing(hop + 1, way, x_peer, 1).wait()

    weights_out[...] = base_all[...] - (step_rate * clip_scale) * precond_all[...]


def copy_out_kernel(
    weights, momentum, factors, weights_out, momentum_out, factors_out, *held_and_sems
):
    held, (loads, stores) = held_and_sems[:3], held_and_sems[3:]
    pieces = []
    for src, mid, dst, parts in (
        (weights, held[0], weights_out, 4),
        (factors, held[2], factors_out, 3),
        (momentum, held[1], momentum_out, 1),
    ):
        size = src.shape[0] // parts
        for k in range(parts):
            span = pl.ds(k * size, size)
            index = len(pieces)
            first = pltpu.make_async_copy(src.at[span], mid.at[span], loads.at[index])
            first.start()
            second = pltpu.make_async_copy(mid.at[span], dst.at[span], stores.at[index])
            pieces.append((first, second))
    for first, second in pieces:
        first.wait()
        second.start()
    for _, second in pieces:
        second.wait()


def fused_step(activations, grads_out, grad_parts, old_factors, block_owner, weights, momentum):
    n = old_factors.shape[1]
    shards = lax.axis_size("shards")
    capacity = (old_factors.shape[0] + shards - 1) // shards + 1
    devices = shards * lax.axis_size("tensor") * lax.axis_size("replica")
    f32 = jnp.float32
    anywhere = pl.BlockSpec(memory_space=pl.ANY)
    vmem = pl.BlockSpec(memory_space=pltpu.VMEM)
    results = pl.pallas_call(
        functools.partial(fused_kernel, float(activations.shape[0] * devices)),
        out_shape=(
            jax.ShapeDtypeStruct(grad_parts.shape[1:], f32),
            jax.ShapeDtypeStruct(momentum.shape, f32),
            jax.ShapeDtypeStruct((capacity, n, n), f32),
        ),
        in_specs=[
            pl.BlockSpec(memory_space=pltpu.SMEM),
            anywhere,
            anywhere,
            anywhere,
            anywhere,
            anywhere,
            anywhere,
        ],
        out_specs=(vmem, vmem, vmem),
        scratch_shapes=[
            pltpu.VMEM(activations.shape, activations.dtype),
            pltpu.VMEM(grads_out.shape, grads_out.dtype),
            pltpu.VMEM(old_factors.shape, f32),
            pltpu.VMEM(weights.shape, f32),
            pltpu.VMEM(momentum.shape, f32),
            pltpu.VMEM((1024, n), f32),
            pltpu.VMEM((2, 256, n), f32),
            pltpu.VMEM((256, n), f32),
            pltpu.VMEM((8, 32, n), f32),
            pltpu.VMEM((8, 32, n), f32),
            pltpu.VMEM((1024, n), f32),
            pltpu.VMEM((n, n), f32),
            pltpu.VMEM((4, 8, n), f32),
            pltpu.VMEM((2, 8, n), f32),
            pltpu.VMEM((8, 8, n), f32),
            pltpu.VMEM((1024, 256), f32),
            pltpu.VMEM((4, n, 256), f32),
            pltpu.VMEM((4, n, 256), f32),
            pltpu.VMEM((2, 8, n), f32),
            pltpu.VMEM((8, 8, n), f32),
            pltpu.VMEM((4, 8, n), f32),
            pltpu.VMEM((1024, 256), f32),
            pltpu.VMEM((1024, 256), f32),
            pltpu.VMEM((17, n, n), f32),
            pltpu.SemaphoreType.DMA((12,)),
            pltpu.SemaphoreType.DMA((72,)),
            pltpu.SemaphoreType.DMA((72,)),
        ],
        compiler_params=pltpu.CompilerParams(
            collective_id=0, has_side_effects=True, vmem_limit_bytes=60 * 1024 * 1024
        ),
        cost_estimate=pl.CostEstimate(
            flops=1_200_000_000, bytes_accessed=10_000_000, transcendentals=0
        ),
    )(block_owner, activations, grads_out, grad_parts, old_factors, weights, momentum)
    return pl.pallas_call(
        copy_out_kernel,
        out_shape=tuple(jax.ShapeDtypeStruct(a.shape, a.dtype) for a in results),
        in_specs=[anywhere] * 3,
        out_specs=(anywhere,) * 3,
        scratch_shapes=[pltpu.VMEM(a.shape, a.dtype) for a in results]
        + [pltpu.SemaphoreType.DMA((8,))] * 2,
        compiler_params=pltpu.CompilerParams(vmem_limit_bytes=60 * 1024 * 1024),
        cost_estimate=pl.CostEstimate(flops=0, bytes_accessed=3_500_000, transcendentals=0),
    )(*results)


def step(activations, grads_out, grad_parts, old_factors, block_owner, weights, momentum):
    sizes = tuple(lax.axis_size(name) for name in ("shards", "tensor", "replica"))
    fits = (
        sizes == (2, 4, 4)
        and weights.shape == (128, 256)
        and old_factors.shape == (16, 128, 128)
        and activations.shape == grads_out.shape == (1024, 1024)
    )
    chosen = fused_step if fits else body
    return chosen(
        activations, grads_out, grad_parts, old_factors, block_owner, weights, momentum
    )


def solution(mesh):
    placed = (
        P(("shards", "tensor", "replica"), None),
        P(("shards", "tensor", "replica"), None),
        P(("shards", "replica"), None, "tensor"),
        P(),
        P(),
        P(("shards", "replica"), "tensor"),
        P(("shards", "replica"), "tensor"),
    )
    return jax.shard_map(
        step,
        mesh=mesh,
        in_specs=placed,
        out_specs=(P(None, "tensor"), P(("shards", "replica"), "tensor"), P("shards", None, None)),
        check_vma=False,
    )
```

```python
import functools

import jax
import jax.numpy as jnp
from jax import lax
from jax.experimental import pallas as pl
from jax.experimental.pallas import tpu as pltpu
from jax.sharding import PartitionSpec as P

MESH = pl.DeviceIdType.MESH

NS_STEPS = 4


exact_mode = lax.Precision.HIGHEST
decay_rate = 0.75
damping = 0.1
damp_shift = 0.001
clip_norm = 256.0
momentum_rate = 0.9
step_rate = 0.05


def sample_stats(samples, block_size):
    sample_rows, width = samples.shape
    blocks = samples.reshape(sample_rows, width // block_size, block_size)
    return jnp.einsum("tnb,tnc->nbc", blocks, blocks, preferred_element_type=jnp.float32)


def build_slots(block_owner, capacity, slot_count):
    block_count = block_owner.shape[0]
    positions = jnp.arange(block_count, dtype=jnp.int32)
    earlier = (block_owner[:, None] == block_owner[None, :]) & (
        positions[None, :] < positions[:, None]
    )
    owner_slot_list = block_owner * capacity + jnp.sum(earlier.astype(jnp.int32), axis=1)
    return (owner_slot_list[None, :] == jnp.arange(slot_count, dtype=jnp.int32)[:, None]).astype(
        jnp.float32
    )


def newton_inverse(mixed_factor_blocks):
    block_size = mixed_factor_blocks.shape[-1]
    identity = jnp.eye(block_size, dtype=jnp.float32)
    traces = jnp.trace(mixed_factor_blocks, axis1=1, axis2=2)
    damped = (
        mixed_factor_blocks + (damping * traces / block_size + damp_shift)[:, None, None] * identity
    )
    bounds = jnp.max(jnp.sum(jnp.abs(damped), axis=2), axis=1)
    approx = identity[None, :, :] / bounds[:, None, None]
    for iteration in range(NS_STEPS):
        left_part = jnp.einsum("nab,nbc->nac", approx, damped, precision=exact_mode)
        approx = 2.0 * approx - jnp.einsum("nab,nbc->nac", left_part, approx, precision=exact_mode)
    return approx


def apply_right(left_part, right_inv, block_size):
    row_count, col_count = left_part.shape
    right_count = col_count // block_size
    return jnp.einsum(
        "rnb,nbc->rnc",
        left_part.reshape(row_count, right_count, block_size),
        right_inv,
        precision=exact_mode,
    ).reshape(row_count, col_count)


def body(activations, grads_out, grad_parts, old_factors, block_owner, weights, momentum):
    shard_count = lax.axis_size("shards")
    block_count = old_factors.shape[0]
    block_size = old_factors.shape[1]
    capacity = (block_count + shard_count - 1) // shard_count + 1
    slot_count = capacity * shard_count
    slot_table = build_slots(block_owner, capacity, slot_count)
    local_stats = jnp.concatenate(
        [sample_stats(activations, block_size), sample_stats(grads_out, block_size)], axis=0
    )
    packed = jnp.dot(
        slot_table, local_stats.reshape(block_count, block_size * block_size), precision=exact_mode
    )
    first_slot = lax.axis_index("shards") * capacity
    summed = lax.psum(packed, ("shards", "tensor", "replica"))
    owned = lax.dynamic_slice_in_dim(summed, first_slot, capacity, 0)
    sample_count = (
        activations.shape[0] * shard_count * lax.axis_size("tensor") * lax.axis_size("replica")
    )
    owned_table = lax.dynamic_slice_in_dim(slot_table, first_slot, capacity, 0)
    old_owned = jnp.dot(
        owned_table, old_factors.reshape(block_count, block_size * block_size), precision=exact_mode
    )
    mixed_factor_blocks = (
        decay_rate * old_owned + (1.0 - decay_rate) * (owned / sample_count)
    ).reshape(capacity, block_size, block_size)
    inverse_owned = newton_inverse(mixed_factor_blocks)
    start_blocks = jnp.zeros((block_count, block_size * block_size), jnp.float32)
    shard_piece = lax.all_gather(inverse_owned, "shards", axis=0, tiled=True)
    piece_rows = shard_piece.shape[0]
    rows_table = lax.slice_in_dim(slot_table, 0, piece_rows, axis=0)
    flat_piece = shard_piece.reshape(piece_rows, block_size * block_size)
    inverse_flat = start_blocks + jnp.einsum(
        "sb,sk->bk", rows_table, flat_piece, precision=exact_mode
    )
    inverse_blocks = inverse_flat.reshape(block_count, block_size, block_size)
    partial_grad = grad_parts[0]
    row_count, col_count = partial_grad.shape
    left_count = row_count // block_size
    right_count = col_count // block_size
    right_first = left_count + lax.axis_index("tensor") * right_count
    right_inv = lax.dynamic_slice_in_dim(inverse_blocks, right_first, right_count, 0)
    left_part = jnp.einsum(
        "nab,nbc->nac",
        inverse_blocks[:left_count],
        partial_grad.reshape(left_count, block_size, col_count),
        precision=exact_mode,
    ).reshape(row_count, col_count)
    precond = apply_right(left_part, right_inv, block_size)
    total_precond, total_grad = (
        lax.psum_scatter(precond, ("shards", "replica"), scatter_dimension=0, tiled=True),
        lax.psum_scatter(partial_grad, ("shards", "replica"), scatter_dimension=0, tiled=True),
    )
    alignment_sum = lax.psum(jnp.sum(total_precond * total_grad), ("shards", "tensor", "replica"))
    clip_scale = jnp.minimum(1.0, clip_norm / jnp.sqrt(alignment_sum))
    momentum_next = momentum_rate * momentum + clip_scale * total_precond
    weights_next = weights - step_rate * momentum_next
    gathered = lax.all_gather(weights_next, ("shards", "replica"), axis=0, tiled=True)
    return (gathered, momentum_next, mixed_factor_blocks)


def remote(src, dst, sends, recvs, index, device):
    return pltpu.make_async_remote_copy(
        src_ref=src,
        dst_ref=dst,
        send_sem=sends.at[index],
        recv_sem=recvs.at[index],
        device_id=device,
        device_id_type=MESH,
    )


def unpack_pair(packed, diagonal, lower, on_diagonal):
    flipped = packed.T
    first = jnp.where(lower, flipped, packed)
    second = jnp.where(lower, packed, jnp.where(on_diagonal, diagonal, flipped))
    return first, second


def split_halves(a):
    high = a.astype(jnp.bfloat16)
    return high, (a - high.astype(jnp.float32)).astype(jnp.bfloat16)


def dot_exact(a, b):
    a_high, a_low = split_halves(a)
    b_high, b_low = split_halves(b)
    dot = functools.partial(jnp.dot, preferred_element_type=jnp.float32)
    return dot(a_high, b_high) + (dot(a_high, b_low) + dot(a_low, b_high))


def ordered_sum(ref, count):
    terms = [ref[k] for k in range(count)]
    while len(terms) > 1:
        terms = [terms[k] + terms[k + 1] for k in range(0, len(terms), 2)]
    return terms[0]


def fused_kernel(
    sample_total,
    owner_ref,
    act_ref,
    gout_ref,
    grad_ref,
    old_ref,
    weights_ref,
    momentum_ref,
    weights_out,
    momentum_out,
    factors_out,
    act_v,
    gout_v,
    old_v,
    weights_v,
    momentum_v,
    packed_v,
    core_in,
    y_in,
    xz_out,
    xz_in,
    full_v,
    left_pair,
    diag_out,
    diag_in,
    diag_xz,
    grad_own,
    grad_x,
    grad_z,
    sum_out,
    sum_xz,
    sum_tensor,
    base_all,
    precond_all,
    mixed_v,
    local_sem,
    sends,
    recvs,
):
    s = lax.axis_index("shards")
    t = lax.axis_index("tensor")
    r = lax.axis_index("replica")
    y = t // 2
    c = t % 2
    n = 128
    half = 512
    quarter = 256
    place = s * 4 + r
    x_peer = (1 - s, t, r)
    y_peer = (s, 2 * (1 - y) + c, r)
    c_peer = (s, 2 * y + 1 - c, r)
    yc_peer = (s, 2 * (1 - y) + 1 - c, r)
    z_ranks = [(r + d) % 4 for d in (1, 2, 3)]
    z_peers = [(s, t, q) for q in z_ranks]
    xz_peers = z_peers + [(1 - s, t, q) for q in z_ranks] + [x_peer]
    xz_places = [s * 4 + q for q in z_ranks] + [(1 - s) * 4 + q for q in z_ranks]
    xz_places = xz_places + [(1 - s) * 4 + r]
    used_sems = [0]

    def part(ref, start, size):
        return ref.at[pl.ds(pl.multiple_of(start, 8), size)]

    def send(src, dst, device):
        copy = remote(src, dst, sends, recvs, used_sems[0], device)
        used_sems[0] += 1
        copy.start()
        return copy

    def load(src, dst, index):
        copy = pltpu.make_async_copy(src, dst, local_sem.at[index])
        copy.start()
        return copy

    barrier = pltpu.get_barrier_semaphore()
    peers = xz_peers + [y_peer, c_peer, yc_peer]
    for peer in peers:
        pl.semaphore_signal(barrier, inc=1, device_id=peer, device_id_type=MESH)

    groups = ((1 - y, 1 - c), (y, 1 - c), (1 - y, c), (y, c))
    starts = [pl.multiple_of(side * half + core * quarter, quarter) for side, core in groups]
    loads = []
    for k, start in enumerate(starts):
        columns = pl.ds(start, quarter)
        loads.append(load(act_ref.at[:, columns], act_v.at[:, columns], 2 * k))
        loads.append(load(gout_ref.at[:, columns], gout_v.at[:, columns], 2 * k + 1))
    weights_load = load(weights_ref, weights_v, 8)
    momentum_load = load(momentum_ref, momentum_v, 9)
    grad_load = load(grad_ref.at[0], grad_own, 10)
    old_load = load(old_ref, old_v, 11)

    rows = lax.broadcasted_iota(jnp.int32, (n, n), 0)
    cols = lax.broadcasted_iota(jnp.int32, (n, n), 1)
    lower = rows > cols
    on_diagonal = rows == cols
    pair_rows = lax.broadcasted_iota(jnp.int32, (8, n), 0)
    identity = on_diagonal.astype(jnp.float32)

    diag = jnp.zeros((8, n), jnp.float32)
    core_copies = []
    for j, (side, core) in enumerate(groups):
        loads[2 * j].wait()
        loads[2 * j + 1].wait()
        start = starts[j]
        a = act_v[:, pl.ds(start, quarter)]
        g = gout_v[:, pl.ds(start, quarter)]
        across = (((0,), (0,)), ((), ()))
        left = lax.dot_general(a, a, across, preferred_element_type=jnp.float32)
        right = lax.dot_general(g, g, across, preferred_element_type=jnp.float32)
        for k in range(2):
            span = slice(k * n, (k + 1) * n)
            second = right[span, span]
            packed_v[pl.ds(start + k * n, n), :] = jnp.where(lower, second, left[span, span])
            row = jnp.sum(jnp.where(on_diagonal, second, 0.0), axis=0, keepdims=True)
            diag = jnp.where(pair_rows == side * 4 + core * 2 + k, row, diag)
        if j == 0:
            pl.semaphore_wait(barrier, len(peers))
        if j < 2:
            core_copies.append(send(part(packed_v, start, quarter), core_in.at[j], c_peer))
        if j == 0:
            grad_load.wait()
            grad_x_copies = [
                send(part(grad_own, (1 - s) * half + q * n, n), grad_x.at[q], x_peer)
                for q in z_ranks + [r]
            ]
        elif j == 1:
            weights_load.wait()
            momentum_load.wait()
            own_rows = pl.ds(pl.multiple_of(place * n, n), n)
            base_all[own_rows, :] = weights_v[...] - (step_rate * momentum_rate) * momentum_v[...]
            base_own = part(base_all, place * n, n)
            base_copies = [send(base_own, base_own, peer) for peer in z_peers]
        elif j == 2:
            core_copies[0].wait()
            packed_v[pl.ds(start, quarter), :] += core_in[0]
            y_copy = send(part(packed_v, start, quarter), y_in, y_peer)
    diag_out[0] = diag
    copy = send(diag_out.at[0], diag_in.at[0], c_peer)
    core_copies[1].wait()
    mine = packed_v[pl.ds(starts[3], quarter), :] + core_in[1]
    copy.wait()
    diag = diag + diag_in[0]
    diag_out[1] = diag
    diag_copy = send(diag_out.at[1], diag_in.at[1], y_peer)
    y_copy.wait()
    xz_out[...] = (mine + y_in[...]).reshape(8, 32, n)
    copies = [
        send(xz_out.at[q], xz_in.at[place], peer) for q, peer in zip(xz_places, xz_peers)
    ]

    def add_gradient(k):
        q = (z_ranks + [r])[k]
        grad_x_copies[k].wait()
        grad_x[q] = grad_x[q] + grad_own[pl.ds(pl.multiple_of(s * half + q * n, n), n), :]
        if k < 3:
            grad_copies.append(send(grad_x.at[q], grad_z.at[r], z_peers[k]))

    grad_copies = []
    diag_copy.wait()
    diag = diag + diag_in[1]
    diag_out[2] = diag
    diag_copies = [send(diag_out.at[2], diag_xz.at[place], peer) for peer in xz_peers]
    xz_in[place] = xz_out[place]
    diag_xz[place] = diag
    for copy in copies:
        copy.wait()
    start = pl.multiple_of(starts[3] + place * 32, 32)
    full_v[pl.ds(start, 32), :] = ordered_sum(xz_in, 8)
    region = part(full_v, start, 32)
    copies = [send(region, region, peer) for peer in xz_peers]
    add_gradient(0)
    add_gradient(1)
    add_gradient(2)
    for copy in diag_copies:
        copy.wait()
    diag_out[3] = ordered_sum(diag_xz, 8)
    for copy in copies:
        copy.wait()

    holder = (s == y) & (r // 2 == c)
    pair_sem = used_sems[0]
    used_sems[0] += 3
    pair_copies = [
        pltpu.make_async_remote_copy(
            src_ref=part(full_v, place * n, n),
            dst_ref=left_pair,
            send_sem=sends.at[pair_sem + k],
            recv_sem=recvs.at[pair_sem],
            device_id=peer,
            device_id_type=MESH,
        )
        for k, peer in enumerate((yc_peer, y_peer, c_peer))
    ]

    @pl.when(holder)
    def _():
        for copy in pair_copies:
            copy.start()
        left_pair[...] = full_v[pl.ds(pl.multiple_of(place * n, n), n), :]

    region = part(full_v, starts[3], quarter)
    y_copy = send(region, region, y_peer)
    core_copies = [send(region, region, c_peer)]
    add_gradient(3)
    grad_z[r] = grad_x[r]
    for copy in base_copies:
        copy.wait()
    region = part(base_all, s * half, half)
    base_copy = send(region, region, x_peer)

    def blend(pair, packed=None):
        if packed is None:
            packed = full_v[pl.ds(pl.multiple_of(pair * n, n), n), :]
        first, second = unpack_pair(
            packed,
            diag_out[3, pl.ds(pair, 1), :],
            lower,
            on_diagonal,
        )
        return (
            decay_rate * old_v[pair] + (1.0 - decay_rate) * (first / sample_total),
            decay_rate * old_v[8 + pair] + (1.0 - decay_rate) * (second / sample_total),
        )

    def invert(blocks):
        scales, rests = [], []
        for block in blocks:
            trace = jnp.sum(jnp.where(on_diagonal, block, 0.0), keepdims=True)
            damped = block + (damping * trace / n + damp_shift) * identity
            bound = jnp.max(
                jnp.sum(jnp.abs(damped), axis=1, keepdims=True), axis=0, keepdims=True
            )
            scales.append(1.0 / bound)
            rests.append(identity - damped / bound)
        inverses = [identity + rest for rest in rests]
        for _ in range(NS_STEPS - 1):
            rests = [dot_exact(rest, rest) for rest in rests]
            inverses = [inv + dot_exact(inv, rest) for inv, rest in zip(inverses, rests)]
        return [inv * scale for inv, scale in zip(inverses, scales)]

    old_load.wait()
    right_inverses = invert([blend(2 * t)[1], blend(2 * t + 1)[1]])

    @pl.when(jnp.logical_not(holder))
    def _():
        pair_copies[0].wait_recv()

    left_inverse = invert([blend(place, left_pair[...])[0]])[0]
    y_copy.wait()
    region = part(full_v, starts[2], quarter)
    core_copies.append(send(region, region, c_peer))

    for copy in grad_copies:
        copy.wait()
    gradient = (grad_z[0] + grad_z[1]) + (grad_z[2] + grad_z[3])
    left = dot_exact(left_inverse, gradient)
    precond = jnp.concatenate(
        [dot_exact(left[:, k * n : (k + 1) * n], right_inverses[k]) for k in range(2)], axis=1
    )
    products = precond * gradient
    products = products[:, :n] + products[:, n:]
    tile = jnp.sum(products.reshape(16, 8, n), axis=0)

    sum_out[0] = tile
    sum_copies = [send(sum_out.at[0], sum_xz.at[place], peer) for peer in xz_peers]
    precond_all[pl.ds(pl.multiple_of(place * n, n), n), :] = precond
    own = part(precond_all, place * n, n)
    x_copies = [send(own, own, x_peer)]

    first_sem = used_sems[0]
    used_sems[0] += 14

    def passing(hop, way, peer, hand_on):
        origin = r - hop if way == 0 else r + hop
        region = part(precond_all, (s * 4 + origin) * n, n)
        index = first_sem + 6 * hand_on + 2 * hop + way
        return remote(region, region, sends, recvs, index, peer)

    ways = ((s, t, r + 1), (s, t, r - 1))

    def sends_on(hop, way):
        return (r >= hop) & (r < 3) if way == 0 else (r <= 3 - hop) & (r > 0)

    def gets(hop, way):
        return r >= hop + 1 if way == 0 else r <= 2 - hop

    def start_hop(hop):
        for way in range(2):

            @pl.when(sends_on(hop, way))
            def _():
                passing(hop, way, ways[way], 0).start()

    def arrived(hop):
        for way in range(2):

            @pl.when(gets(hop, way))
            def _():
                back = ways[1 - way]
                origin = r - hop - 1 if way == 0 else r + hop + 1
                region = part(precond_all, (s * 4 + origin) * n, n)
                index = first_sem + 2 * hop + way
                remote(region, region, sends, recvs, index, back).wait_recv()

    def hand_on(hop):
        for way in range(2):

            @pl.when(gets(hop, way))
            def _():
                passing(hop + 1, way, x_peer, 1).start()

    start_hop(0)
    sum_xz[place] = tile
    for copy in sum_copies:
        copy.wait()
    tile = ordered_sum(sum_xz, 8)
    sum_out[1] = tile
    sum_copies = [
        send(sum_out.at[1], sum_tensor.at[t], peer) for peer in (c_peer, y_peer, yc_peer)
    ]
    sum_tensor[t] = tile
    arrived(0)
    start_hop(1)
    hand_on(0)
    for copy in sum_copies:
        copy.wait()
    alignment = jnp.sum(ordered_sum(sum_tensor, 4), keepdims=True)
    clip_scale = jnp.minimum(1.0, clip_norm / jnp.sqrt(alignment))
    momentum_out[...] = momentum_rate * momentum_v[...] + clip_scale * precond
    arrived(1)
    start_hop(2)
    hand_on(1)

    for copy in core_copies:
        copy.wait()

    @pl.when(holder)
    def _():
        for copy in pair_copies:
            copy.wait_send()

    for pair in range(8):
        mixed_v[pair], mixed_v[8 + pair] = blend(pair)
    mixed_v[16] = jnp.zeros((n, n), jnp.float32)
    block_total = owner_ref.shape[0]
    chosen = [jnp.int32(block_total)] * factors_out.shape[0]
    used = jnp.int32(0)
    for b in range(block_total):
        here = owner_ref[b] == s
        for k in range(min(b + 1, len(chosen))):
            chosen[k] = jnp.where(here & (used == k), jnp.int32(b), chosen[k])
        used = used + jnp.where(here, jnp.int32(1), jnp.int32(0))
    for k in range(len(chosen)):
        factors_out[k] = mixed_v[chosen[k]]

    arrived(2)
    hand_on(2)

    def finish(side):
        span = pl.ds(pl.multiple_of(side * half, half), half)
        step_scale = step_rate * clip_scale
        weights_out[span, :] = base_all[span, :] - step_scale * precond_all[span, :]

    finish(s)
    base_copy.wait()
    for copy in x_copies:
        copy.wait()
    for hop in range(3):
        for way in range(2):

            @pl.when(sends_on(hop, way))
            def _():
                passing(hop, way, ways[way], 0).wait_send()

            @pl.when(gets(hop, way))
            def _():
                passing(hop + 1, way, x_peer, 1).wait()

    finish(1 - s)


def copy_out_kernel(
    weights, momentum, factors, weights_out, momentum_out, factors_out, *held_and_sems
):
    held, (loads, stores) = held_and_sems[:3], held_and_sems[3:]
    pieces = []
    for src, mid, dst, parts in (
        (weights, held[0], weights_out, 4),
        (factors, held[2], factors_out, 3),
        (momentum, held[1], momentum_out, 1),
    ):
        size = src.shape[0] // parts
        for k in range(parts):
            span = pl.ds(k * size, size)
            index = len(pieces)
            first = pltpu.make_async_copy(src.at[span], mid.at[span], loads.at[index])
            first.start()
            second = pltpu.make_async_copy(mid.at[span], dst.at[span], stores.at[index])
            pieces.append((first, second))
    for first, second in pieces:
        first.wait()
        second.start()
    for _, second in pieces:
        second.wait()


def fused_step(activations, grads_out, grad_parts, old_factors, block_owner, weights, momentum):
    n = old_factors.shape[1]
    shards = lax.axis_size("shards")
    capacity = (old_factors.shape[0] + shards - 1) // shards + 1
    devices = shards * lax.axis_size("tensor") * lax.axis_size("replica")
    f32 = jnp.float32
    anywhere = pl.BlockSpec(memory_space=pl.ANY)
    vmem = pl.BlockSpec(memory_space=pltpu.VMEM)
    results = pl.pallas_call(
        functools.partial(fused_kernel, float(activations.shape[0] * devices)),
        out_shape=(
            jax.ShapeDtypeStruct(grad_parts.shape[1:], f32),
            jax.ShapeDtypeStruct(momentum.shape, f32),
            jax.ShapeDtypeStruct((capacity, n, n), f32),
        ),
        in_specs=[
            pl.BlockSpec(memory_space=pltpu.SMEM),
            anywhere,
            anywhere,
            anywhere,
            anywhere,
            anywhere,
            anywhere,
        ],
        out_specs=(vmem, vmem, vmem),
        scratch_shapes=[
            pltpu.VMEM(activations.shape, activations.dtype),
            pltpu.VMEM(grads_out.shape, grads_out.dtype),
            pltpu.VMEM(old_factors.shape, f32),
            pltpu.VMEM(weights.shape, f32),
            pltpu.VMEM(momentum.shape, f32),
            pltpu.VMEM((1024, n), f32),
            pltpu.VMEM((2, 256, n), f32),
            pltpu.VMEM((256, n), f32),
            pltpu.VMEM((8, 32, n), f32),
            pltpu.VMEM((8, 32, n), f32),
            pltpu.VMEM((1024, n), f32),
            pltpu.VMEM((n, n), f32),
            pltpu.VMEM((4, 8, n), f32),
            pltpu.VMEM((2, 8, n), f32),
            pltpu.VMEM((8, 8, n), f32),
            pltpu.VMEM((1024, 256), f32),
            pltpu.VMEM((4, n, 256), f32),
            pltpu.VMEM((4, n, 256), f32),
            pltpu.VMEM((2, 8, n), f32),
            pltpu.VMEM((8, 8, n), f32),
            pltpu.VMEM((4, 8, n), f32),
            pltpu.VMEM((1024, 256), f32),
            pltpu.VMEM((1024, 256), f32),
            pltpu.VMEM((17, n, n), f32),
            pltpu.SemaphoreType.DMA((12,)),
            pltpu.SemaphoreType.DMA((72,)),
            pltpu.SemaphoreType.DMA((72,)),
        ],
        compiler_params=pltpu.CompilerParams(
            collective_id=0, has_side_effects=True, vmem_limit_bytes=60 * 1024 * 1024
        ),
        cost_estimate=pl.CostEstimate(
            flops=1_200_000_000, bytes_accessed=10_000_000, transcendentals=0
        ),
    )(block_owner, activations, grads_out, grad_parts, old_factors, weights, momentum)
    return pl.pallas_call(
        copy_out_kernel,
        out_shape=tuple(jax.ShapeDtypeStruct(a.shape, a.dtype) for a in results),
        in_specs=[anywhere] * 3,
        out_specs=(anywhere,) * 3,
        scratch_shapes=[pltpu.VMEM(a.shape, a.dtype) for a in results]
        + [pltpu.SemaphoreType.DMA((8,))] * 2,
        compiler_params=pltpu.CompilerParams(vmem_limit_bytes=60 * 1024 * 1024),
        cost_estimate=pl.CostEstimate(flops=0, bytes_accessed=3_500_000, transcendentals=0),
    )(*results)


def step(activations, grads_out, grad_parts, old_factors, block_owner, weights, momentum):
    sizes = tuple(lax.axis_size(name) for name in ("shards", "tensor", "replica"))
    fits = (
        sizes == (2, 4, 4)
        and weights.shape == (128, 256)
        and old_factors.shape == (16, 128, 128)
        and activations.shape == grads_out.shape == (1024, 1024)
    )
    chosen = fused_step if fits else body
    return chosen(
        activations, grads_out, grad_parts, old_factors, block_owner, weights, momentum
    )


def solution(mesh):
    placed = (
        P(("shards", "tensor", "replica"), None),
        P(("shards", "tensor", "replica"), None),
        P(("shards", "replica"), None, "tensor"),
        P(),
        P(),
        P(("shards", "replica"), "tensor"),
        P(("shards", "replica"), "tensor"),
    )
    return jax.shard_map(
        step,
        mesh=mesh,
        in_specs=placed,
        out_specs=(P(None, "tensor"), P(("shards", "replica"), "tensor"), P("shards", None, None)),
        check_vma=False,
    )
```

```python
import functools

import jax
import jax.numpy as jnp
from jax import lax
from jax.experimental import pallas as pl
from jax.experimental.pallas import tpu as pltpu
from jax.sharding import PartitionSpec as P

MESH = pl.DeviceIdType.MESH

NS_STEPS = 4


exact_mode = lax.Precision.HIGHEST
decay_rate = 0.75
damping = 0.1
damp_shift = 0.001
clip_norm = 256.0
momentum_rate = 0.9
step_rate = 0.05


def sample_stats(samples, block_size):
    sample_rows, width = samples.shape
    blocks = samples.reshape(sample_rows, width // block_size, block_size)
    return jnp.einsum("tnb,tnc->nbc", blocks, blocks, preferred_element_type=jnp.float32)


def build_slots(block_owner, capacity, slot_count):
    block_count = block_owner.shape[0]
    positions = jnp.arange(block_count, dtype=jnp.int32)
    earlier = (block_owner[:, None] == block_owner[None, :]) & (
        positions[None, :] < positions[:, None]
    )
    owner_slot_list = block_owner * capacity + jnp.sum(earlier.astype(jnp.int32), axis=1)
    return (owner_slot_list[None, :] == jnp.arange(slot_count, dtype=jnp.int32)[:, None]).astype(
        jnp.float32
    )


def newton_inverse(mixed_factor_blocks):
    block_size = mixed_factor_blocks.shape[-1]
    identity = jnp.eye(block_size, dtype=jnp.float32)
    traces = jnp.trace(mixed_factor_blocks, axis1=1, axis2=2)
    damped = (
        mixed_factor_blocks + (damping * traces / block_size + damp_shift)[:, None, None] * identity
    )
    bounds = jnp.max(jnp.sum(jnp.abs(damped), axis=2), axis=1)
    approx = identity[None, :, :] / bounds[:, None, None]
    for iteration in range(NS_STEPS):
        left_part = jnp.einsum("nab,nbc->nac", approx, damped, precision=exact_mode)
        approx = 2.0 * approx - jnp.einsum("nab,nbc->nac", left_part, approx, precision=exact_mode)
    return approx


def apply_right(left_part, right_inv, block_size):
    row_count, col_count = left_part.shape
    right_count = col_count // block_size
    return jnp.einsum(
        "rnb,nbc->rnc",
        left_part.reshape(row_count, right_count, block_size),
        right_inv,
        precision=exact_mode,
    ).reshape(row_count, col_count)


def body(activations, grads_out, grad_parts, old_factors, block_owner, weights, momentum):
    shard_count = lax.axis_size("shards")
    block_count = old_factors.shape[0]
    block_size = old_factors.shape[1]
    capacity = (block_count + shard_count - 1) // shard_count + 1
    slot_count = capacity * shard_count
    slot_table = build_slots(block_owner, capacity, slot_count)
    local_stats = jnp.concatenate(
        [sample_stats(activations, block_size), sample_stats(grads_out, block_size)], axis=0
    )
    packed = jnp.dot(
        slot_table, local_stats.reshape(block_count, block_size * block_size), precision=exact_mode
    )
    first_slot = lax.axis_index("shards") * capacity
    summed = lax.psum(packed, ("shards", "tensor", "replica"))
    owned = lax.dynamic_slice_in_dim(summed, first_slot, capacity, 0)
    sample_count = (
        activations.shape[0] * shard_count * lax.axis_size("tensor") * lax.axis_size("replica")
    )
    owned_table = lax.dynamic_slice_in_dim(slot_table, first_slot, capacity, 0)
    old_owned = jnp.dot(
        owned_table, old_factors.reshape(block_count, block_size * block_size), precision=exact_mode
    )
    mixed_factor_blocks = (
        decay_rate * old_owned + (1.0 - decay_rate) * (owned / sample_count)
    ).reshape(capacity, block_size, block_size)
    inverse_owned = newton_inverse(mixed_factor_blocks)
    start_blocks = jnp.zeros((block_count, block_size * block_size), jnp.float32)
    shard_piece = lax.all_gather(inverse_owned, "shards", axis=0, tiled=True)
    piece_rows = shard_piece.shape[0]
    rows_table = lax.slice_in_dim(slot_table, 0, piece_rows, axis=0)
    flat_piece = shard_piece.reshape(piece_rows, block_size * block_size)
    inverse_flat = start_blocks + jnp.einsum(
        "sb,sk->bk", rows_table, flat_piece, precision=exact_mode
    )
    inverse_blocks = inverse_flat.reshape(block_count, block_size, block_size)
    partial_grad = grad_parts[0]
    row_count, col_count = partial_grad.shape
    left_count = row_count // block_size
    right_count = col_count // block_size
    right_first = left_count + lax.axis_index("tensor") * right_count
    right_inv = lax.dynamic_slice_in_dim(inverse_blocks, right_first, right_count, 0)
    left_part = jnp.einsum(
        "nab,nbc->nac",
        inverse_blocks[:left_count],
        partial_grad.reshape(left_count, block_size, col_count),
        precision=exact_mode,
    ).reshape(row_count, col_count)
    precond = apply_right(left_part, right_inv, block_size)
    total_precond, total_grad = (
        lax.psum_scatter(precond, ("shards", "replica"), scatter_dimension=0, tiled=True),
        lax.psum_scatter(partial_grad, ("shards", "replica"), scatter_dimension=0, tiled=True),
    )
    alignment_sum = lax.psum(jnp.sum(total_precond * total_grad), ("shards", "tensor", "replica"))
    clip_scale = jnp.minimum(1.0, clip_norm / jnp.sqrt(alignment_sum))
    momentum_next = momentum_rate * momentum + clip_scale * total_precond
    weights_next = weights - step_rate * momentum_next
    gathered = lax.all_gather(weights_next, ("shards", "replica"), axis=0, tiled=True)
    return (gathered, momentum_next, mixed_factor_blocks)


def remote(src, dst, sends, recvs, index, device):
    return pltpu.make_async_remote_copy(
        src_ref=src,
        dst_ref=dst,
        send_sem=sends.at[index],
        recv_sem=recvs.at[index],
        device_id=device,
        device_id_type=MESH,
    )


def unpack_pair(packed, diagonal, lower, on_diagonal):
    flipped = packed.T
    first = jnp.where(lower, flipped, packed)
    second = jnp.where(lower, packed, jnp.where(on_diagonal, diagonal, flipped))
    return first, second


def split_halves(a):
    high = a.astype(jnp.bfloat16)
    return high, (a - high.astype(jnp.float32)).astype(jnp.bfloat16)


def dot_exact(a, b):
    a_high, a_low = split_halves(a)
    b_high, b_low = split_halves(b)
    dot = functools.partial(jnp.dot, preferred_element_type=jnp.float32)
    return dot(a_high, b_high) + (dot(a_high, b_low) + dot(a_low, b_high))


def ordered_sum(ref, count):
    terms = [ref[k] for k in range(count)]
    while len(terms) > 1:
        terms = [terms[k] + terms[k + 1] for k in range(0, len(terms), 2)]
    return terms[0]


def fused_kernel(
    sample_total,
    owner_ref,
    act_ref,
    gout_ref,
    grad_ref,
    old_ref,
    weights_ref,
    momentum_ref,
    weights_out,
    momentum_out,
    factors_out,
    act_v,
    gout_v,
    old_v,
    weights_v,
    momentum_v,
    packed_v,
    core_in,
    y_in,
    xz_out,
    xz_in,
    full_v,
    left_pair,
    diag_out,
    diag_in,
    diag_xz,
    grad_own,
    grad_x,
    grad_z,
    sum_out,
    sum_xz,
    sum_tensor,
    base_all,
    precond_all,
    mixed_v,
    local_sem,
    sends,
    recvs,
):
    s = lax.axis_index("shards")
    t = lax.axis_index("tensor")
    r = lax.axis_index("replica")
    y = t // 2
    c = t % 2
    n = 128
    half = 512
    quarter = 256
    place = s * 4 + r
    x_peer = (1 - s, t, r)
    y_peer = (s, 2 * (1 - y) + c, r)
    c_peer = (s, 2 * y + 1 - c, r)
    yc_peer = (s, 2 * (1 - y) + 1 - c, r)
    z_ranks = [(r + d) % 4 for d in (1, 2, 3)]
    z_peers = [(s, t, q) for q in z_ranks]
    xz_peers = z_peers + [(1 - s, t, q) for q in z_ranks] + [x_peer]
    xz_places = [s * 4 + q for q in z_ranks] + [(1 - s) * 4 + q for q in z_ranks]
    xz_places = xz_places + [(1 - s) * 4 + r]
    used_sems = [0]

    def part(ref, start, size):
        return ref.at[pl.ds(pl.multiple_of(start, 8), size)]

    def send(src, dst, device):
        copy = remote(src, dst, sends, recvs, used_sems[0], device)
        used_sems[0] += 1
        copy.start()
        return copy

    def load(src, dst, index):
        copy = pltpu.make_async_copy(src, dst, local_sem.at[index])
        copy.start()
        return copy

    barrier = pltpu.get_barrier_semaphore()
    peers = xz_peers + [y_peer, c_peer, yc_peer]
    for peer in peers:
        pl.semaphore_signal(barrier, inc=1, device_id=peer, device_id_type=MESH)

    groups = ((1 - y, 1 - c), (y, 1 - c), (1 - y, c), (y, c))
    starts = [pl.multiple_of(side * half + core * quarter, quarter) for side, core in groups]
    loads = []
    for k, start in enumerate(starts):
        columns = pl.ds(start, quarter)
        loads.append(load(act_ref.at[:, columns], act_v.at[:, columns], 2 * k))
        loads.append(load(gout_ref.at[:, columns], gout_v.at[:, columns], 2 * k + 1))
    weights_load = load(weights_ref, weights_v, 8)
    momentum_load = load(momentum_ref, momentum_v, 9)
    grad_load = load(grad_ref.at[0], grad_own, 10)
    old_load = load(old_ref, old_v, 11)

    rows = lax.broadcasted_iota(jnp.int32, (n, n), 0)
    cols = lax.broadcasted_iota(jnp.int32, (n, n), 1)
    lower = rows > cols
    on_diagonal = rows == cols
    pair_rows = lax.broadcasted_iota(jnp.int32, (8, n), 0)
    identity = on_diagonal.astype(jnp.float32)

    diag = jnp.zeros((8, n), jnp.float32)
    core_copies = []
    for j, (side, core) in enumerate(groups):
        loads[2 * j].wait()
        loads[2 * j + 1].wait()
        start = starts[j]
        a = act_v[:, pl.ds(start, quarter)]
        g = gout_v[:, pl.ds(start, quarter)]
        across = (((0,), (0,)), ((), ()))
        left = lax.dot_general(a, a, across, preferred_element_type=jnp.float32)
        right = lax.dot_general(g, g, across, preferred_element_type=jnp.float32)
        for k in range(2):
            span = slice(k * n, (k + 1) * n)
            second = right[span, span]
            packed_v[pl.ds(start + k * n, n), :] = jnp.where(lower, second, left[span, span])
            row = jnp.sum(jnp.where(on_diagonal, second, 0.0), axis=0, keepdims=True)
            diag = jnp.where(pair_rows == side * 4 + core * 2 + k, row, diag)
        if j == 0:
            pl.semaphore_wait(barrier, len(peers))
        if j < 2:
            core_copies.append(send(part(packed_v, start, quarter), core_in.at[j], c_peer))
        if j == 0:
            grad_load.wait()
            grad_x_copies = [
                send(part(grad_own, (1 - s) * half + q * n, n), grad_x.at[q], x_peer)
                for q in z_ranks + [r]
            ]
        elif j == 1:
            weights_load.wait()
            momentum_load.wait()
            own_rows = pl.ds(pl.multiple_of(place * n, n), n)
            base_all[own_rows, :] = weights_v[...] - (step_rate * momentum_rate) * momentum_v[...]
            base_own = part(base_all, place * n, n)
            base_copies = [send(base_own, base_own, peer) for peer in z_peers]
        elif j == 2:
            core_copies[0].wait()
            packed_v[pl.ds(start, quarter), :] += core_in[0]
            y_copy = send(part(packed_v, start, quarter), y_in, y_peer)
    diag_out[0] = diag
    copy = send(diag_out.at[0], diag_in.at[0], c_peer)
    core_copies[1].wait()
    mine = packed_v[pl.ds(starts[3], quarter), :] + core_in[1]
    copy.wait()
    diag = diag + diag_in[0]
    diag_out[1] = diag
    diag_copy = send(diag_out.at[1], diag_in.at[1], y_peer)
    y_copy.wait()
    xz_out[...] = (mine + y_in[...]).reshape(8, 32, n)
    copies = [
        send(xz_out.at[q], xz_in.at[place], peer) for q, peer in zip(xz_places, xz_peers)
    ]

    def add_gradient(k):
        q = (z_ranks + [r])[k]
        grad_x_copies[k].wait()
        grad_x[q] = grad_x[q] + grad_own[pl.ds(pl.multiple_of(s * half + q * n, n), n), :]
        if k < 3:
            grad_copies.append(send(grad_x.at[q], grad_z.at[r], z_peers[k]))

    grad_copies = []
    diag_copy.wait()
    diag = diag + diag_in[1]
    diag_out[2] = diag
    diag_copies = [send(diag_out.at[2], diag_xz.at[place], peer) for peer in xz_peers]
    xz_in[place] = xz_out[place]
    diag_xz[place] = diag
    add_gradient(0)
    for copy in copies:
        copy.wait()
    start = pl.multiple_of(starts[3] + place * 32, 32)
    full_v[pl.ds(start, 32), :] = ordered_sum(xz_in, 8)
    region = part(full_v, start, 32)
    copies = [send(region, region, peer) for peer in xz_peers]
    add_gradient(1)
    add_gradient(2)
    for copy in diag_copies:
        copy.wait()
    diag_out[3] = ordered_sum(diag_xz, 8)
    for copy in copies:
        copy.wait()

    holder = (s == y) & (r // 2 == c)
    pair_sem = used_sems[0]
    used_sems[0] += 3
    pair_copies = [
        pltpu.make_async_remote_copy(
            src_ref=part(full_v, place * n, n),
            dst_ref=left_pair,
            send_sem=sends.at[pair_sem + k],
            recv_sem=recvs.at[pair_sem],
            device_id=peer,
            device_id_type=MESH,
        )
        for k, peer in enumerate((yc_peer, y_peer, c_peer))
    ]

    @pl.when(holder)
    def _():
        for copy in pair_copies:
            copy.start()
        left_pair[...] = full_v[pl.ds(pl.multiple_of(place * n, n), n), :]

    region = part(full_v, starts[3], quarter)
    y_copy = send(region, region, y_peer)
    core_copies = [send(region, region, c_peer)]
    add_gradient(3)
    grad_z[r] = grad_x[r]
    for copy in base_copies:
        copy.wait()
    region = part(base_all, s * half, half)
    base_copy = send(region, region, x_peer)

    def blend(pair, packed=None):
        if packed is None:
            packed = full_v[pl.ds(pl.multiple_of(pair * n, n), n), :]
        first, second = unpack_pair(
            packed,
            diag_out[3, pl.ds(pair, 1), :],
            lower,
            on_diagonal,
        )
        return (
            decay_rate * old_v[pair] + (1.0 - decay_rate) * (first / sample_total),
            decay_rate * old_v[8 + pair] + (1.0 - decay_rate) * (second / sample_total),
        )

    def invert(blocks):
        scales, rests = [], []
        for block in blocks:
            trace = jnp.sum(jnp.where(on_diagonal, block, 0.0), keepdims=True)
            damped = block + (damping * trace / n + damp_shift) * identity
            bound = jnp.max(
                jnp.sum(jnp.abs(damped), axis=1, keepdims=True), axis=0, keepdims=True
            )
            scales.append(1.0 / bound)
            rests.append(identity - damped / bound)
        inverses = [identity + rest for rest in rests]
        for _ in range(NS_STEPS - 1):
            rests = [dot_exact(rest, rest) for rest in rests]
            inverses = [inv + dot_exact(inv, rest) for inv, rest in zip(inverses, rests)]
        return [inv * scale for inv, scale in zip(inverses, scales)]

    old_load.wait()
    right_inverses = invert([blend(2 * t)[1], blend(2 * t + 1)[1]])

    @pl.when(jnp.logical_not(holder))
    def _():
        pair_copies[0].wait_recv()

    left_inverse = invert([blend(place, left_pair[...])[0]])[0]
    y_copy.wait()
    region = part(full_v, starts[2], quarter)
    core_copies.append(send(region, region, c_peer))

    for copy in grad_copies:
        copy.wait()
    gradient = (grad_z[0] + grad_z[1]) + (grad_z[2] + grad_z[3])
    left = dot_exact(left_inverse, gradient)
    precond = jnp.concatenate(
        [dot_exact(left[:, k * n : (k + 1) * n], right_inverses[k]) for k in range(2)], axis=1
    )
    products = precond * gradient
    products = products[:, :n] + products[:, n:]
    tile = jnp.sum(products.reshape(16, 8, n), axis=0)

    sum_out[0] = tile
    sum_copies = [send(sum_out.at[0], sum_xz.at[place], peer) for peer in xz_peers]
    precond_all[pl.ds(pl.multiple_of(place * n, n), n), :] = precond
    own = part(precond_all, place * n, n)
    x_copies = [send(own, own, x_peer)]

    first_sem = used_sems[0]
    used_sems[0] += 14

    def passing(hop, way, peer, hand_on):
        origin = r - hop if way == 0 else r + hop
        region = part(precond_all, (s * 4 + origin) * n, n)
        index = first_sem + 6 * hand_on + 2 * hop + way
        return remote(region, region, sends, recvs, index, peer)

    ways = ((s, t, r + 1), (s, t, r - 1))

    def sends_on(hop, way):
        return (r >= hop) & (r < 3) if way == 0 else (r <= 3 - hop) & (r > 0)

    def gets(hop, way):
        return r >= hop + 1 if way == 0 else r <= 2 - hop

    def start_hop(hop):
        for way in range(2):

            @pl.when(sends_on(hop, way))
            def _():
                passing(hop, way, ways[way], 0).start()

    def arrived(hop):
        for way in range(2):

            @pl.when(gets(hop, way))
            def _():
                back = ways[1 - way]
                origin = r - hop - 1 if way == 0 else r + hop + 1
                region = part(precond_all, (s * 4 + origin) * n, n)
                index = first_sem + 2 * hop + way
                remote(region, region, sends, recvs, index, back).wait_recv()

    def hand_on(hop):
        for way in range(2):

            @pl.when(gets(hop, way))
            def _():
                passing(hop + 1, way, x_peer, 1).start()

    start_hop(0)
    sum_xz[place] = tile
    for copy in sum_copies:
        copy.wait()
    tile = ordered_sum(sum_xz, 8)
    sum_out[1] = tile
    sum_copies = [
        send(sum_out.at[1], sum_tensor.at[t], peer) for peer in (c_peer, y_peer, yc_peer)
    ]
    sum_tensor[t] = tile
    arrived(0)
    start_hop(1)
    hand_on(0)
    for copy in sum_copies:
        copy.wait()
    alignment = jnp.sum(ordered_sum(sum_tensor, 4), keepdims=True)
    clip_scale = jnp.minimum(1.0, clip_norm / jnp.sqrt(alignment))
    momentum_out[...] = momentum_rate * momentum_v[...] + clip_scale * precond
    arrived(1)
    start_hop(2)
    hand_on(1)

    for copy in core_copies:
        copy.wait()

    @pl.when(holder)
    def _():
        for copy in pair_copies:
            copy.wait_send()

    for pair in range(8):
        mixed_v[pair], mixed_v[8 + pair] = blend(pair)
    mixed_v[16] = jnp.zeros((n, n), jnp.float32)
    block_total = owner_ref.shape[0]
    chosen = [jnp.int32(block_total)] * factors_out.shape[0]
    used = jnp.int32(0)
    for b in range(block_total):
        here = owner_ref[b] == s
        for k in range(min(b + 1, len(chosen))):
            chosen[k] = jnp.where(here & (used == k), jnp.int32(b), chosen[k])
        used = used + jnp.where(here, jnp.int32(1), jnp.int32(0))
    for k in range(len(chosen)):
        factors_out[k] = mixed_v[chosen[k]]

    arrived(2)
    hand_on(2)

    def finish(side):
        span = pl.ds(pl.multiple_of(side * half, half), half)
        step_scale = step_rate * clip_scale
        weights_out[span, :] = base_all[span, :] - step_scale * precond_all[span, :]

    finish(s)
    base_copy.wait()
    for copy in x_copies:
        copy.wait()
    for hop in range(3):
        for way in range(2):

            @pl.when(sends_on(hop, way))
            def _():
                passing(hop, way, ways[way], 0).wait_send()

            @pl.when(gets(hop, way))
            def _():
                passing(hop + 1, way, x_peer, 1).wait()

    finish(1 - s)


def copy_out_kernel(
    weights, momentum, factors, weights_out, momentum_out, factors_out, *held_and_sems
):
    held, (loads, stores) = held_and_sems[:3], held_and_sems[3:]
    pieces = []
    for src, mid, dst, parts in (
        (weights, held[0], weights_out, 4),
        (factors, held[2], factors_out, 3),
        (momentum, held[1], momentum_out, 1),
    ):
        size = src.shape[0] // parts
        for k in range(parts):
            span = pl.ds(k * size, size)
            index = len(pieces)
            first = pltpu.make_async_copy(src.at[span], mid.at[span], loads.at[index])
            first.start()
            second = pltpu.make_async_copy(mid.at[span], dst.at[span], stores.at[index])
            pieces.append((first, second))
    for first, second in pieces:
        first.wait()
        second.start()
    for _, second in pieces:
        second.wait()


def fused_step(activations, grads_out, grad_parts, old_factors, block_owner, weights, momentum):
    n = old_factors.shape[1]
    shards = lax.axis_size("shards")
    capacity = (old_factors.shape[0] + shards - 1) // shards + 1
    devices = shards * lax.axis_size("tensor") * lax.axis_size("replica")
    f32 = jnp.float32
    anywhere = pl.BlockSpec(memory_space=pl.ANY)
    vmem = pl.BlockSpec(memory_space=pltpu.VMEM)
    results = pl.pallas_call(
        functools.partial(fused_kernel, float(activations.shape[0] * devices)),
        out_shape=(
            jax.ShapeDtypeStruct(grad_parts.shape[1:], f32),
            jax.ShapeDtypeStruct(momentum.shape, f32),
            jax.ShapeDtypeStruct((capacity, n, n), f32),
        ),
        in_specs=[
            pl.BlockSpec(memory_space=pltpu.SMEM),
            anywhere,
            anywhere,
            anywhere,
            anywhere,
            anywhere,
            anywhere,
        ],
        out_specs=(vmem, vmem, vmem),
        scratch_shapes=[
            pltpu.VMEM(activations.shape, activations.dtype),
            pltpu.VMEM(grads_out.shape, grads_out.dtype),
            pltpu.VMEM(old_factors.shape, f32),
            pltpu.VMEM(weights.shape, f32),
            pltpu.VMEM(momentum.shape, f32),
            pltpu.VMEM((1024, n), f32),
            pltpu.VMEM((2, 256, n), f32),
            pltpu.VMEM((256, n), f32),
            pltpu.VMEM((8, 32, n), f32),
            pltpu.VMEM((8, 32, n), f32),
            pltpu.VMEM((1024, n), f32),
            pltpu.VMEM((n, n), f32),
            pltpu.VMEM((4, 8, n), f32),
            pltpu.VMEM((2, 8, n), f32),
            pltpu.VMEM((8, 8, n), f32),
            pltpu.VMEM((1024, 256), f32),
            pltpu.VMEM((4, n, 256), f32),
            pltpu.VMEM((4, n, 256), f32),
            pltpu.VMEM((2, 8, n), f32),
            pltpu.VMEM((8, 8, n), f32),
            pltpu.VMEM((4, 8, n), f32),
            pltpu.VMEM((1024, 256), f32),
            pltpu.VMEM((1024, 256), f32),
            pltpu.VMEM((17, n, n), f32),
            pltpu.SemaphoreType.DMA((12,)),
            pltpu.SemaphoreType.DMA((72,)),
            pltpu.SemaphoreType.DMA((72,)),
        ],
        compiler_params=pltpu.CompilerParams(
            collective_id=0, has_side_effects=True, vmem_limit_bytes=60 * 1024 * 1024
        ),
        cost_estimate=pl.CostEstimate(
            flops=1_200_000_000, bytes_accessed=10_000_000, transcendentals=0
        ),
    )(block_owner, activations, grads_out, grad_parts, old_factors, weights, momentum)
    return pl.pallas_call(
        copy_out_kernel,
        out_shape=tuple(jax.ShapeDtypeStruct(a.shape, a.dtype) for a in results),
        in_specs=[anywhere] * 3,
        out_specs=(anywhere,) * 3,
        scratch_shapes=[pltpu.VMEM(a.shape, a.dtype) for a in results]
        + [pltpu.SemaphoreType.DMA((8,))] * 2,
        compiler_params=pltpu.CompilerParams(vmem_limit_bytes=60 * 1024 * 1024),
        cost_estimate=pl.CostEstimate(flops=0, bytes_accessed=3_500_000, transcendentals=0),
    )(*results)


def step(activations, grads_out, grad_parts, old_factors, block_owner, weights, momentum):
    sizes = tuple(lax.axis_size(name) for name in ("shards", "tensor", "replica"))
    fits = (
        sizes == (2, 4, 4)
        and weights.shape == (128, 256)
        and old_factors.shape == (16, 128, 128)
        and activations.shape == grads_out.shape == (1024, 1024)
    )
    chosen = fused_step if fits else body
    return chosen(
        activations, grads_out, grad_parts, old_factors, block_owner, weights, momentum
    )


def solution(mesh):
    placed = (
        P(("shards", "tensor", "replica"), None),
        P(("shards", "tensor", "replica"), None),
        P(("shards", "replica"), None, "tensor"),
        P(),
        P(),
        P(("shards", "replica"), "tensor"),
        P(("shards", "replica"), "tensor"),
    )
    return jax.shard_map(
        step,
        mesh=mesh,
        in_specs=placed,
        out_specs=(P(None, "tensor"), P(("shards", "replica"), "tensor"), P("shards", None, None)),
        check_vma=False,
    )
```
